32 devices in a mesh: epoch: 2 (over x), tile: 16 (over z, y, core).
Axes of the slice: x: 2, y: 2, z: 4, core: 2. Of those that a mesh axis runs over, the one named last changes fastest.
Arguments:
- owners: int32 [2, 2048], P('epoch', 'tile'), may hold values from 0 to 15, as said below
- row_offsets: int32 [2, 2048], P('epoch', 'tile'), may hold values from 0 to 224
- col_offsets: int32 [2, 2048], P('epoch', 'tile'), may hold values from 0 to 4064
- samples: bfloat16 [2, 2048, 2, 256], P('epoch', 'tile'), may hold values from -6 to 6
- coords: float32 [2, 2048, 2, 256], P('epoch', 'tile'), may hold values from 4 to 28
- taper_rows: float32 [16, 256], P('epoch'), may hold values from 1 to 4
- taper_cols: float32 [4096], P('tile'), may hold values from 1 to 4
Outputs:
- image: float32 [16, 256, 4096], P('epoch', None, 'tile')
The draws below stay inside these ranges and needn't reach their ends.
Inputs may be any that keep to these rules, and one draw needn't show every extreme that they name: `owners`: in every epoch, within each aligned block of 128 slots (the slots of one index of tile), no owner tile is named more than 10 times, and one owner tile is named exactly 10 times in every block of that epoch.
All inputs are finite; a program needn't handle non-finite values.
Results may differ from the reference program's by a relative error of at most 0.0053.
Values may be sent and summed in bfloat16 or wider, within the bound.
A program may use at most 128 MiB of HBM per device.

```python
import math
import jax
import jax.numpy as jnp
from jax import lax

G = 4096
SUB = 32
NK = 256
S_DEV = 128
EPOCHS = 2
TILES = 16
SLOTS = 2048
CAP = 10
BAND = 256


def draw_owners(key, part):
    key_level, key_hot, key_noise, key_order = jax.random.split(key, 4)
    pool_size = TILES * CAP
    level = jax.random.randint(key_level, (EPOCHS, TILES), 0, 4, dtype=jnp.int32)
    hot_tile = jax.random.randint(key_hot, (EPOCHS,), 0, TILES, dtype=jnp.int32)
    cand_owner = jnp.arange(pool_size, dtype=jnp.int32) // CAP
    boost = level[:, cand_owner] + 4 * (cand_owner[None, :] == hot_tile[:, None]).astype(jnp.int32)
    noise = jax.random.randint(key_noise, (EPOCHS, TILES, pool_size), 0, 65536, dtype=jnp.int32)
    scores = (boost[:, None, :] * 65536 + noise) * pool_size + jnp.arange(pool_size, dtype=jnp.int32)[None, None, :]
    top_values, chosen = lax.top_k(scores, S_DEV)
    picked = (chosen // CAP).astype(jnp.int32)
    order_keys = jax.random.randint(key_order, (EPOCHS, TILES, S_DEV), 0, 65536, dtype=jnp.int32) * S_DEV + jnp.arange(S_DEV, dtype=jnp.int32)[None, None, :]
    order = jnp.argsort(order_keys, axis=-1)
    shuffled = jnp.take_along_axis(picked, order, axis=-1)
    return shuffled.reshape(EPOCHS, TILES * S_DEV).astype(jnp.int32)


def with_ends(array, rng, least, largest):
    index_at = [jax.random.randint(jax.random.fold_in(rng, axis), (), 0, length) for axis, length in enumerate(array.shape)]
    longest = array.shape.index(max(array.shape))
    beside = index_at[:longest] + [(index_at[longest] + 1) % array.shape[longest]] + index_at[longest + 1:]
    return array.at[tuple(index_at)].set(least).at[tuple(beside)].set(largest)


def block_levels(key, dims, pieces, smallest, top_value):
    gain = 1.0
    for dim, blocks in pieces:
        draws = jax.random.uniform(jax.random.fold_in(jax.random.fold_in(key, 6), dim), (blocks,), jnp.float32, smallest / len(pieces), top_value / len(pieces))
        gain = gain * jnp.repeat(jnp.exp(draws), dims[dim] // blocks).reshape((-1,) + (1,) * (len(dims) - 1 - dim))
    return gain


def normal_values(rng, extent, deviation, limit, shards=(), kind=jnp.bfloat16):
    gain = block_levels(rng, extent, shards, -0.22, 0.18) if shards else 1.0
    values = jax.random.normal(rng, extent, jnp.float32) * deviation * gain
    return jnp.minimum(jnp.maximum(values, -limit), limit).astype(kind)


def setup_inputs(seed: int = 0) -> dict:
    streams_of = jax.random.split(jax.random.key(seed), 8)
    owners = draw_owners(jax.random.fold_in(streams_of[7], 71), 0)
    row_offsets = with_ends(jax.random.randint(streams_of[1], (EPOCHS, SLOTS), 0, BAND - SUB + 1), jax.random.fold_in(streams_of[1], 1), 0, BAND - SUB).astype(jnp.int32)
    col_offsets = with_ends(jax.random.randint(streams_of[2], (EPOCHS, SLOTS), 0, G - SUB + 1), jax.random.fold_in(streams_of[2], 1), 0, G - SUB).astype(jnp.int32)
    samples = normal_values(streams_of[3], (EPOCHS, SLOTS, 2, NK), 1.0, 6.0, ((0, 2), (1, 16)))
    coords = jnp.clip(4.0 + 24.0 * jax.random.uniform(streams_of[4], (EPOCHS, SLOTS, 2, NK), jnp.float32) ** block_levels(streams_of[4], (EPOCHS, SLOTS, 2, NK), ((0, 2), (1, 16)), -0.2, 0.2), 4.0, 28.0)
    taper_rows = jnp.clip(jnp.exp(math.log(4.0) - 1.3862944 * jax.random.uniform(streams_of[5], (TILES, BAND), jnp.float32) ** block_levels(streams_of[5], (TILES, BAND), ((0, 2),), -0.2, 0.2)), 1.0, 4.0)
    taper_cols = jnp.clip(jnp.exp(math.log(4.0) - 1.3862944 * jax.random.uniform(streams_of[6], (G,), jnp.float32) ** block_levels(streams_of[6], (G,), ((0, 16),), -0.2, 0.2)), 1.0, 4.0)
    return {"owners": owners, "row_offsets": row_offsets, "col_offsets": col_offsets, "samples": samples, "coords": coords, "taper_rows": taper_rows, "taper_cols": taper_cols}


def kernel_weights(distance):
    return jnp.square(jnp.maximum(1.0 - jnp.square(distance * 0.25), 0.0))

def grid_block(block_samples, block_coords):
    cell_pos = jnp.arange(SUB, dtype=jnp.float32)
    along_u = kernel_weights(cell_pos[None, :, None] - block_coords[:, 0, None, :]).astype(jnp.bfloat16)
    along_v = kernel_weights(cell_pos[None, None, :] - block_coords[:, 1, :, None])
    weighted = (jnp.transpose(block_samples, (0, 2, 1)).astype(jnp.float32)[:, :, :, None] * along_v[:, :, None, :]).astype(jnp.bfloat16)
    weighted = weighted.reshape(block_samples.shape[0], block_samples.shape[2], 2 * SUB)
    return jnp.einsum('sxk,skz->sxz', along_u.astype(jnp.float32), weighted.astype(jnp.float32)).astype(jnp.bfloat16)

def reference(owners, row_offsets, col_offsets, samples, coords, taper_rows, taper_cols):
    total = jnp.zeros((G * 2 * G,), jnp.float32)
    cell_steps = jnp.arange(SUB, dtype=jnp.int32)
    part_steps = jnp.arange(2, dtype=jnp.int32)
    for epoch_num in range(EPOCHS):
        epoch_samples = samples[epoch_num].reshape(TILES, S_DEV, 2, NK)
        epoch_coords = coords[epoch_num].reshape(TILES, S_DEV, 2, NK)
        subgrids = lax.map(lambda pair: grid_block(pair[0], pair[1]), (epoch_samples, epoch_coords))
        subgrids = subgrids.reshape(SLOTS, SUB, 2, SUB)
        slot_owner = owners[epoch_num].astype(jnp.int32)
        counts = jnp.zeros((TILES,), jnp.float32).at[slot_owner].add(1.0)
        weight = 1.0 / counts[slot_owner]
        row_index = (slot_owner * BAND + row_offsets[epoch_num]).astype(jnp.int32)[:, None] + cell_steps[None, :]
        col_index = col_offsets[epoch_num].astype(jnp.int32)[:, None] + cell_steps[None, :]
        flat_index = (row_index[:, :, None, None] * 2 + part_steps[None, None, :, None]) * G + col_index[:, None, None, :]
        values = subgrids.astype(jnp.float32) * weight[:, None, None, None]
        band_grid = jnp.zeros((G * 2 * G,), jnp.float32).at[flat_index.reshape(-1)].add(values.reshape(-1))
        rounded = lax.optimization_barrier(band_grid.astype(jnp.bfloat16)).astype(jnp.float32)
        total = total + rounded
    grid = total.reshape(G, 2, G)
    complex_grid = lax.complex(grid[:, 0, :], grid[:, 1, :])
    score_sum = jnp.real(jnp.fft.ifft2(complex_grid)) * float(G * G)
    reordered = score_sum.reshape(G, BAND, TILES).transpose(0, 2, 1).reshape(G, G)
    arranged = reordered.reshape(BAND, TILES, G).transpose(1, 0, 2)
    image_scale = math.sqrt(S_DEV) / (64.0 * TILES * math.sqrt(EPOCHS))
    result = arranged * image_scale * taper_rows[:, :, None] * taper_cols[None, None, :]
    return result.astype(jnp.float32)
```

```python
import functools
import math

import jax
import jax.numpy as jnp
import numpy as np
from jax import lax
from jax.experimental import pallas as pl
from jax.experimental.pallas import tpu as pltpu
from jax.sharding import PartitionSpec as P

SUB = 32
LANES = 128
EDGE = 16
FIELDS = 8
UNROLL = 8
VMEM_BYTES = 56 * 1024 * 1024
MESH = pl.DeviceIdType.MESH


def dft(values, wanted, modulus=None):
    count = len(values)
    if all(v is None for v in values):
        return [None] * wanted
    if count == 1:
        return list(values)
    half = count // 2
    need = min(wanted, half)
    even, odd = dft(values[0::2], need), dft(values[1::2], need)
    low, high = [], []
    for k in range(need):
        e, o = even[k], odd[k]
        t = None if o is None else turn(o, k, count)
        low.append(plus(e, t))
        if half + k < wanted:
            high.append(minus(e, t))
    return low + high


def turn(value, k, count):
    re, im = value
    s = math.sqrt(0.5)
    k %= count
    if k == 0:
        return re, im
    if 2 * k == count:
        return -re, -im
    if 4 * k == count:
        return -im, re
    if 8 * k == count:
        return (re - im) * s, (re + im) * s
    if 8 * k == 3 * count:
        return (re + im) * -s, (re - im) * s
    c, s = math.cos(2 * math.pi * k / count), math.sin(2 * math.pi * k / count)
    return re * c - im * s, re * s + im * c


def plus(a, b):
    if a is None or b is None:
        return b if a is None else a
    return a[0] + b[0], a[1] + b[1]


def minus(a, b):
    if b is None:
        return a
    if a is None:
        return -b[0], -b[1]
    return a[0] - b[0], a[1] - b[1]


def epoch_turn(value, j, epoch, epoch_count):
    angles = [2 * math.pi * ((j * e) % epoch_count) / epoch_count for e in range(epoch_count)]

    def pick(numbers):
        chosen = jnp.float32(numbers[0])
        for e in range(1, epoch_count):
            chosen = jnp.where(epoch == e, jnp.float32(numbers[e]), chosen)
        return chosen

    cos, sin = [round(math.cos(a), 15) for a in angles], [round(math.sin(a), 15) for a in angles]
    re, im = value
    if not any(sin):
        if all(c == 1.0 for c in cos):
            return value
        c = pick(cos)
        return re * c, im * c
    c, s = pick(cos), pick(sin)
    return re * c - im * s, re * s + im * c


def grid_kernel(
    sizes, owner_ref, row_ref, col_ref, coords_ref, samples_ref, pool_ref, meta_ref, *scratch
):
    tile_count, epoch_count, capacity, lane_step, band = sizes
    packed, points, t_send, t_recv, x_send, x_recv = scratch
    me, epoch = lax.axis_index("tile"), lax.axis_index("epoch")
    n_slots = owner_ref.shape[1]
    n_samples = coords_ref.shape[1] // 2
    half = tile_count // 2
    per_meta = LANES // lane_step
    groups = -(-tile_count // per_meta)
    slot_rows = SUB // 2

    barrier = pltpu.get_barrier_semaphore()

    def greet(k, carry):
        peer = lax.rem(me + k, tile_count)
        pl.semaphore_signal(barrier, inc=1, device_id={"tile": peer}, device_id_type=MESH)
        return carry

    lax.fori_loop(1, tile_count, greet, 0)
    for k in range(1, epoch_count):
        peer = lax.rem(epoch + k, epoch_count)
        pl.semaphore_signal(barrier, inc=1, device_id={"epoch": peer}, device_id_type=MESH)

    owner = owner_ref[...]
    mirrored = owner >= half
    target = jnp.where(mirrored, 2 * (tile_count - 1 - owner) + 1, 2 * owner)
    row = jnp.where(mirrored, band - (SUB - 1) - row_ref[...], row_ref[...])
    col = jnp.where(mirrored, tile_count * band - (SUB - 1) - col_ref[...], col_ref[...])
    mine = lax.broadcasted_iota(jnp.int32, (tile_count, n_slots), 0) == target
    before = lax.broadcasted_iota(jnp.int32, (n_slots, n_slots), 0) < lax.broadcasted_iota(
        jnp.int32, (n_slots, n_slots), 1
    )
    rank = jnp.dot(
        jnp.where(mine, 1.0, 0.0).astype(jnp.bfloat16),
        jnp.where(before, 1.0, 0.0).astype(jnp.bfloat16),
        preferred_element_type=jnp.float32,
    ).astype(jnp.int32)
    key = jnp.where(mine, rank, -LANES)
    fields = [jnp.ones_like(row), row, col // LANES, col % LANES]
    fields = jnp.concatenate(fields + [jnp.zeros_like(row)] * (EDGE - len(fields)), 0)
    fields = fields.astype(jnp.float32).astype(jnp.bfloat16)
    lane = lax.broadcasted_iota(jnp.int32, (LANES, n_slots), 0) - lax.rem(me, per_meta) * lane_step
    first = lax.broadcasted_iota(jnp.int32, (lane_step, n_slots), 0)
    hits = []
    for t in range(tile_count):
        hits.append(jnp.where(key[t : t + 1] == first, 1.0, 0.0))
        spot = jnp.where(key[t : t + 1] == lane, 1.0, 0.0).astype(jnp.bfloat16)
        packed[t, capacity * slot_rows :, :] = lax.dot_general(
            fields, spot, (((1,), (1,)), ((), ())), preferred_element_type=jnp.float32
        ).astype(jnp.bfloat16)
    hits = jnp.concatenate(hits, 0)
    here = jnp.dot(
        hits,
        coords_ref[...] * 0.25,
        precision=lax.Precision.HIGHEST,
        preferred_element_type=jnp.float32,
    )
    values = jnp.dot(
        hits.astype(jnp.bfloat16), samples_ref[...], preferred_element_type=jnp.float32
    )
    for t in range(tile_count):
        rows = slice(t * lane_step, (t + 1) * lane_step)
        points[t, 0:lane_step] = here[rows]
        points[t, lane_step:] = values[rows]

    pl.semaphore_wait(barrier, tile_count + epoch_count - 2)

    cell_iota = lax.broadcasted_iota(jnp.int32, (SUB, n_samples), 0)

    def weights(cells, at):
        distance = cells - at
        return jnp.square(jnp.maximum(1.0 - distance * distance, 0.0))

    def make(tile):
        flip = lax.rem(tile, 2)
        cells = jnp.where(flip == 1, SUB - 1 - cell_iota, cell_iota).astype(jnp.float32) * 0.25
        sign = (1 - 2 * flip).astype(jnp.float32)
        for k in range(capacity):
            along_u = weights(cells, points[tile, k : k + 1, :n_samples]).astype(jnp.bfloat16)
            along_v = weights(cells, points[tile, k : k + 1, n_samples:])
            at = lane_step + k
            re = points[tile, at : at + 1, :n_samples] * along_v
            im = (points[tile, at : at + 1, n_samples:] * sign) * along_v
            subgrid = lax.dot_general(
                along_u,
                jnp.concatenate([re, im], 0).astype(jnp.bfloat16),
                (((1,), (1,)), ((), ())),
                preferred_element_type=jnp.float32,
            )
            packed[tile, k * slot_rows : (k + 1) * slot_rows, :] = jnp.concatenate(
                [subgrid[:slot_rows], subgrid[slot_rows:]], 1
            ).astype(jnp.bfloat16)

    def tile_copy(k):
        peer = lax.rem(me + k, tile_count)
        return pltpu.make_async_remote_copy(
            src_ref=packed.at[peer],
            dst_ref=pool_ref.at[me],
            send_sem=t_send.at[k],
            recv_sem=t_recv.at[k],
            device_id={"tile": peer},
            device_id_type=MESH,
        )

    def epoch_copy(k, j):
        origin = lax.rem(me + tile_count - k, tile_count)
        return pltpu.make_async_remote_copy(
            src_ref=pool_ref.at[origin],
            dst_ref=pool_ref.at[j * tile_count + origin],
            send_sem=x_send.at[(j - 1) * tile_count + k],
            recv_sem=x_recv.at[(j - 1) * tile_count + k],
            device_id={"epoch": lax.rem(epoch + j, epoch_count)},
            device_id_type=MESH,
        )

    make(me)
    pool_ref[me] = packed[me]
    for j in range(1, epoch_count):
        epoch_copy(0, j).start()

    def send(k, carry):
        make(lax.rem(me + k, tile_count))
        tile_copy(k).start()
        return carry

    lax.fori_loop(1, tile_count, send, 0)

    def forward(k, carry):
        tile_copy(k).wait_recv()
        for j in range(1, epoch_count):
            epoch_copy(k, j).start()
        return carry

    lax.fori_loop(1, tile_count, forward, 0)

    def sent_all(k, carry):
        tile_copy(k).wait_send()
        return carry

    lax.fori_loop(1, tile_count, sent_all, 0)

    def crossed(k, carry):
        for j in range(1, epoch_count):
            epoch_copy(k, j).wait()
        return carry

    lax.fori_loop(0, tile_count, crossed, 0)

    for j in range(epoch_count):
        for g in range(groups):
            total = jnp.zeros((EDGE, LANES), jnp.float32)
            for s in range(g * per_meta, min(tile_count, (g + 1) * per_meta)):
                total += pool_ref[j * tile_count + s, capacity * slot_rows :, :].astype(jnp.float32)
            meta_ref[j * groups + g] = total[:FIELDS].astype(jnp.int32)


def band_kernel(
    sizes, meta_ref, pool_ref, cos_ref, sin_ref, second_ref, out_ref, acc, turned_ref, wanted, scale
):
    tile_count, epoch_count, capacity, lane_step, band = sizes
    epoch = lax.axis_index("epoch")
    lane_blocks, acc_rows = acc.shape[1] - 1, acc.shape[2]
    rows_here = band // epoch_count
    spare = acc_rows - SUB
    slot_rows = SUB // 2
    per_meta = LANES // lane_step
    groups = -(-tile_count // per_meta)
    first_row = epoch * rows_here - SUB

    def clear(i, carry):
        acc[0, i] = jnp.zeros((acc_rows, LANES), jnp.float32)
        acc[1, i] = jnp.zeros((acc_rows, LANES), jnp.float32)
        return carry

    lax.fori_loop(0, lane_blocks + 1, clear, 0)

    found = jnp.int32(0)
    for e in range(epoch_count):
        held = jnp.int32(0)
        for g in range(groups):
            at = e * groups + g

            def look(s, carry, at=at):
                found, held = carry
                for k in range(capacity):
                    lane = s * lane_step + k
                    valid = meta_ref[at, 0, lane]
                    row = meta_ref[at, 1, lane] - first_row
                    inside = (valid > 0) & (row > 0) & (row < rows_here + SUB)
                    wanted[found] = at * LANES + lane
                    found += jnp.where(inside, 1, 0)
                    held += valid
                return found, held

            count = min(tile_count - g * per_meta, per_meta)
            found, held = lax.fori_loop(0, count, look, (found, held))
        scale[e] = 1.0 / jnp.full((SUB, LANES), jnp.maximum(held, 1), jnp.int32).astype(jnp.float32)
    for k in range(UNROLL):
        wanted[found + k] = -1

    shape = (SUB, 2 * LANES)
    steps = lax.broadcasted_iota(jnp.int32, shape, 1) - lax.broadcasted_iota(jnp.int32, shape, 0)

    def per_batch(b, carry):
        placed = []
        for k in range(UNROLL):
            entry = wanted[b * UNROLL + k]
            index = jnp.maximum(entry, 0)
            at, lane = index // LANES, lax.rem(index, LANES)
            e, g = at // groups, lax.rem(at, groups)
            source = e * tile_count + g * per_meta + lane // lane_step
            row = jnp.where(entry < 0, spare, meta_ref[at, 1, lane] - first_row)
            block = meta_ref[at, 2, lane]
            start = meta_ref[at, 3, lane]
            first = pl.multiple_of(lax.rem(lane, lane_step) * slot_rows, slot_rows)
            data = pool_ref[source, pl.ds(first, slot_rows), :]
            parts = jnp.concatenate(
                [data[:, i * SUB : (i + 1) * SUB] for i in (0, 2, 1, 3)], 0
            )
            select = jnp.where(steps == start, 1.0, 0.0).astype(jnp.bfloat16)
            window = jnp.dot(parts, select, preferred_element_type=jnp.float32)
            placed.append((row, block, scale[e], window))
        for row, block, factor, window in placed:
            for p in range(2):
                for h in range(2):
                    acc[p, block + h, pl.ds(row, SUB), :] += (
                        window[p * SUB : (p + 1) * SUB, h * LANES : (h + 1) * LANES] * factor
                    )
        return carry

    lax.fori_loop(0, (found + UNROLL - 1) // UNROLL, per_batch, 0)

    block_len = band
    group = min(16, rows_here)
    width = min(LANES, block_len)
    chunks = block_len // width

    def per_group(first, size):
        for h in range(chunks):
            values = []
            for a in range(tile_count):
                col = a * block_len + h * width
                lane, at = col % LANES, col // LANES
                value = [acc[p, at, pl.ds(SUB + first, size), lane : lane + width] for p in range(2)]
                if col == 0:
                    for p in range(2):
                        value[p] += acc[p, lane_blocks, pl.ds(SUB + first, size), :width]
                values.append(tuple(value))
            lanes = slice(h * width, (h + 1) * width)
            for m, (re, im) in enumerate(dft(values, tile_count)):
                c, s = cos_ref[m : m + 1, lanes], sin_ref[m : m + 1, lanes]
                turned = (re * c - im * s, re * s + im * c)
                for p in range(2):
                    start = p * block_len + h * width
                    turned_ref[m, pl.ds(first, size), start : start + width] = turned[p].astype(
                        jnp.bfloat16
                    )

    def row_group(i, carry):
        per_group(pl.multiple_of(i * group, group), group)
        return carry

    lax.fori_loop(0, rows_here // group, row_group, 0)
    per_group(rows_here, EDGE)

    parts = 2 * chunks
    edge_row = lax.broadcasted_iota(jnp.int32, (EDGE, width), 0)
    has_edge = jnp.where(epoch == epoch_count - 1, 1.0, 0.0)

    def per_tile(m, carry):
        moved = jnp.dot(turned_ref[m], second_ref[...], preferred_element_type=jnp.float32)
        edge = jnp.zeros((EDGE, width), jnp.float32)
        for q in range(parts):
            piece = moved[:, q * width : (q + 1) * width]
            out_ref[m, q * rows_here : (q + 1) * rows_here, :] = piece[:rows_here].astype(
                jnp.bfloat16
            )
            edge = jnp.where(edge_row == q, piece[rows_here : rows_here + 1] * has_edge, edge)
        out_ref[m, parts * rows_here :, :] = edge.astype(jnp.bfloat16)
        return carry

    lax.fori_loop(0, tile_count, per_tile, 0)


def swap_kernel(tile_count, epoch_count, own_ref, full_ref, *scratch):
    landed, folded, p_send, p_recv, t_send, t_recv, x_send, x_recv = scratch
    me, epoch = lax.axis_index("tile"), lax.axis_index("epoch")
    half = tile_count // 2
    mine, side = me // 2, lax.rem(me, 2)
    partner = me + 1 - 2 * side

    barrier = pltpu.get_barrier_semaphore()

    def greet(k, carry):
        peer = lax.rem(mine + k, half) * 2 + side
        pl.semaphore_signal(barrier, inc=1, device_id={"tile": peer}, device_id_type=MESH)
        return carry

    lax.fori_loop(1, half, greet, 0)
    pl.semaphore_signal(barrier, inc=1, device_id={"tile": partner}, device_id_type=MESH)
    for k in range(1, epoch_count):
        peer = lax.rem(epoch + k, epoch_count)
        pl.semaphore_signal(barrier, inc=1, device_id={"epoch": peer}, device_id_type=MESH)
    pl.semaphore_wait(barrier, half + epoch_count - 1)

    def partner_copy(k):
        return pltpu.make_async_remote_copy(
            src_ref=own_ref.at[lax.rem(mine + k, half) * 2 + 1 - side],
            dst_ref=landed.at[k],
            send_sem=p_send.at[k],
            recv_sem=p_recv.at[k],
            device_id={"tile": partner},
            device_id_type=MESH,
        )

    def tile_copy(k):
        return pltpu.make_async_remote_copy(
            src_ref=folded.at[k],
            dst_ref=full_ref.at[epoch * half + mine],
            send_sem=t_send.at[k],
            recv_sem=t_recv.at[k],
            device_id={"tile": lax.rem(mine + k, half) * 2 + side},
            device_id_type=MESH,
        )

    def epoch_copy(k, j):
        origin = epoch * half + lax.rem(mine + half - k, half)
        return pltpu.make_async_remote_copy(
            src_ref=full_ref.at[origin],
            dst_ref=full_ref.at[origin],
            send_sem=x_send.at[(j - 1) * half + k],
            recv_sem=x_recv.at[(j - 1) * half + k],
            device_id={"epoch": lax.rem(epoch + j, epoch_count)},
            device_id_type=MESH,
        )

    def give(k, carry):
        partner_copy(k).start()
        return carry

    lax.fori_loop(0, half, give, 0)

    def fold(k):
        partner_copy(k).wait_recv()
        both = own_ref[lax.rem(mine + k, half) * 2 + side].astype(jnp.float32) + landed[k].astype(
            jnp.float32
        )
        return both.astype(jnp.bfloat16)

    full_ref[epoch * half + mine] = fold(0)
    for j in range(1, epoch_count):
        epoch_copy(0, j).start()

    def send(k, carry):
        folded[k] = fold(k)
        tile_copy(k).start()
        return carry

    lax.fori_loop(1, half, send, 0)

    def forward(k, carry):
        tile_copy(k).wait_recv()
        for j in range(1, epoch_count):
            epoch_copy(k, j).start()
        return carry

    lax.fori_loop(1, half, forward, 0)

    def finish(k, carry):
        tile_copy(k).wait_send()
        return carry

    lax.fori_loop(1, half, finish, 0)

    def settle(k, carry):
        partner_copy(k).wait_send()
        for j in range(1, epoch_count):
            epoch_copy(k, j).wait()
        return carry

    lax.fori_loop(0, half, settle, 0)


def image_kernel(
    sizes, image_scale, epoch_ref, full_ref, last_ref, rows_ref, cols_ref, out_ref, mixed
):
    tile_count, epoch_count = sizes
    half, kept = tile_count // 2, tile_count // epoch_count
    width = full_ref.shape[2]
    block_len = out_ref.shape[1]
    chunks = block_len // width
    parts = 2 * chunks
    rows_here = block_len // epoch_count
    group = min(16, rows_here)
    epoch = epoch_ref[0]

    @pl.when(pl.program_id(0) == 0)
    def _():
        def per_group(e, first, edges):
            for h in range(chunks):
                values = []
                for j in range(half):
                    value = tuple(
                        full_ref[
                            e * half + j, pl.ds((h * 2 + p) * rows_here + first, group), :
                        ].astype(jnp.float32)
                        for p in range(2)
                    )
                    values.append(epoch_turn(value, j, epoch, epoch_count))
                done = dft(values + [None] * half, kept)
                if edges is not None:
                    top = lax.broadcasted_iota(jnp.int32, (group, width), 0) == 0
                    done = [
                        tuple(a + jnp.where(top, b, 0.0) for a, b in zip(part, edge))
                        for part, edge in zip(done, edges[h])
                    ]
                for c, part in enumerate(done):
                    for p in range(2):
                        row = p * block_len + e * rows_here + first
                        if not isinstance(row, int):
                            row = pl.multiple_of(row, group)
                        mixed[c, pl.ds(row, group), h * width : (h + 1) * width] = part[p].astype(
                            jnp.bfloat16
                        )

        edges = []
        for h in range(chunks):
            values = [None]
            for j in range(half):
                block = full_ref[(epoch_count - 1) * half + j, parts * rows_here :, :].astype(
                    jnp.float32
                )
                value = tuple(block[h * 2 + p : h * 2 + p + 1] for p in range(2))
                values.append(epoch_turn(value, j + 1, epoch, epoch_count))
            edges.append(dft(values + [None] * (tile_count - half - 1), kept))
        per_group(0, 0, edges)
        for e in range(epoch_count):

            def step(i, carry, e=e):
                per_group(e, pl.multiple_of(i * group, group), None)
                return carry

            lax.fori_loop(1 if e == 0 else 0, rows_here // group, step, 0)

    c = pl.program_id(0)
    pixels = jnp.dot(last_ref[0], mixed[c], preferred_element_type=jnp.float32)
    out_ref[0] = pixels * (rows_ref[0] * image_scale) * cols_ref[...]


def turns(product, modulus):
    angles = (product % modulus) * (2.0 * math.pi / modulus)
    return np.cos(angles), np.sin(angles)


def make_tables(tile_count, block_len):
    grid_size = tile_count * block_len
    long_idx = np.arange(block_len)
    tile_idx = np.arange(tile_count)
    turn_cos, turn_sin = turns(tile_idx[:, None] * long_idx[None, :], grid_size)
    c, s = turns(long_idx[:, None] * long_idx[None, :], block_len)
    second = np.stack([np.stack([c, s], 1), np.stack([-s, c], 1)], 0)
    width = min(LANES, block_len)
    second = second.reshape(2 * block_len, 2, block_len // width, width)
    second = second.transpose(0, 2, 1, 3).reshape(2 * block_len, 2 * block_len)
    pixel = long_idx[None, :] * tile_count + tile_idx[:, None]
    c, s = turns(pixel[:, :, None] * long_idx[None, None, :], grid_size)
    last = np.concatenate([c, -s], -1)
    return (
        turn_cos.astype(np.float32),
        turn_sin.astype(np.float32),
        second.astype(jnp.bfloat16),
        last.astype(jnp.bfloat16),
    )


def vmem(count):
    return [pl.BlockSpec(memory_space=pltpu.VMEM)] * count


def body(tables, owners, row_offsets, col_offsets, samples, coords, taper_rows, taper_cols):
    tile_count = lax.axis_size("tile")
    epoch_count = lax.axis_size("epoch")
    n_slots = owners.shape[1]
    n_samples = samples.shape[3]
    capacity = max(2, n_slots * 5 // (4 * tile_count))
    capacity += capacity % 2
    lane_step = max(8, 1 << (capacity - 1).bit_length())
    band = taper_cols.shape[0]
    width = min(LANES, band)
    half, kept = tile_count // 2, tile_count // epoch_count
    rows_here = band // epoch_count
    parts = 2 * (band // width)
    turn_cos, turn_sin, second, last = tables
    sizes = (tile_count, epoch_count, capacity, lane_step, band)
    block_rows = capacity * SUB // 2 + EDGE
    meta_rows = epoch_count * -(-tile_count // (LANES // lane_step))

    tile_sems = pltpu.SemaphoreType.DMA((tile_count,))
    epoch_sems = pltpu.SemaphoreType.DMA(((epoch_count - 1) * tile_count,))
    pool, meta = pl.pallas_call(
        functools.partial(grid_kernel, sizes),
        out_shape=[
            jax.ShapeDtypeStruct((epoch_count * tile_count, block_rows, LANES), jnp.bfloat16),
            jax.ShapeDtypeStruct((meta_rows, FIELDS, LANES), jnp.int32),
        ],
        in_specs=vmem(5),
        out_specs=vmem(2),
        scratch_shapes=[
            pltpu.VMEM((tile_count, block_rows, LANES), jnp.bfloat16),
            pltpu.VMEM((tile_count, 2 * lane_step, 2 * n_samples), jnp.float32),
            tile_sems,
            tile_sems,
            epoch_sems,
            epoch_sems,
        ],
        compiler_params=pltpu.CompilerParams(
            vmem_limit_bytes=VMEM_BYTES, collective_id=1, has_side_effects=True
        ),
        name="grid_slots",
    )(
        owners,
        row_offsets,
        col_offsets,
        coords.reshape(n_slots, 2 * n_samples),
        samples.reshape(n_slots, 2 * n_samples),
    )

    lane_blocks = tile_count * band // LANES
    block_shape = (parts * rows_here + EDGE, width)
    own = pl.pallas_call(
        functools.partial(band_kernel, sizes),
        out_shape=jax.ShapeDtypeStruct((tile_count, *block_shape), jnp.bfloat16),
        in_specs=[pl.BlockSpec(memory_space=pltpu.SMEM)] + vmem(4),
        out_specs=vmem(1)[0],
        scratch_shapes=[
            pltpu.VMEM((2, lane_blocks + 1, rows_here + 3 * SUB, LANES), jnp.float32),
            pltpu.VMEM((tile_count, rows_here + EDGE, 2 * band), jnp.bfloat16),
            pltpu.SMEM((epoch_count * tile_count * capacity + UNROLL,), jnp.int32),
            pltpu.VMEM((epoch_count, SUB, LANES), jnp.float32),
        ],
        compiler_params=pltpu.CompilerParams(vmem_limit_bytes=VMEM_BYTES),
        name="band_rows",
    )(meta, pool, jnp.asarray(turn_cos), jnp.asarray(turn_sin), jnp.asarray(second))

    half_sems = pltpu.SemaphoreType.DMA((half,))
    epoch_sems = pltpu.SemaphoreType.DMA(((epoch_count - 1) * half,))
    full = pl.pallas_call(
        functools.partial(swap_kernel, tile_count, epoch_count),
        out_shape=jax.ShapeDtypeStruct((epoch_count * half, *block_shape), jnp.bfloat16),
        in_specs=vmem(1),
        out_specs=vmem(1)[0],
        scratch_shapes=[
            pltpu.VMEM((half, *block_shape), jnp.bfloat16),
            pltpu.VMEM((half, *block_shape), jnp.bfloat16),
            half_sems,
            half_sems,
            half_sems,
            half_sems,
            epoch_sems,
            epoch_sems,
        ],
        compiler_params=pltpu.CompilerParams(
            vmem_limit_bytes=VMEM_BYTES, collective_id=0, has_side_effects=True
        ),
        name="swap_rows",
    )(own)

    image_scale = math.sqrt(n_slots) / (64.0 * tile_count * math.sqrt(epoch_count))
    return pl.pallas_call(
        functools.partial(image_kernel, (tile_count, epoch_count), image_scale),
        grid_spec=pltpu.PrefetchScalarGridSpec(
            num_scalar_prefetch=1,
            grid=(kept,),
            in_specs=[
                pl.BlockSpec(memory_space=pltpu.VMEM),
                pl.BlockSpec((1, band, 2 * band), lambda c, e: (e[0] * kept + c, 0, 0)),
                pl.BlockSpec((1, band, 1), lambda c, e: (c, 0, 0)),
                pl.BlockSpec((1, band), lambda c, e: (0, 0)),
            ],
            out_specs=pl.BlockSpec((1, band, band), lambda c, e: (c, 0, 0)),
            scratch_shapes=[pltpu.VMEM((kept, 2 * band, band), jnp.bfloat16)],
        ),
        out_shape=jax.ShapeDtypeStruct((kept, band, band), jnp.float32),
        compiler_params=pltpu.CompilerParams(vmem_limit_bytes=VMEM_BYTES),
        name="image_rows",
    )(
        lax.axis_index("epoch").astype(jnp.int32)[None],
        full,
        jnp.asarray(last),
        taper_rows[:, :, None],
        taper_cols[None, :],
    )


def solution(mesh):
    placed = (
        P("epoch", "tile"),
        P("epoch", "tile"),
        P("epoch", "tile"),
        P("epoch", "tile", None, None),
        P("epoch", "tile", None, None),
        P("epoch", None),
        P("tile"),
    )

    def whole(owners, row_offsets, col_offsets, samples, coords, taper_rows, taper_cols):
        tables = make_tables(mesh.shape["tile"], taper_cols.shape[0] // mesh.shape["tile"])
        return jax.shard_map(
            functools.partial(body, tables),
            mesh=mesh,
            in_specs=placed,
            out_specs=P("epoch", None, "tile"),
            check_vma=False,
        )(owners, row_offsets, col_offsets, samples, coords, taper_rows, taper_cols)

    return whole
```

```python
import functools
import math

import jax
import jax.numpy as jnp
import numpy as np
from jax import lax
from jax.experimental import pallas as pl
from jax.experimental.pallas import tpu as pltpu
from jax.sharding import PartitionSpec as P

SUB = 32
LANES = 128
EDGE = 16
FIELDS = 8
UNROLL = 8
VMEM_BYTES = 56 * 1024 * 1024
MESH = pl.DeviceIdType.MESH


def dft(values, wanted, modulus=None):
    count = len(values)
    if all(v is None for v in values):
        return [None] * wanted
    if count == 1:
        return list(values)
    half = count // 2
    need = min(wanted, half)
    even, odd = dft(values[0::2], need), dft(values[1::2], need)
    low, high = [], []
    for k in range(need):
        e, o = even[k], odd[k]
        t = None if o is None else turn(o, k, count)
        low.append(plus(e, t))
        if half + k < wanted:
            high.append(minus(e, t))
    return low + high


def turn(value, k, count):
    re, im = value
    s = math.sqrt(0.5)
    k %= count
    if k == 0:
        return re, im
    if 2 * k == count:
        return -re, -im
    if 4 * k == count:
        return -im, re
    if 8 * k == count:
        return (re - im) * s, (re + im) * s
    if 8 * k == 3 * count:
        return (re + im) * -s, (re - im) * s
    c, s = math.cos(2 * math.pi * k / count), math.sin(2 * math.pi * k / count)
    return re * c - im * s, re * s + im * c


def plus(a, b):
    if a is None or b is None:
        return b if a is None else a
    return a[0] + b[0], a[1] + b[1]


def minus(a, b):
    if b is None:
        return a
    if a is None:
        return -b[0], -b[1]
    return a[0] - b[0], a[1] - b[1]


def epoch_turn(value, j, epoch, epoch_count):
    angles = [2 * math.pi * ((j * e) % epoch_count) / epoch_count for e in range(epoch_count)]

    def pick(numbers):
        chosen = jnp.float32(numbers[0])
        for e in range(1, epoch_count):
            chosen = jnp.where(epoch == e, jnp.float32(numbers[e]), chosen)
        return chosen

    cos, sin = [round(math.cos(a), 15) for a in angles], [round(math.sin(a), 15) for a in angles]
    re, im = value
    if not any(sin):
        if all(c == 1.0 for c in cos):
            return value
        c = pick(cos)
        return re * c, im * c
    c, s = pick(cos), pick(sin)
    return re * c - im * s, re * s + im * c


def grid_kernel(
    sizes, owner_ref, row_ref, col_ref, coords_ref, samples_ref, pool_ref, meta_ref, *scratch
):
    tile_count, epoch_count, capacity, lane_step, band = sizes
    packed, points, t_send, t_recv, x_send, x_recv = scratch
    me, epoch = lax.axis_index("tile"), lax.axis_index("epoch")
    n_slots = owner_ref.shape[1]
    n_samples = coords_ref.shape[3]
    half = tile_count // 2
    per_meta = LANES // lane_step
    groups = -(-tile_count // per_meta)
    slot_rows = SUB // 2

    barrier = pltpu.get_barrier_semaphore()

    def greet(k, carry):
        peer = lax.rem(me + k, tile_count)
        pl.semaphore_signal(barrier, inc=1, device_id={"tile": peer}, device_id_type=MESH)
        return carry

    lax.fori_loop(1, tile_count, greet, 0)
    for k in range(1, epoch_count):
        peer = lax.rem(epoch + k, epoch_count)
        pl.semaphore_signal(barrier, inc=1, device_id={"epoch": peer}, device_id_type=MESH)

    owner = owner_ref[...]
    mirrored = owner >= half
    target = jnp.where(mirrored, 2 * (tile_count - 1 - owner) + 1, 2 * owner)
    row = jnp.where(mirrored, band - (SUB - 1) - row_ref[...], row_ref[...])
    col = jnp.where(mirrored, tile_count * band - (SUB - 1) - col_ref[...], col_ref[...])
    mine = lax.broadcasted_iota(jnp.int32, (tile_count, n_slots), 0) == target
    before = lax.broadcasted_iota(jnp.int32, (n_slots, n_slots), 0) < lax.broadcasted_iota(
        jnp.int32, (n_slots, n_slots), 1
    )
    rank = jnp.dot(
        jnp.where(mine, 1.0, 0.0).astype(jnp.bfloat16),
        jnp.where(before, 1.0, 0.0).astype(jnp.bfloat16),
        preferred_element_type=jnp.float32,
    ).astype(jnp.int32)
    key = jnp.where(mine, rank, -LANES)
    fields = [jnp.ones_like(row), row, col // LANES, col % LANES]
    fields = jnp.concatenate(fields + [jnp.zeros_like(row)] * (EDGE - len(fields)), 0)
    fields = fields.astype(jnp.float32).astype(jnp.bfloat16)
    lane = lax.broadcasted_iota(jnp.int32, (LANES, n_slots), 0) - lax.rem(me, per_meta) * lane_step
    first = lax.broadcasted_iota(jnp.int32, (lane_step, n_slots), 0)
    hits = []
    for t in range(tile_count):
        hits.append(jnp.where(key[t : t + 1] == first, 1.0, 0.0))
        spot = jnp.where(key[t : t + 1] == lane, 1.0, 0.0).astype(jnp.bfloat16)
        packed[t, capacity * slot_rows :, :] = lax.dot_general(
            fields, spot, (((1,), (1,)), ((), ())), preferred_element_type=jnp.float32
        ).astype(jnp.bfloat16)
    hits = jnp.concatenate(hits, 0)
    here = jnp.dot(
        hits,
        jnp.concatenate([coords_ref[0, :, p, :] for p in range(2)], 1) * 0.25,
        precision=lax.Precision.HIGHEST,
        preferred_element_type=jnp.float32,
    )
    samples = samples_ref[0].astype(jnp.float32)
    samples = jnp.concatenate([samples[:, p, :] for p in range(2)], 1).astype(jnp.bfloat16)
    values = jnp.dot(hits.astype(jnp.bfloat16), samples, preferred_element_type=jnp.float32)
    for t in range(tile_count):
        rows = slice(t * lane_step, (t + 1) * lane_step)
        points[t, 0:lane_step] = here[rows]
        points[t, lane_step:] = values[rows]

    pl.semaphore_wait(barrier, tile_count + epoch_count - 2)

    cell_iota = lax.broadcasted_iota(jnp.int32, (SUB, n_samples), 0)

    def weights(cells, at):
        distance = cells - at
        return jnp.square(jnp.maximum(1.0 - distance * distance, 0.0))

    def make(tile):
        flip = lax.rem(tile, 2)
        cells = jnp.where(flip == 1, SUB - 1 - cell_iota, cell_iota).astype(jnp.float32) * 0.25
        sign = (1 - 2 * flip).astype(jnp.float32)
        for k in range(capacity):
            along_u = weights(cells, points[tile, k : k + 1, :n_samples]).astype(jnp.bfloat16)
            along_v = weights(cells, points[tile, k : k + 1, n_samples:])
            at = lane_step + k
            re = points[tile, at : at + 1, :n_samples] * along_v
            im = (points[tile, at : at + 1, n_samples:] * sign) * along_v
            subgrid = lax.dot_general(
                along_u,
                jnp.concatenate([re, im], 0).astype(jnp.bfloat16),
                (((1,), (1,)), ((), ())),
                preferred_element_type=jnp.float32,
            )
            packed[tile, k * slot_rows : (k + 1) * slot_rows, :] = jnp.concatenate(
                [subgrid[:slot_rows], subgrid[slot_rows:]], 1
            ).astype(jnp.bfloat16)

    def tile_copy(k):
        peer = lax.rem(me + k, tile_count)
        return pltpu.make_async_remote_copy(
            src_ref=packed.at[peer],
            dst_ref=pool_ref.at[me],
            send_sem=t_send.at[k],
            recv_sem=t_recv.at[k],
            device_id={"tile": peer},
            device_id_type=MESH,
        )

    def epoch_copy(k, j):
        origin = lax.rem(me + tile_count - k, tile_count)
        return pltpu.make_async_remote_copy(
            src_ref=pool_ref.at[origin],
            dst_ref=pool_ref.at[j * tile_count + origin],
            send_sem=x_send.at[(j - 1) * tile_count + k],
            recv_sem=x_recv.at[(j - 1) * tile_count + k],
            device_id={"epoch": lax.rem(epoch + j, epoch_count)},
            device_id_type=MESH,
        )

    make(me)
    pool_ref[me] = packed[me]
    for j in range(1, epoch_count):
        epoch_copy(0, j).start()

    def send(k, carry):
        make(lax.rem(me + k, tile_count))
        tile_copy(k).start()
        return carry

    lax.fori_loop(1, tile_count, send, 0)

    def forward(k, carry):
        tile_copy(k).wait_recv()
        for j in range(1, epoch_count):
            epoch_copy(k, j).start()
        return carry

    lax.fori_loop(1, tile_count, forward, 0)

    def sent_all(k, carry):
        tile_copy(k).wait_send()
        return carry

    lax.fori_loop(1, tile_count, sent_all, 0)

    def crossed(k, carry):
        for j in range(1, epoch_count):
            epoch_copy(k, j).wait()
        return carry

    lax.fori_loop(0, tile_count, crossed, 0)

    for j in range(epoch_count):
        for g in range(groups):
            total = jnp.zeros((EDGE, LANES), jnp.float32)
            for s in range(g * per_meta, min(tile_count, (g + 1) * per_meta)):
                total += pool_ref[j * tile_count + s, capacity * slot_rows :, :].astype(jnp.float32)
            meta_ref[j * groups + g] = total[:FIELDS].astype(jnp.int32)


def place_kernel(sizes, meta_ref, pool_ref, acc, wanted, scale):
    tile_count, epoch_count, capacity, lane_step, band = sizes
    epoch = lax.axis_index("epoch")
    lane_blocks, acc_rows = acc.shape[1] - 1, acc.shape[2]
    rows_here = band // epoch_count
    spare = acc_rows - SUB
    slot_rows = SUB // 2
    per_meta = LANES // lane_step
    groups = -(-tile_count // per_meta)
    first_row = epoch * rows_here - SUB

    def clear(i, carry):
        acc[0, i] = jnp.zeros((acc_rows, LANES), jnp.float32)
        acc[1, i] = jnp.zeros((acc_rows, LANES), jnp.float32)
        return carry

    lax.fori_loop(0, lane_blocks + 1, clear, 0)

    found = jnp.int32(0)
    for e in range(epoch_count):
        held = jnp.int32(0)
        for g in range(groups):
            at = e * groups + g

            def look(s, carry, at=at):
                found, held = carry
                for k in range(capacity):
                    lane = s * lane_step + k
                    valid = meta_ref[at, 0, lane]
                    row = meta_ref[at, 1, lane] - first_row
                    inside = (valid > 0) & (row > 0) & (row < rows_here + SUB)
                    wanted[found] = at * LANES + lane
                    found += jnp.where(inside, 1, 0)
                    held += valid
                return found, held

            count = min(tile_count - g * per_meta, per_meta)
            found, held = lax.fori_loop(0, count, look, (found, held))
        scale[e] = 1.0 / jnp.full((SUB, LANES), jnp.maximum(held, 1), jnp.int32).astype(jnp.float32)
    for k in range(UNROLL):
        wanted[found + k] = -1

    shape = (SUB, 2 * LANES)
    steps = lax.broadcasted_iota(jnp.int32, shape, 1) - lax.broadcasted_iota(jnp.int32, shape, 0)

    def per_batch(b, carry):
        placed = []
        for k in range(UNROLL):
            entry = wanted[b * UNROLL + k]
            index = jnp.maximum(entry, 0)
            at, lane = index // LANES, lax.rem(index, LANES)
            e, g = at // groups, lax.rem(at, groups)
            source = e * tile_count + g * per_meta + lane // lane_step
            row = jnp.where(entry < 0, spare, meta_ref[at, 1, lane] - first_row)
            block = meta_ref[at, 2, lane]
            start = meta_ref[at, 3, lane]
            first = pl.multiple_of(lax.rem(lane, lane_step) * slot_rows, slot_rows)
            data = pool_ref[source, pl.ds(first, slot_rows), :]
            parts = jnp.concatenate(
                [data[:, i * SUB : (i + 1) * SUB] for i in (0, 2, 1, 3)], 0
            )
            select = jnp.where(steps == start, 1.0, 0.0).astype(jnp.bfloat16)
            window = jnp.dot(parts, select, preferred_element_type=jnp.float32)
            placed.append((row, block, scale[e], window))
        for row, block, factor, window in placed:
            for p in range(2):
                for h in range(2):
                    acc[p, block + h, pl.ds(row, SUB), :] += (
                        window[p * SUB : (p + 1) * SUB, h * LANES : (h + 1) * LANES] * factor
                    )
        return carry

    lax.fori_loop(0, (found + UNROLL - 1) // UNROLL, per_batch, 0)


def swap_kernel(sizes, cuts, acc_ref, cos_ref, sin_ref, second_ref, mixed_ref, *scratch):
    tile_count, epoch_count, band = sizes
    turned, given, landed, folded, full = scratch[:5]
    p_send, p_recv, t_send, t_recv, x_send, x_recv = scratch[5:]
    me, epoch = lax.axis_index("tile"), lax.axis_index("epoch")
    half, kept = tile_count // 2, tile_count // epoch_count
    mine, side = me // 2, lax.rem(me, 2)
    partner = me + 1 - 2 * side
    rows_here = band // epoch_count
    cut_rows = rows_here // cuts
    width = min(LANES, band)
    chunks = band // width
    parts = 2 * chunks
    lane_blocks = acc_ref.shape[1] - 1
    group = min(16, cut_rows)
    batch = min(4, half)

    barrier = pltpu.get_barrier_semaphore()

    def greet(k, carry):
        peer = lax.rem(mine + k, half) * 2 + side
        pl.semaphore_signal(barrier, inc=1, device_id={"tile": peer}, device_id_type=MESH)
        return carry

    lax.fori_loop(1, half, greet, 0)
    pl.semaphore_signal(barrier, inc=1, device_id={"tile": partner}, device_id_type=MESH)
    for k in range(1, epoch_count):
        peer = lax.rem(epoch + k, epoch_count)
        pl.semaphore_signal(barrier, inc=1, device_id={"epoch": peer}, device_id_type=MESH)

    def rows_of(cut):
        edge = EDGE if cut == cuts - 1 else 0
        return pl.ds(cut * parts * cut_rows, parts * cut_rows + edge)

    def partner_copy(cut, k):
        return pltpu.make_async_remote_copy(
            src_ref=given.at[k, rows_of(cut)],
            dst_ref=landed.at[k, rows_of(cut)],
            send_sem=p_send.at[cut * half + k],
            recv_sem=p_recv.at[cut * half + k],
            device_id={"tile": partner},
            device_id_type=MESH,
        )

    def tile_copy(cut, k):
        return pltpu.make_async_remote_copy(
            src_ref=folded.at[k, rows_of(cut)],
            dst_ref=full.at[epoch * half + mine, rows_of(cut)],
            send_sem=t_send.at[cut * half + k],
            recv_sem=t_recv.at[cut * half + k],
            device_id={"tile": lax.rem(mine + k, half) * 2 + side},
            device_id_type=MESH,
        )

    def epoch_copy(cut, k, j):
        origin = epoch * half + lax.rem(mine + half - k, half)
        at = (cut * (epoch_count - 1) + j - 1) * half + k
        return pltpu.make_async_remote_copy(
            src_ref=full.at[origin, rows_of(cut)],
            dst_ref=full.at[origin, rows_of(cut)],
            send_sem=x_send.at[at],
            recv_sem=x_recv.at[at],
            device_id={"epoch": lax.rem(epoch + j, epoch_count)},
            device_id_type=MESH,
        )

    def transform(first, size):
        for h in range(chunks):
            values = []
            for a in range(tile_count):
                col = a * band + h * width
                lane, at = col % LANES, col // LANES
                value = [
                    acc_ref[p, at, pl.ds(SUB + first, size), lane : lane + width] for p in range(2)
                ]
                if col == 0:
                    for p in range(2):
                        value[p] += acc_ref[p, lane_blocks, pl.ds(SUB + first, size), :width]
                values.append(tuple(value))
            lanes = slice(h * width, (h + 1) * width)
            for m, (re, im) in enumerate(dft(values, tile_count)):
                c, s = cos_ref[m : m + 1, lanes], sin_ref[m : m + 1, lanes]
                pair = (re * c - im * s, re * s + im * c)
                for p in range(2):
                    start = p * band + h * width
                    turned[m, pl.ds(first, size), start : start + width] = pair[p].astype(
                        jnp.bfloat16
                    )

    edge_row = lax.broadcasted_iota(jnp.int32, (EDGE, width), 0)
    has_edge = jnp.where(epoch == epoch_count - 1, 1.0, 0.0)

    def sections(cut, tiles):
        rows = cut_rows + (EDGE if cut == cuts - 1 else 0)
        stack = [turned[tile, cut * cut_rows : cut * cut_rows + rows, :] for tile in tiles]
        moved = jnp.dot(
            jnp.concatenate(stack, 0), second_ref[...], preferred_element_type=jnp.float32
        )
        blocks = []
        for i in range(len(tiles)):
            pieces = [
                moved[i * rows : (i + 1) * rows, q * width : (q + 1) * width] for q in range(parts)
            ]
            block = [piece[:cut_rows] for piece in pieces]
            if cut == cuts - 1:
                edge = jnp.zeros((EDGE, width), jnp.float32)
                for q, piece in enumerate(pieces):
                    edge = jnp.where(edge_row == q, piece[cut_rows : cut_rows + 1] * has_edge, edge)
                block.append(edge)
            blocks.append(jnp.concatenate(block, 0))
        return blocks

    def forward(cut, first, last):
        def step(k, carry):
            tile_copy(cut, k).wait_recv()
            for j in range(1, epoch_count):
                epoch_copy(cut, k, j).start()
            return carry

        lax.fori_loop(first, last, step, 0)

    early = min(3, half)
    for cut in range(cuts):

        def row_group(i, carry):
            transform(pl.multiple_of(i * group, group), group)
            return carry

        lax.fori_loop(cut * cut_rows // group, (cut + 1) * cut_rows // group, row_group, 0)
        if cut == cuts - 1:
            transform(rows_here, EDGE)
        if cut == 0:
            pl.semaphore_wait(barrier, half + epoch_count - 1)
        else:
            forward(cut - 1, 1, early)
        for b in range(0, half, batch):
            tiles = [lax.rem(mine + b + i, half) * 2 + 1 - side for i in range(batch)]
            for i, block in enumerate(sections(cut, tiles)):
                given[b + i, rows_of(cut), :] = block.astype(jnp.bfloat16)
                partner_copy(cut, b + i).start()
        for b in range(0, half, batch):
            tiles = [lax.rem(mine + b + i, half) * 2 + side for i in range(batch)]
            for i, block in enumerate(sections(cut, tiles)):
                k = b + i
                partner_copy(cut, k).wait_recv()
                both = (block + landed[k, rows_of(cut), :].astype(jnp.float32)).astype(jnp.bfloat16)
                if k == 0:
                    full[epoch * half + mine, rows_of(cut), :] = both
                    for j in range(1, epoch_count):
                        epoch_copy(cut, 0, j).start()
                else:
                    folded[k, rows_of(cut), :] = both
                    tile_copy(cut, k).start()
    for cut in range(cuts):
        forward(cut, early if cut < cuts - 1 else 1, half)

    def mix_rows(e, cut, first, edges=None):
        for h in range(chunks):
            values = []
            for j in range(half):
                value = tuple(
                    full[
                        e * half + j, pl.ds((cut * parts + h * 2 + p) * cut_rows + first, group), :
                    ].astype(jnp.float32)
                    for p in range(2)
                )
                values.append(epoch_turn(value, j, epoch, epoch_count))
            done = dft(values + [None] * half, kept)
            if edges is not None:
                top = lax.broadcasted_iota(jnp.int32, (group, width), 0) == 0
                done = [
                    tuple(a + jnp.where(top, b, 0.0) for a, b in zip(part, edge))
                    for part, edge in zip(done, edges[h])
                ]
            for c, part in enumerate(done):
                for p in range(2):
                    row = pl.multiple_of(
                        p * band + e * rows_here + cut * cut_rows + first, group
                    )
                    mixed_ref[c, pl.ds(row, group), h * width : (h + 1) * width] = part[p].astype(
                        jnp.bfloat16
                    )

    def mix(e, cut):
        def step(i, carry):
            mix_rows(e, cut, pl.multiple_of(i * group, group))
            return carry

        lax.fori_loop(0, cut_rows // group, step, 0)

    for cut in range(cuts):
        mix(epoch, cut)
    for cut in range(cuts):
        for j in range(1, epoch_count):

            def arrive(k, carry, cut=cut, j=j):
                epoch_copy(cut, k, j).wait_recv()
                return carry

            lax.fori_loop(0, half, arrive, 0)
            mix(lax.rem(epoch + epoch_count - j, epoch_count), cut)

    edges = []
    for h in range(chunks):
        values = [None]
        for j in range(half):
            block = full[(epoch_count - 1) * half + j, cuts * parts * cut_rows :, :]
            block = block.astype(jnp.float32)
            value = tuple(block[h * 2 + p : h * 2 + p + 1] for p in range(2))
            values.append(epoch_turn(value, j + 1, epoch, epoch_count))
        edges.append(dft(values + [None] * (tile_count - half - 1), kept))
    mix_rows(0, 0, 0, edges)

    for cut in range(cuts):

        def finish(k, carry, cut=cut):
            tile_copy(cut, k).wait_send()
            return carry

        lax.fori_loop(1, half, finish, 0)

        def settle(k, carry, cut=cut):
            partner_copy(cut, k).wait_send()
            for j in range(1, epoch_count):
                epoch_copy(cut, k, j).wait_send()
            return carry

        lax.fori_loop(0, half, settle, 0)


def image_kernel(image_scale, epoch_ref, mixed_ref, last_ref, rows_ref, cols_ref, out_ref, tall):
    c = pl.program_id(0)

    @pl.when(c == 0)
    def _():
        tall[...] = jnp.transpose(rows_ref[...]) * image_scale

    lane = lax.broadcasted_iota(jnp.int32, tall.shape, 1)
    factor = jnp.sum(jnp.where(lane == c, tall[...], 0.0), 1, keepdims=True)
    pixels = jnp.dot(last_ref[0], mixed_ref[c], preferred_element_type=jnp.float32)
    out_ref[0] = pixels * factor * cols_ref[...]


def turns(product, modulus):
    angles = (product % modulus) * (2.0 * math.pi / modulus)
    return np.cos(angles), np.sin(angles)


def make_tables(tile_count, block_len):
    grid_size = tile_count * block_len
    long_idx = np.arange(block_len)
    tile_idx = np.arange(tile_count)
    turn_cos, turn_sin = turns(tile_idx[:, None] * long_idx[None, :], grid_size)
    c, s = turns(long_idx[:, None] * long_idx[None, :], block_len)
    second = np.stack([np.stack([c, s], 1), np.stack([-s, c], 1)], 0)
    width = min(LANES, block_len)
    second = second.reshape(2 * block_len, 2, block_len // width, width)
    second = second.transpose(0, 2, 1, 3).reshape(2 * block_len, 2 * block_len)
    pixel = long_idx[None, :] * tile_count + tile_idx[:, None]
    c, s = turns(pixel[:, :, None] * long_idx[None, None, :], grid_size)
    last = np.concatenate([c, -s], -1)
    return (
        turn_cos.astype(np.float32),
        turn_sin.astype(np.float32),
        second.astype(jnp.bfloat16),
        last.astype(jnp.bfloat16),
    )


def vmem(count):
    return [pl.BlockSpec(memory_space=pltpu.VMEM)] * count


def body(tables, owners, row_offsets, col_offsets, samples, coords, taper_rows, taper_cols):
    tile_count = lax.axis_size("tile")
    epoch_count = lax.axis_size("epoch")
    n_slots = owners.shape[1]
    n_samples = samples.shape[3]
    capacity = max(2, n_slots * 5 // (4 * tile_count))
    capacity += capacity % 2
    lane_step = max(8, 1 << (capacity - 1).bit_length())
    band = taper_cols.shape[0]
    width = min(LANES, band)
    half, kept = tile_count // 2, tile_count // epoch_count
    rows_here = band // epoch_count
    parts = 2 * (band // width)
    turn_cos, turn_sin, second, last = tables
    sizes = (tile_count, epoch_count, capacity, lane_step, band)
    block_rows = capacity * SUB // 2 + EDGE
    meta_rows = epoch_count * -(-tile_count // (LANES // lane_step))

    tile_sems = pltpu.SemaphoreType.DMA((tile_count,))
    epoch_sems = pltpu.SemaphoreType.DMA(((epoch_count - 1) * tile_count,))
    pool, meta = pl.pallas_call(
        functools.partial(grid_kernel, sizes),
        out_shape=[
            jax.ShapeDtypeStruct((epoch_count * tile_count, block_rows, LANES), jnp.bfloat16),
            jax.ShapeDtypeStruct((meta_rows, FIELDS, LANES), jnp.int32),
        ],
        in_specs=vmem(5),
        out_specs=vmem(2),
        scratch_shapes=[
            pltpu.VMEM((tile_count, block_rows, LANES), jnp.bfloat16),
            pltpu.VMEM((tile_count, 2 * lane_step, 2 * n_samples), jnp.float32),
            tile_sems,
            tile_sems,
            epoch_sems,
            epoch_sems,
        ],
        compiler_params=pltpu.CompilerParams(
            vmem_limit_bytes=VMEM_BYTES, collective_id=1, has_side_effects=True
        ),
        name="grid_slots",
    )(
        owners,
        row_offsets,
        col_offsets,
        coords,
        samples,
    )

    lane_blocks = tile_count * band // LANES
    acc = pl.pallas_call(
        functools.partial(place_kernel, sizes),
        out_shape=jax.ShapeDtypeStruct(
            (2, lane_blocks + 1, rows_here + 3 * SUB, LANES), jnp.float32
        ),
        in_specs=[pl.BlockSpec(memory_space=pltpu.SMEM)] + vmem(1),
        out_specs=vmem(1)[0],
        scratch_shapes=[
            pltpu.SMEM((epoch_count * tile_count * capacity + UNROLL,), jnp.int32),
            pltpu.VMEM((epoch_count, SUB, LANES), jnp.float32),
        ],
        compiler_params=pltpu.CompilerParams(vmem_limit_bytes=VMEM_BYTES),
        name="place_slots",
    )(meta, pool)

    cuts = 2 if rows_here % 32 == 0 else 1
    block_shape = (parts * rows_here + EDGE, width)
    sems = [pltpu.SemaphoreType.DMA((cuts * half,))] * 4
    sems += [pltpu.SemaphoreType.DMA((cuts * (epoch_count - 1) * half,))] * 2
    mixed = pl.pallas_call(
        functools.partial(swap_kernel, (tile_count, epoch_count, band), cuts),
        out_shape=jax.ShapeDtypeStruct((kept, 2 * band, band), jnp.bfloat16),
        in_specs=vmem(4),
        out_specs=vmem(1)[0],
        scratch_shapes=[
            pltpu.VMEM((tile_count, rows_here + EDGE, 2 * band), jnp.bfloat16),
            pltpu.VMEM((half, *block_shape), jnp.bfloat16),
            pltpu.VMEM((half, *block_shape), jnp.bfloat16),
            pltpu.VMEM((half, *block_shape), jnp.bfloat16),
            pltpu.VMEM((epoch_count * half, *block_shape), jnp.bfloat16),
            *sems,
        ],
        compiler_params=pltpu.CompilerParams(
            vmem_limit_bytes=VMEM_BYTES, collective_id=0, has_side_effects=True
        ),
        name="swap_rows",
    )(acc, jnp.asarray(turn_cos), jnp.asarray(turn_sin), jnp.asarray(second))

    image_scale = math.sqrt(n_slots) / (64.0 * tile_count * math.sqrt(epoch_count))
    return pl.pallas_call(
        functools.partial(image_kernel, image_scale),
        grid_spec=pltpu.PrefetchScalarGridSpec(
            num_scalar_prefetch=1,
            grid=(kept,),
            in_specs=[
                pl.BlockSpec(memory_space=pltpu.VMEM),
                pl.BlockSpec((1, band, 2 * band), lambda c, e: (e[0] * kept + c, 0, 0)),
                pl.BlockSpec((kept, band), lambda c, e: (0, 0)),
                pl.BlockSpec((1, band), lambda c, e: (0, 0)),
            ],
            out_specs=pl.BlockSpec((1, band, band), lambda c, e: (c, 0, 0)),
            scratch_shapes=[pltpu.VMEM((band, kept), jnp.float32)],
        ),
        out_shape=jax.ShapeDtypeStruct((kept, band, band), jnp.float32),
        compiler_params=pltpu.CompilerParams(vmem_limit_bytes=VMEM_BYTES),
        name="image_rows",
    )(
        lax.axis_index("epoch").astype(jnp.int32)[None],
        mixed,
        jnp.asarray(last),
        taper_rows,
        taper_cols[None, :],
    )


def solution(mesh):
    placed = (
        P("epoch", "tile"),
        P("epoch", "tile"),
        P("epoch", "tile"),
        P("epoch", "tile", None, None),
        P("epoch", "tile", None, None),
        P("epoch", None),
        P("tile"),
    )

    def whole(owners, row_offsets, col_offsets, samples, coords, taper_rows, taper_cols):
        tables = make_tables(mesh.shape["tile"], taper_cols.shape[0] // mesh.shape["tile"])
        return jax.shard_map(
            functools.partial(body, tables),
            mesh=mesh,
            in_specs=placed,
            out_specs=P("epoch", None, "tile"),
            check_vma=False,
        )(owners, row_offsets, col_offsets, samples, coords, taper_rows, taper_cols)

    return whole
```

```python
import functools
import math

import jax
import jax.numpy as jnp
import numpy as np
from jax import lax
from jax.experimental import pallas as pl
from jax.experimental.pallas import tpu as pltpu
from jax.sharding import PartitionSpec as P

SUB = 32
LANES = 128
EDGE = 16
FIELDS = 8
UNROLL = 8
BEHIND = 3
VMEM_BYTES = 56 * 1024 * 1024
MESH = pl.DeviceIdType.MESH


def dft(values, wanted, modulus=None):
    count = len(values)
    if all(v is None for v in values):
        return [None] * wanted
    if count == 1:
        return list(values)
    half = count // 2
    need = min(wanted, half)
    even, odd = dft(values[0::2], need), dft(values[1::2], need)
    low, high = [], []
    for k in range(need):
        e, o = even[k], odd[k]
        t = None if o is None else turn(o, k, count)
        low.append(plus(e, t))
        if half + k < wanted:
            high.append(minus(e, t))
    return low + high


def turn(value, k, count):
    re, im = value
    s = math.sqrt(0.5)
    k %= count
    if k == 0:
        return re, im
    if 2 * k == count:
        return -re, -im
    if 4 * k == count:
        return -im, re
    if 8 * k == count:
        return (re - im) * s, (re + im) * s
    if 8 * k == 3 * count:
        return (re + im) * -s, (re - im) * s
    c, s = math.cos(2 * math.pi * k / count), math.sin(2 * math.pi * k / count)
    return re * c - im * s, re * s + im * c


def plus(a, b):
    if a is None or b is None:
        return b if a is None else a
    return a[0] + b[0], a[1] + b[1]


def minus(a, b):
    if b is None:
        return a
    if a is None:
        return -b[0], -b[1]
    return a[0] - b[0], a[1] - b[1]


def epoch_turn(value, j, epoch, epoch_count):
    angles = [2 * math.pi * ((j * e) % epoch_count) / epoch_count for e in range(epoch_count)]

    def pick(numbers):
        chosen = jnp.float32(numbers[0])
        for e in range(1, epoch_count):
            chosen = jnp.where(epoch == e, jnp.float32(numbers[e]), chosen)
        return chosen

    cos, sin = [round(math.cos(a), 15) for a in angles], [round(math.sin(a), 15) for a in angles]
    re, im = value
    if not any(sin):
        if all(c == 1.0 for c in cos):
            return value
        c = pick(cos)
        return re * c, im * c
    c, s = pick(cos), pick(sin)
    return re * c - im * s, re * s + im * c


def exclusive(a, b, count):
    total = 0
    for bit in range(count.bit_length() - 1):
        x, y = lax.rem(a // (1 << bit), 2), lax.rem(b // (1 << bit), 2)
        total += (x + y - 2 * x * y) * (1 << bit)
    return total


def near_and_far(i, count):
    return jnp.where(
        i == count - 2,
        count - 1,
        jnp.where(lax.rem(i, 2) == 0, 1 + i // 2, count // 2 + i // 2),
    )


def grid_kernel(
    sizes,
    owner_ref,
    row_ref,
    col_ref,
    coords_ref,
    samples_ref,
    pool_ref,
    list_ref,
    weight_ref,
    *scratch,
):
    tile_count, epoch_count, capacity, lane_step, band = sizes
    packed, points, t_send, t_recv, x_send, x_recv = scratch
    me, epoch = lax.axis_index("tile"), lax.axis_index("epoch")
    n_slots = owner_ref.shape[1]
    n_samples = coords_ref.shape[3]
    half = tile_count // 2
    per_meta = LANES // lane_step
    groups = -(-tile_count // per_meta)
    slot_rows = SUB // 2

    barrier = pltpu.get_barrier_semaphore()

    def greet(k, carry):
        peer = lax.rem(me + k, tile_count)
        pl.semaphore_signal(barrier, inc=1, device_id={"tile": peer}, device_id_type=MESH)
        return carry

    lax.fori_loop(1, tile_count, greet, 0)
    for k in range(1, epoch_count):
        peer = lax.rem(epoch + k, epoch_count)
        pl.semaphore_signal(barrier, inc=1, device_id={"epoch": peer}, device_id_type=MESH)

    owner = owner_ref[...]
    mirrored = owner >= half
    target = jnp.where(mirrored, 2 * (tile_count - 1 - owner) + 1, 2 * owner)
    row = jnp.where(mirrored, band - (SUB - 1) - row_ref[...], row_ref[...])
    col = jnp.where(mirrored, tile_count * band - (SUB - 1) - col_ref[...], col_ref[...])
    mine = lax.broadcasted_iota(jnp.int32, (tile_count, n_slots), 0) == target
    before = lax.broadcasted_iota(jnp.int32, (n_slots, n_slots), 0) < lax.broadcasted_iota(
        jnp.int32, (n_slots, n_slots), 1
    )
    rank = jnp.dot(
        jnp.where(mine, 1.0, 0.0).astype(jnp.bfloat16),
        jnp.where(before, 1.0, 0.0).astype(jnp.bfloat16),
        preferred_element_type=jnp.float32,
    ).astype(jnp.int32)
    key = jnp.where(mine, rank, -LANES)
    fields = [jnp.ones_like(row), row, col // LANES, col % LANES]
    fields = jnp.concatenate(fields + [jnp.zeros_like(row)] * (EDGE - len(fields)), 0)
    fields = fields.astype(jnp.float32).astype(jnp.bfloat16)
    lane = lax.broadcasted_iota(jnp.int32, (LANES, n_slots), 0) - lax.rem(me, per_meta) * lane_step
    first = lax.broadcasted_iota(jnp.int32, (lane_step, n_slots), 0)
    hits = []
    for t in range(tile_count):
        hits.append(jnp.where(key[t : t + 1] == first, 1.0, 0.0))
        spot = jnp.where(key[t : t + 1] == lane, 1.0, 0.0).astype(jnp.bfloat16)
        packed[t, capacity * slot_rows :, :] = lax.dot_general(
            fields, spot, (((1,), (1,)), ((), ())), preferred_element_type=jnp.float32
        ).astype(jnp.bfloat16)
    hits = jnp.concatenate(hits, 0)
    here = jnp.dot(
        hits,
        jnp.concatenate([coords_ref[0, :, p, :] for p in range(2)], 1) * 0.25,
        precision=lax.Precision.HIGHEST,
        preferred_element_type=jnp.float32,
    )
    samples = samples_ref[0].astype(jnp.float32)
    samples = jnp.concatenate([samples[:, p, :] for p in range(2)], 1).astype(jnp.bfloat16)
    values = jnp.dot(hits.astype(jnp.bfloat16), samples, preferred_element_type=jnp.float32)
    for t in range(tile_count):
        rows = slice(t * lane_step, (t + 1) * lane_step)
        points[t, 0:lane_step] = here[rows]
        points[t, lane_step:] = values[rows]

    pl.semaphore_wait(barrier, tile_count + epoch_count - 2)

    cell_iota = lax.broadcasted_iota(jnp.int32, (SUB, n_samples), 0)

    def weights(cells, at):
        distance = cells - at
        return jnp.square(jnp.maximum(1.0 - distance * distance, 0.0))

    def make(tile):
        flip = lax.rem(tile, 2)
        cells = jnp.where(flip == 1, SUB - 1 - cell_iota, cell_iota).astype(jnp.float32) * 0.25
        sign = (1 - 2 * flip).astype(jnp.float32)
        for k in range(capacity):
            along_u = weights(cells, points[tile, k : k + 1, :n_samples]).astype(jnp.bfloat16)
            along_v = weights(cells, points[tile, k : k + 1, n_samples:])
            at = lane_step + k
            re = points[tile, at : at + 1, :n_samples] * along_v
            im = (points[tile, at : at + 1, n_samples:] * sign) * along_v
            subgrid = lax.dot_general(
                along_u,
                jnp.concatenate([re, im], 0).astype(jnp.bfloat16),
                (((1,), (1,)), ((), ())),
                preferred_element_type=jnp.float32,
            )
            packed[tile, k * slot_rows : (k + 1) * slot_rows, :] = jnp.concatenate(
                [subgrid[:slot_rows], subgrid[slot_rows:]], 1
            ).astype(jnp.bfloat16)

    def tile_copy(k):
        peer = exclusive(me, k, tile_count)
        return pltpu.make_async_remote_copy(
            src_ref=packed.at[peer],
            dst_ref=pool_ref.at[me],
            send_sem=t_send.at[k],
            recv_sem=t_recv.at[k],
            device_id={"tile": peer},
            device_id_type=MESH,
        )

    def epoch_copy(k, j):
        origin = exclusive(me, k, tile_count)
        return pltpu.make_async_remote_copy(
            src_ref=pool_ref.at[origin],
            dst_ref=pool_ref.at[j * tile_count + origin],
            send_sem=x_send.at[(j - 1) * tile_count + k],
            recv_sem=x_recv.at[(j - 1) * tile_count + k],
            device_id={"epoch": lax.rem(epoch + j, epoch_count)},
            device_id_type=MESH,
        )

    make(me)
    pool_ref[me] = packed[me]
    for j in range(1, epoch_count):
        epoch_copy(0, j).start()

    def send(i):
        k = near_and_far(i, tile_count)
        make(exclusive(me, k, tile_count))
        tile_copy(k).start()

    def forward(i):
        k = near_and_far(i, tile_count)
        tile_copy(k).wait_recv()
        for j in range(1, epoch_count):
            epoch_copy(k, j).start()

    behind = min(BEHIND, tile_count - 1)

    def first_sends(i, carry):
        send(i)
        return carry

    def both(i, carry):
        send(i)
        forward(i - behind)
        return carry

    def last_forwards(i, carry):
        forward(i)
        return carry

    lax.fori_loop(0, behind, first_sends, 0)
    lax.fori_loop(behind, tile_count - 1, both, 0)
    lax.fori_loop(tile_count - 1 - behind, tile_count - 1, last_forwards, 0)

    def sent_all(k, carry):
        tile_copy(k).wait_send()
        return carry

    lax.fori_loop(1, tile_count, sent_all, 0)

    rows_here = band // epoch_count
    first_row = (epoch * rows_here - SUB).astype(jnp.float32)
    spots = groups * LANES
    below = lax.broadcasted_iota(jnp.int32, (LANES, LANES), 0) < lax.broadcasted_iota(
        jnp.int32, (LANES, LANES), 1
    )
    below = jnp.where(below, 1.0, 0.0).astype(jnp.bfloat16)
    spot = lax.broadcasted_iota(jnp.int32, (spots, LANES), 0).astype(jnp.float32)
    lanes = lax.broadcasted_iota(jnp.int32, (1, LANES), 1)
    field = lax.broadcasted_iota(jnp.int32, (FIELDS, spots), 0)

    def list_slots(j):
        found, held = jnp.zeros((1, 1), jnp.float32), jnp.zeros((1, 1), jnp.float32)
        gathered = jnp.zeros((EDGE, spots), jnp.float32)
        for g in range(groups):
            total = jnp.zeros((EDGE, LANES), jnp.float32)
            for s in range(g * per_meta, min(tile_count, (g + 1) * per_meta)):
                total += pool_ref[j * tile_count + s, capacity * slot_rows :, :].astype(jnp.float32)
            valid, row = total[0:1], total[1:2] - first_row
            inside = (valid > 0) & (row > 0) & (row < rows_here + SUB)
            mask = jnp.where(inside, 1.0, 0.0)
            order = jnp.dot(
                mask.astype(jnp.bfloat16), below, preferred_element_type=jnp.float32
            )
            chosen = spot == jnp.where(inside, order + found, -1.0)
            source = (g * per_meta + lanes // lane_step).astype(jnp.float32)
            place = (lanes % lane_step).astype(jnp.float32)
            rows = [source, row, total[2:3], total[3:4], place]
            rows = jnp.concatenate(rows + [jnp.zeros_like(row)] * (EDGE - len(rows)), 0)
            gathered += lax.dot_general(
                rows.astype(jnp.bfloat16),
                jnp.where(chosen, 1.0, 0.0).astype(jnp.bfloat16),
                (((1,), (1,)), ((), ())),
                preferred_element_type=jnp.float32,
            )
            found += jnp.sum(mask, 1, keepdims=True)
            held += jnp.sum(valid, 1, keepdims=True)
        listed = jnp.where(field == FIELDS - 1, found, gathered[:FIELDS])
        list_ref[j] = listed.astype(jnp.int32)
        weight_ref[j] = jnp.broadcast_to(1.0 / jnp.maximum(held, 1.0), (FIELDS, LANES))

    list_slots(0)
    for j in range(1, epoch_count):

        def arrived(k, carry, j=j):
            epoch_copy(k, j).wait_recv()
            return carry

        lax.fori_loop(0, tile_count, arrived, 0)
        list_slots(j)

    def crossed(k, carry):
        for j in range(1, epoch_count):
            epoch_copy(k, j).wait_send()
        return carry

    lax.fori_loop(0, tile_count, crossed, 0)


def place_kernel(tile_count, list_ref, weight_ref, pool_ref, acc):
    acc_rows = acc.shape[2]
    slot_rows = SUB // 2

    def clear(i, carry):
        acc[0, i] = jnp.zeros((acc_rows, LANES), jnp.float32)
        acc[1, i] = jnp.zeros((acc_rows, LANES), jnp.float32)
        return carry

    lax.fori_loop(0, acc.shape[1], clear, 0)
    lanes = lax.broadcasted_iota(jnp.int32, (slot_rows, LANES), 1)

    for e in range(list_ref.shape[0]):
        weight = jnp.concatenate([weight_ref[e]] * (slot_rows // FIELDS), 0)

        def per_batch(b, carry, e=e, weight=weight):
            placed = []
            for k in range(UNROLL):
                at = b * UNROLL + k
                source, row, block, start, place = (list_ref[e, f, at] for f in range(5))
                first = pl.multiple_of(place * slot_rows, slot_rows)
                data = pool_ref[e * tile_count + source, pl.ds(first, slot_rows), :]
                data = data.astype(jnp.float32) * weight
                turned = [
                    pltpu.roll(data, lax.rem(start + (LANES - i * SUB), LANES), 1)
                    for i in range(4)
                ]
                near = (lanes >= start) & (lanes < start + SUB)
                far = lanes < start + SUB - LANES
                windows = [
                    jnp.concatenate([jnp.where(mask, turned[i], 0.0) for i in (p, 2 + p)], 0)
                    for p in range(2)
                    for mask in (near, far)
                ]
                placed.append((row, block, windows))
            for row, block, windows in placed:
                spots = [(p, block + h, pl.ds(row, SUB)) for p in range(2) for h in range(2)]
                sums = [acc[spot] + window for spot, window in zip(spots, windows)]
                for spot, total in zip(spots, sums):
                    acc[spot] = total
            return carry

        lax.fori_loop(0, (list_ref[e, FIELDS - 1, 0] + UNROLL - 1) // UNROLL, per_batch, 0)


def swap_kernel(sizes, cuts, acc_ref, cos_ref, sin_ref, second_ref, mixed_ref, *scratch):
    tile_count, epoch_count, band = sizes
    turned, given, landed, folded, full = scratch[:5]
    p_send, p_recv, t_send, t_recv, x_send, x_recv = scratch[5:]
    me, epoch = lax.axis_index("tile"), lax.axis_index("epoch")
    half, kept = tile_count // 2, tile_count // epoch_count
    mine, side = me // 2, lax.rem(me, 2)
    partner = me + 1 - 2 * side
    rows_here = band // epoch_count
    cut_rows = rows_here // cuts
    width = min(LANES, band)
    chunks = band // width
    parts = 2 * chunks
    lane_blocks = acc_ref.shape[1] - 1
    group = min(16, cut_rows)
    batch = min(4, half)

    barrier = pltpu.get_barrier_semaphore()

    def greet(k, carry):
        peer = exclusive(mine, k, half) * 2 + side
        pl.semaphore_signal(barrier, inc=1, device_id={"tile": peer}, device_id_type=MESH)
        return carry

    lax.fori_loop(1, half, greet, 0)
    pl.semaphore_signal(barrier, inc=1, device_id={"tile": partner}, device_id_type=MESH)
    for k in range(1, epoch_count):
        peer = lax.rem(epoch + k, epoch_count)
        pl.semaphore_signal(barrier, inc=1, device_id={"epoch": peer}, device_id_type=MESH)

    def rows_of(cut):
        edge = EDGE if cut == cuts - 1 else 0
        return pl.ds(cut * parts * cut_rows, parts * cut_rows + edge)

    def partner_copy(cut, k):
        return pltpu.make_async_remote_copy(
            src_ref=given.at[k, rows_of(cut)],
            dst_ref=landed.at[k, rows_of(cut)],
            send_sem=p_send.at[cut * half + k],
            recv_sem=p_recv.at[cut * half + k],
            device_id={"tile": partner},
            device_id_type=MESH,
        )

    def tile_copy(cut, k):
        return pltpu.make_async_remote_copy(
            src_ref=folded.at[k, rows_of(cut)],
            dst_ref=full.at[epoch * half + mine, rows_of(cut)],
            send_sem=t_send.at[cut * half + k],
            recv_sem=t_recv.at[cut * half + k],
            device_id={"tile": exclusive(mine, k, half) * 2 + side},
            device_id_type=MESH,
        )

    def epoch_copy(cut, k, j):
        origin = epoch * half + exclusive(mine, k, half)
        at = (cut * (epoch_count - 1) + j - 1) * half + k
        return pltpu.make_async_remote_copy(
            src_ref=full.at[origin, rows_of(cut)],
            dst_ref=full.at[origin, rows_of(cut)],
            send_sem=x_send.at[at],
            recv_sem=x_recv.at[at],
            device_id={"epoch": lax.rem(epoch + j, epoch_count)},
            device_id_type=MESH,
        )

    def transform(first, size):
        for h in range(chunks):
            values = []
            for a in range(tile_count):
                col = a * band + h * width
                lane, at = col % LANES, col // LANES
                value = [
                    acc_ref[p, at, pl.ds(SUB + first, size), lane : lane + width] for p in range(2)
                ]
                if col == 0:
                    for p in range(2):
                        value[p] += acc_ref[p, lane_blocks, pl.ds(SUB + first, size), :width]
                values.append(tuple(value))
            lanes = slice(h * width, (h + 1) * width)
            for m, (re, im) in enumerate(dft(values, tile_count)):
                c, s = cos_ref[m : m + 1, lanes], sin_ref[m : m + 1, lanes]
                pair = (re * c - im * s, re * s + im * c)
                for p in range(2):
                    start = p * band + h * width
                    turned[m, pl.ds(first, size), start : start + width] = pair[p].astype(
                        jnp.bfloat16
                    )

    edge_row = lax.broadcasted_iota(jnp.int32, (EDGE, width), 0)
    has_edge = jnp.where(epoch == epoch_count - 1, 1.0, 0.0)

    def sections(cut, tiles):
        rows = cut_rows + (EDGE if cut == cuts - 1 else 0)
        stack = [turned[tile, cut * cut_rows : cut * cut_rows + rows, :] for tile in tiles]
        moved = jnp.dot(
            jnp.concatenate(stack, 0), second_ref[...], preferred_element_type=jnp.float32
        )
        blocks = []
        for i in range(len(tiles)):
            pieces = [
                moved[i * rows : (i + 1) * rows, q * width : (q + 1) * width] for q in range(parts)
            ]
            block = [piece[:cut_rows] for piece in pieces]
            if cut == cuts - 1:
                edge = jnp.zeros((EDGE, width), jnp.float32)
                for q, piece in enumerate(pieces):
                    edge = jnp.where(edge_row == q, piece[cut_rows : cut_rows + 1] * has_edge, edge)
                block.append(edge)
            blocks.append(jnp.concatenate(block, 0))
        return blocks

    def forward(cut, k):
        tile_copy(cut, k).wait_recv()
        for j in range(1, epoch_count):
            epoch_copy(cut, k, j).start()

    order = [0] + [k for pair in zip(range(1, half), range(half // 2, half)) for k in pair]
    order = order[: 1 + 2 * (half // 2 - 1)] + [half - 1] if half > 1 else [0]
    pending = []
    for cut in range(cuts):

        def row_group(i, carry):
            transform(pl.multiple_of(i * group, group), group)
            return carry

        if not pending:
            steps = cut_rows // group
            lax.fori_loop(cut * steps, (cut + 1) * steps, row_group, 0)
        else:
            for i in range(cut_rows // group):
                transform(cut * cut_rows + i * group, group)
                if pending:
                    forward(*pending.pop(0))
        if cut == cuts - 1:
            transform(rows_here, EDGE)
        if cut == 0:
            pl.semaphore_wait(barrier, half + epoch_count - 1)
        for b in range(0, half, batch):
            ks = order[b : b + batch]
            tiles = [exclusive(mine, k, half) * 2 + 1 - side for k in ks]
            for k, block in zip(ks, sections(cut, tiles)):
                given[k, rows_of(cut), :] = block.astype(jnp.bfloat16)
                partner_copy(cut, k).start()
        for b in range(0, half, batch):
            ks = order[b : b + batch]
            tiles = [exclusive(mine, k, half) * 2 + side for k in ks]
            for k, block in zip(ks, sections(cut, tiles)):
                partner_copy(cut, k).wait_recv()
                both = (block + landed[k, rows_of(cut), :].astype(jnp.float32)).astype(jnp.bfloat16)
                if k == 0:
                    full[epoch * half + mine, rows_of(cut), :] = both
                    for j in range(1, epoch_count):
                        epoch_copy(cut, 0, j).start()
                else:
                    folded[k, rows_of(cut), :] = both
                    tile_copy(cut, k).start()
                if cut > 0 and pending:
                    forward(*pending.pop(0))
        pending += [(cut, k) for k in order[1:]]
    for cut, k in pending:
        forward(cut, k)

    def mix_rows(e, cut, first, edges=None):
        for h in range(chunks):
            values = []
            for j in range(half):
                value = tuple(
                    full[
                        e * half + j, pl.ds((cut * parts + h * 2 + p) * cut_rows + first, group), :
                    ].astype(jnp.float32)
                    for p in range(2)
                )
                values.append(epoch_turn(value, j, epoch, epoch_count))
            done = dft(values + [None] * half, kept)
            if edges is not None:
                top = lax.broadcasted_iota(jnp.int32, (group, width), 0) == 0
                done = [
                    tuple(a + jnp.where(top, b, 0.0) for a, b in zip(part, edge))
                    for part, edge in zip(done, edges[h])
                ]
            for c, part in enumerate(done):
                for p in range(2):
                    row = pl.multiple_of(
                        p * band + e * rows_here + cut * cut_rows + first, group
                    )
                    mixed_ref[c, pl.ds(row, group), h * width : (h + 1) * width] = part[p].astype(
                        jnp.bfloat16
                    )

    def mix(e, cut):
        def step(i, carry):
            mix_rows(e, cut, pl.multiple_of(i * group, group))
            return carry

        lax.fori_loop(0, cut_rows // group, step, 0)

    for cut in range(cuts):
        mix(epoch, cut)
    for cut in range(cuts):
        for j in range(1, epoch_count):

            def arrive(k, carry, cut=cut, j=j):
                epoch_copy(cut, k, j).wait_recv()
                return carry

            lax.fori_loop(0, half, arrive, 0)
            mix(lax.rem(epoch + epoch_count - j, epoch_count), cut)

    edges = []
    for h in range(chunks):
        values = [None]
        for j in range(half):
            block = full[(epoch_count - 1) * half + j, cuts * parts * cut_rows :, :]
            block = block.astype(jnp.float32)
            value = tuple(block[h * 2 + p : h * 2 + p + 1] for p in range(2))
            values.append(epoch_turn(value, j + 1, epoch, epoch_count))
        edges.append(dft(values + [None] * (tile_count - half - 1), kept))
    mix_rows(0, 0, 0, edges)

    for cut in range(cuts):

        def finish(k, carry, cut=cut):
            tile_copy(cut, k).wait_send()
            return carry

        lax.fori_loop(1, half, finish, 0)

        def settle(k, carry, cut=cut):
            partner_copy(cut, k).wait_send()
            for j in range(1, epoch_count):
                epoch_copy(cut, k, j).wait_send()
            return carry

        lax.fori_loop(0, half, settle, 0)


def image_kernel(image_scale, epoch_ref, mixed_ref, last_ref, rows_ref, cols_ref, out_ref, tall):
    c = pl.program_id(0)

    @pl.when(c == 0)
    def _():
        tall[...] = jnp.transpose(rows_ref[...]) * image_scale

    lane = lax.broadcasted_iota(jnp.int32, tall.shape, 1)
    factor = jnp.sum(jnp.where(lane == c, tall[...], 0.0), 1, keepdims=True)
    pixels = jnp.dot(last_ref[0], mixed_ref[c], preferred_element_type=jnp.float32)
    out_ref[0] = pixels * factor * cols_ref[...]


def turns(product, modulus):
    angles = (product % modulus) * (2.0 * math.pi / modulus)
    return np.cos(angles), np.sin(angles)


def make_tables(tile_count, block_len):
    grid_size = tile_count * block_len
    long_idx = np.arange(block_len)
    tile_idx = np.arange(tile_count)
    turn_cos, turn_sin = turns(tile_idx[:, None] * long_idx[None, :], grid_size)
    c, s = turns(long_idx[:, None] * long_idx[None, :], block_len)
    second = np.stack([np.stack([c, s], 1), np.stack([-s, c], 1)], 0)
    width = min(LANES, block_len)
    second = second.reshape(2 * block_len, 2, block_len // width, width)
    second = second.transpose(0, 2, 1, 3).reshape(2 * block_len, 2 * block_len)
    pixel = long_idx[None, :] * tile_count + tile_idx[:, None]
    c, s = turns(pixel[:, :, None] * long_idx[None, None, :], grid_size)
    last = np.concatenate([c, -s], -1)
    return (
        turn_cos.astype(np.float32),
        turn_sin.astype(np.float32),
        second.astype(jnp.bfloat16),
        last.astype(jnp.bfloat16),
    )


def vmem(count):
    return [pl.BlockSpec(memory_space=pltpu.VMEM)] * count


def body(tables, owners, row_offsets, col_offsets, samples, coords, taper_rows, taper_cols):
    tile_count = lax.axis_size("tile")
    epoch_count = lax.axis_size("epoch")
    n_slots = owners.shape[1]
    n_samples = samples.shape[3]
    capacity = max(2, n_slots * 5 // (4 * tile_count))
    capacity += capacity % 2
    lane_step = max(8, 1 << (capacity - 1).bit_length())
    band = taper_cols.shape[0]
    width = min(LANES, band)
    half, kept = tile_count // 2, tile_count // epoch_count
    rows_here = band // epoch_count
    parts = 2 * (band // width)
    turn_cos, turn_sin, second, last = tables
    sizes = (tile_count, epoch_count, capacity, lane_step, band)
    block_rows = capacity * SUB // 2 + EDGE
    spots = -(-tile_count // (LANES // lane_step)) * LANES

    tile_sems = pltpu.SemaphoreType.DMA((tile_count,))
    epoch_sems = pltpu.SemaphoreType.DMA(((epoch_count - 1) * tile_count,))
    pool, slot_list, weights = pl.pallas_call(
        functools.partial(grid_kernel, sizes),
        out_shape=[
            jax.ShapeDtypeStruct((epoch_count * tile_count, block_rows, LANES), jnp.bfloat16),
            jax.ShapeDtypeStruct((epoch_count, FIELDS, spots), jnp.int32),
            jax.ShapeDtypeStruct((epoch_count, FIELDS, LANES), jnp.float32),
        ],
        in_specs=vmem(5),
        out_specs=vmem(3),
        scratch_shapes=[
            pltpu.VMEM((tile_count, block_rows, LANES), jnp.bfloat16),
            pltpu.VMEM((tile_count, 2 * lane_step, 2 * n_samples), jnp.float32),
            tile_sems,
            tile_sems,
            epoch_sems,
            epoch_sems,
        ],
        compiler_params=pltpu.CompilerParams(
            vmem_limit_bytes=VMEM_BYTES, collective_id=1, has_side_effects=True
        ),
        name="grid_slots",
    )(
        owners,
        row_offsets,
        col_offsets,
        coords,
        samples,
    )

    lane_blocks = tile_count * band // LANES
    acc = pl.pallas_call(
        functools.partial(place_kernel, tile_count),
        out_shape=jax.ShapeDtypeStruct(
            (2, lane_blocks + 1, rows_here + 2 * SUB, LANES), jnp.float32
        ),
        in_specs=[pl.BlockSpec(memory_space=pltpu.SMEM)] + vmem(2),
        out_specs=vmem(1)[0],
        compiler_params=pltpu.CompilerParams(vmem_limit_bytes=VMEM_BYTES),
        name="place_slots",
    )(slot_list, weights, pool)

    cuts = 2 if rows_here % 32 == 0 else 1
    block_shape = (parts * rows_here + EDGE, width)
    sems = [pltpu.SemaphoreType.DMA((cuts * half,))] * 4
    sems += [pltpu.SemaphoreType.DMA((cuts * (epoch_count - 1) * half,))] * 2
    mixed = pl.pallas_call(
        functools.partial(swap_kernel, (tile_count, epoch_count, band), cuts),
        out_shape=jax.ShapeDtypeStruct((kept, 2 * band, band), jnp.bfloat16),
        in_specs=vmem(4),
        out_specs=vmem(1)[0],
        scratch_shapes=[
            pltpu.VMEM((tile_count, rows_here + EDGE, 2 * band), jnp.bfloat16),
            pltpu.VMEM((half, *block_shape), jnp.bfloat16),
            pltpu.VMEM((half, *block_shape), jnp.bfloat16),
            pltpu.VMEM((half, *block_shape), jnp.bfloat16),
            pltpu.VMEM((epoch_count * half, *block_shape), jnp.bfloat16),
            *sems,
        ],
        compiler_params=pltpu.CompilerParams(
            vmem_limit_bytes=VMEM_BYTES, collective_id=0, has_side_effects=True
        ),
        name="swap_rows",
    )(acc, jnp.asarray(turn_cos), jnp.asarray(turn_sin), jnp.asarray(second))

    image_scale = math.sqrt(n_slots) / (64.0 * tile_count * math.sqrt(epoch_count))
    return pl.pallas_call(
        functools.partial(image_kernel, image_scale),
        grid_spec=pltpu.PrefetchScalarGridSpec(
            num_scalar_prefetch=1,
            grid=(kept,),
            in_specs=[
                pl.BlockSpec(memory_space=pltpu.VMEM),
                pl.BlockSpec((1, band, 2 * band), lambda c, e: (e[0] * kept + c, 0, 0)),
                pl.BlockSpec((kept, band), lambda c, e: (0, 0)),
                pl.BlockSpec((1, band), lambda c, e: (0, 0)),
            ],
            out_specs=pl.BlockSpec((1, band, band), lambda c, e: (c, 0, 0)),
            scratch_shapes=[pltpu.VMEM((band, kept), jnp.float32)],
        ),
        out_shape=jax.ShapeDtypeStruct((kept, band, band), jnp.float32),
        compiler_params=pltpu.CompilerParams(vmem_limit_bytes=VMEM_BYTES),
        name="image_rows",
    )(
        lax.axis_index("epoch").astype(jnp.int32)[None],
        mixed,
        jnp.asarray(last),
        taper_rows,
        taper_cols[None, :],
    )


def solution(mesh):
    placed = (
        P("epoch", "tile"),
        P("epoch", "tile"),
        P("epoch", "tile"),
        P("epoch", "tile", None, None),
        P("epoch", "tile", None, None),
        P("epoch", None),
        P("tile"),
    )

    def whole(owners, row_offsets, col_offsets, samples, coords, taper_rows, taper_cols):
        tables = make_tables(mesh.shape["tile"], taper_cols.shape[0] // mesh.shape["tile"])
        return jax.shard_map(
            functools.partial(body, tables),
            mesh=mesh,
            in_specs=placed,
            out_specs=P("epoch", None, "tile"),
            check_vma=False,
        )(owners, row_offsets, col_offsets, samples, coords, taper_rows, taper_cols)

    return whole
```

```python
import functools
import math

import jax
import jax.numpy as jnp
import numpy as np
from jax import lax
from jax.experimental import pallas as pl
from jax.experimental.pallas import tpu as pltpu
from jax.sharding import PartitionSpec as P

SUB = 32
LANES = 128
EDGE = 16
FIELDS = 8
UNROLL = 8
BEHIND = 3
VMEM_BYTES = 24 * 1024 * 1024
MESH = pl.DeviceIdType.MESH


def dft(values, wanted, modulus=None):
    count = len(values)
    if all(v is None for v in values):
        return [None] * wanted
    if count == 1:
        return list(values)
    half = count // 2
    need = min(wanted, half)
    even, odd = dft(values[0::2], need), dft(values[1::2], need)
    low, high = [], []
    for k in range(need):
        e, o = even[k], odd[k]
        t = None if o is None else turn(o, k, count)
        low.append(plus(e, t))
        if half + k < wanted:
            high.append(minus(e, t))
    return low + high


def turn(value, k, count):
    re, im = value
    s = math.sqrt(0.5)
    k %= count
    if k == 0:
        return re, im
    if 2 * k == count:
        return -re, -im
    if 4 * k == count:
        return -im, re
    if 8 * k == count:
        return (re - im) * s, (re + im) * s
    if 8 * k == 3 * count:
        return (re + im) * -s, (re - im) * s
    c, s = math.cos(2 * math.pi * k / count), math.sin(2 * math.pi * k / count)
    return re * c - im * s, re * s + im * c


def plus(a, b):
    if a is None or b is None:
        return b if a is None else a
    return a[0] + b[0], a[1] + b[1]


def minus(a, b):
    if b is None:
        return a
    if a is None:
        return -b[0], -b[1]
    return a[0] - b[0], a[1] - b[1]


def epoch_turn(value, j, epoch, epoch_count):
    angles = [2 * math.pi * ((j * e) % epoch_count) / epoch_count for e in range(epoch_count)]

    def pick(numbers):
        chosen = jnp.float32(numbers[0])
        for e in range(1, epoch_count):
            chosen = jnp.where(epoch == e, jnp.float32(numbers[e]), chosen)
        return chosen

    cos, sin = [round(math.cos(a), 15) for a in angles], [round(math.sin(a), 15) for a in angles]
    re, im = value
    if not any(sin):
        if all(c == 1.0 for c in cos):
            return value
        c = pick(cos)
        return re * c, im * c
    c, s = pick(cos), pick(sin)
    return re * c - im * s, re * s + im * c


def exclusive(a, b, count):
    total = 0
    for bit in range(count.bit_length() - 1):
        x, y = lax.rem(a // (1 << bit), 2), lax.rem(b // (1 << bit), 2)
        total += (x + y - 2 * x * y) * (1 << bit)
    return total


def near_and_far(i, count):
    return jnp.where(
        i == count - 2,
        count - 1,
        jnp.where(lax.rem(i, 2) == 0, 1 + i // 2, count // 2 + i // 2),
    )


def grid_kernel(
    sizes,
    *refs,
):
    tile_count, epoch_count, capacity, lane_step, band = sizes
    inputs, (pool_ref, list_ref, weight_ref), scratch = refs[:5], refs[5:8], refs[8:]
    owner_ref, row_ref, col_ref, coords_ref, samples_ref, in_sem = scratch[:6]
    packed, points, t_send, t_recv, x_send, x_recv = scratch[6:]
    fetches = [
        pltpu.make_async_copy(given, held, in_sem.at[i])
        for i, (given, held) in enumerate(zip(inputs, scratch))
    ]
    for fetch in fetches:
        fetch.start()
    me, epoch = lax.axis_index("tile"), lax.axis_index("epoch")
    n_slots = owner_ref.shape[1]
    n_samples = coords_ref.shape[3]
    half = tile_count // 2
    per_meta = LANES // lane_step
    groups = -(-tile_count // per_meta)
    slot_rows = SUB // 2

    barrier = pltpu.get_barrier_semaphore()

    def greet(k, carry):
        peer = lax.rem(me + k, tile_count)
        pl.semaphore_signal(barrier, inc=1, device_id={"tile": peer}, device_id_type=MESH)
        return carry

    lax.fori_loop(1, tile_count, greet, 0)
    for k in range(1, epoch_count):
        peer = lax.rem(epoch + k, epoch_count)
        pl.semaphore_signal(barrier, inc=1, device_id={"epoch": peer}, device_id_type=MESH)

    for fetch in fetches:
        fetch.wait()
    owner = owner_ref[...]
    mirrored = owner >= half
    target = jnp.where(mirrored, 2 * (tile_count - 1 - owner) + 1, 2 * owner)
    row = jnp.where(mirrored, band - (SUB - 1) - row_ref[...], row_ref[...])
    col = jnp.where(mirrored, tile_count * band - (SUB - 1) - col_ref[...], col_ref[...])
    mine = lax.broadcasted_iota(jnp.int32, (tile_count, n_slots), 0) == target
    before = lax.broadcasted_iota(jnp.int32, (n_slots, n_slots), 0) < lax.broadcasted_iota(
        jnp.int32, (n_slots, n_slots), 1
    )
    rank = jnp.dot(
        jnp.where(mine, 1.0, 0.0).astype(jnp.bfloat16),
        jnp.where(before, 1.0, 0.0).astype(jnp.bfloat16),
        preferred_element_type=jnp.float32,
    ).astype(jnp.int32)
    key = jnp.where(mine, rank, -LANES)
    fields = [jnp.ones_like(row), row, col // LANES, col % LANES]
    fields = jnp.concatenate(fields + [jnp.zeros_like(row)] * (EDGE - len(fields)), 0)
    fields = fields.astype(jnp.float32).astype(jnp.bfloat16)
    lane = lax.broadcasted_iota(jnp.int32, (LANES, n_slots), 0) - lax.rem(me, per_meta) * lane_step
    first = lax.broadcasted_iota(jnp.int32, (lane_step, n_slots), 0)
    hits = []
    for t in range(tile_count):
        hits.append(jnp.where(key[t : t + 1] == first, 1.0, 0.0))
        spot = jnp.where(key[t : t + 1] == lane, 1.0, 0.0).astype(jnp.bfloat16)
        packed[t, capacity * slot_rows :, :] = lax.dot_general(
            fields, spot, (((1,), (1,)), ((), ())), preferred_element_type=jnp.float32
        ).astype(jnp.bfloat16)
    hits = jnp.concatenate(hits, 0)
    here = jnp.dot(
        hits,
        jnp.concatenate([coords_ref[0, :, p, :] for p in range(2)], 1) * 0.25,
        precision=lax.Precision.HIGHEST,
        preferred_element_type=jnp.float32,
    )
    samples = samples_ref[0].astype(jnp.float32)
    samples = jnp.concatenate([samples[:, p, :] for p in range(2)], 1).astype(jnp.bfloat16)
    values = jnp.dot(hits.astype(jnp.bfloat16), samples, preferred_element_type=jnp.float32)
    for t in range(tile_count):
        rows = slice(t * lane_step, (t + 1) * lane_step)
        points[t, 0:lane_step] = here[rows]
        points[t, lane_step:] = values[rows]

    pl.semaphore_wait(barrier, tile_count + epoch_count - 2)

    cell_iota = lax.broadcasted_iota(jnp.int32, (SUB, n_samples), 0)

    def weights(cells, at):
        distance = cells - at
        return jnp.square(jnp.maximum(1.0 - distance * distance, 0.0))

    def make(tile):
        flip = lax.rem(tile, 2)
        cells = jnp.where(flip == 1, SUB - 1 - cell_iota, cell_iota).astype(jnp.float32) * 0.25
        sign = (1 - 2 * flip).astype(jnp.float32)
        for k in range(capacity):
            along_u = weights(cells, points[tile, k : k + 1, :n_samples]).astype(jnp.bfloat16)
            along_v = weights(cells, points[tile, k : k + 1, n_samples:])
            at = lane_step + k
            re = points[tile, at : at + 1, :n_samples] * along_v
            im = (points[tile, at : at + 1, n_samples:] * sign) * along_v
            subgrid = lax.dot_general(
                along_u,
                jnp.concatenate([re, im], 0).astype(jnp.bfloat16),
                (((1,), (1,)), ((), ())),
                preferred_element_type=jnp.float32,
            )
            packed[tile, k * slot_rows : (k + 1) * slot_rows, :] = jnp.concatenate(
                [subgrid[:slot_rows], subgrid[slot_rows:]], 1
            ).astype(jnp.bfloat16)

    def tile_copy(k):
        peer = exclusive(me, k, tile_count)
        return pltpu.make_async_remote_copy(
            src_ref=packed.at[peer],
            dst_ref=pool_ref.at[me],
            send_sem=t_send.at[k],
            recv_sem=t_recv.at[k],
            device_id={"tile": peer},
            device_id_type=MESH,
        )

    def epoch_copy(k, j):
        origin = exclusive(me, k, tile_count)
        return pltpu.make_async_remote_copy(
            src_ref=pool_ref.at[origin],
            dst_ref=pool_ref.at[j * tile_count + origin],
            send_sem=x_send.at[(j - 1) * tile_count + k],
            recv_sem=x_recv.at[(j - 1) * tile_count + k],
            device_id={"epoch": lax.rem(epoch + j, epoch_count)},
            device_id_type=MESH,
        )

    make(me)
    pool_ref[me] = packed[me]
    for j in range(1, epoch_count):
        epoch_copy(0, j).start()

    def send(i):
        k = near_and_far(i, tile_count)
        make(exclusive(me, k, tile_count))
        tile_copy(k).start()

    def forward(i):
        k = near_and_far(i, tile_count)
        tile_copy(k).wait_recv()
        for j in range(1, epoch_count):
            epoch_copy(k, j).start()

    behind = min(BEHIND, tile_count - 1)

    def first_sends(i, carry):
        send(i)
        return carry

    def both(i, carry):
        send(i)
        forward(i - behind)
        return carry

    def last_forwards(i, carry):
        forward(i)
        return carry

    lax.fori_loop(0, behind, first_sends, 0)
    lax.fori_loop(behind, tile_count - 1, both, 0)
    lax.fori_loop(tile_count - 1 - behind, tile_count - 1, last_forwards, 0)

    def sent_all(k, carry):
        tile_copy(k).wait_send()
        return carry

    lax.fori_loop(1, tile_count, sent_all, 0)

    rows_here = band // epoch_count
    first_row = (epoch * rows_here - SUB).astype(jnp.float32)
    spots = groups * LANES
    below = lax.broadcasted_iota(jnp.int32, (LANES, LANES), 0) < lax.broadcasted_iota(
        jnp.int32, (LANES, LANES), 1
    )
    below = jnp.where(below, 1.0, 0.0).astype(jnp.bfloat16)
    spot = lax.broadcasted_iota(jnp.int32, (spots, LANES), 0).astype(jnp.float32)
    lanes = lax.broadcasted_iota(jnp.int32, (1, LANES), 1)
    field = lax.broadcasted_iota(jnp.int32, (FIELDS, spots), 0)

    def list_slots(j):
        found, held = jnp.zeros((1, 1), jnp.float32), jnp.zeros((1, 1), jnp.float32)
        gathered = jnp.zeros((EDGE, spots), jnp.float32)
        for g in range(groups):
            total = jnp.zeros((EDGE, LANES), jnp.float32)
            for s in range(g * per_meta, min(tile_count, (g + 1) * per_meta)):
                total += pool_ref[j * tile_count + s, capacity * slot_rows :, :].astype(jnp.float32)
            valid, row = total[0:1], total[1:2] - first_row
            inside = (valid > 0) & (row > 0) & (row < rows_here + SUB)
            mask = jnp.where(inside, 1.0, 0.0)
            order = jnp.dot(
                mask.astype(jnp.bfloat16), below, preferred_element_type=jnp.float32
            )
            chosen = spot == jnp.where(inside, order + found, -1.0)
            source = (g * per_meta + lanes // lane_step).astype(jnp.float32)
            place = (lanes % lane_step).astype(jnp.float32)
            rows = [source, row, total[2:3], total[3:4], place]
            rows = jnp.concatenate(rows + [jnp.zeros_like(row)] * (EDGE - len(rows)), 0)
            gathered += lax.dot_general(
                rows.astype(jnp.bfloat16),
                jnp.where(chosen, 1.0, 0.0).astype(jnp.bfloat16),
                (((1,), (1,)), ((), ())),
                preferred_element_type=jnp.float32,
            )
            found += jnp.sum(mask, 1, keepdims=True)
            held += jnp.sum(valid, 1, keepdims=True)
        listed = jnp.where(field == FIELDS - 1, found, gathered[:FIELDS])
        list_ref[j] = listed.astype(jnp.int32)
        weight_ref[j] = jnp.broadcast_to(1.0 / jnp.maximum(held, 1.0), (FIELDS, LANES))

    list_slots(0)
    for j in range(1, epoch_count):

        def arrived(k, carry, j=j):
            epoch_copy(k, j).wait_recv()
            return carry

        lax.fori_loop(0, tile_count, arrived, 0)
        list_slots(j)

    def crossed(k, carry):
        for j in range(1, epoch_count):
            epoch_copy(k, j).wait_send()
        return carry

    lax.fori_loop(0, tile_count, crossed, 0)


def place_kernel(tile_count, list_ref, weight_ref, pool_ref, acc):
    acc_rows = acc.shape[2]
    slot_rows = SUB // 2

    def clear(i, carry):
        acc[0, i] = jnp.zeros((acc_rows, LANES), jnp.float32)
        acc[1, i] = jnp.zeros((acc_rows, LANES), jnp.float32)
        return carry

    lax.fori_loop(0, acc.shape[1], clear, 0)
    lanes = lax.broadcasted_iota(jnp.int32, (slot_rows, LANES), 1)

    for e in range(list_ref.shape[0]):
        weight = jnp.concatenate([weight_ref[e]] * (slot_rows // FIELDS), 0)

        def per_batch(b, carry, e=e, weight=weight):
            placed = []
            for k in range(UNROLL):
                at = b * UNROLL + k
                source, row, block, start, place = (list_ref[e, f, at] for f in range(5))
                first = pl.multiple_of(place * slot_rows, slot_rows)
                data = pool_ref[e * tile_count + source, pl.ds(first, slot_rows), :]
                data = data.astype(jnp.float32) * weight
                turned = [
                    pltpu.roll(data, lax.rem(start + (LANES - i * SUB), LANES), 1)
                    for i in range(4)
                ]
                near = (lanes >= start) & (lanes < start + SUB)
                far = lanes < start + SUB - LANES
                windows = [
                    jnp.concatenate([jnp.where(mask, turned[i], 0.0) for i in (p, 2 + p)], 0)
                    for p in range(2)
                    for mask in (near, far)
                ]
                placed.append((row, block, windows))
            for row, block, windows in placed:
                spots = [(p, block + h, pl.ds(row, SUB)) for p in range(2) for h in range(2)]
                sums = [acc[spot] + window for spot, window in zip(spots, windows)]
                for spot, total in zip(spots, sums):
                    acc[spot] = total
            return carry

        lax.fori_loop(0, (list_ref[e, FIELDS - 1, 0] + UNROLL - 1) // UNROLL, per_batch, 0)


def swap_kernel(
    sizes, cuts, acc_ref, cos_ref, sin_ref, second_ref, last_ref, mixed_ref, here_ref, *scratch
):
    tile_count, epoch_count, band = sizes
    table_sem, scratch = scratch[0], scratch[1:]
    turned, given, landed, folded, full = scratch[:5]
    p_send, p_recv, t_send, t_recv, x_send, x_recv = scratch[5:]
    me, epoch = lax.axis_index("tile"), lax.axis_index("epoch")
    half, kept = tile_count // 2, tile_count // epoch_count
    mine, side = me // 2, lax.rem(me, 2)
    partner = me + 1 - 2 * side
    table_copy = pltpu.make_async_copy(
        last_ref.at[pl.ds(epoch * kept, kept)], here_ref, table_sem.at[0]
    )
    table_copy.start()
    rows_here = band // epoch_count
    cut_rows = rows_here // cuts
    width = min(LANES, band)
    chunks = band // width
    parts = 2 * chunks
    lane_blocks = acc_ref.shape[1] - 1
    group = min(16, cut_rows)
    batch = min(4, half)

    barrier = pltpu.get_barrier_semaphore()

    def greet(k, carry):
        peer = exclusive(mine, k, half) * 2 + side
        pl.semaphore_signal(barrier, inc=1, device_id={"tile": peer}, device_id_type=MESH)
        return carry

    lax.fori_loop(1, half, greet, 0)
    pl.semaphore_signal(barrier, inc=1, device_id={"tile": partner}, device_id_type=MESH)
    for k in range(1, epoch_count):
        peer = lax.rem(epoch + k, epoch_count)
        pl.semaphore_signal(barrier, inc=1, device_id={"epoch": peer}, device_id_type=MESH)

    def rows_of(cut):
        edge = EDGE if cut == cuts - 1 else 0
        return pl.ds(cut * parts * cut_rows, parts * cut_rows + edge)

    def partner_copy(cut, k):
        return pltpu.make_async_remote_copy(
            src_ref=given.at[k, rows_of(cut)],
            dst_ref=landed.at[k, rows_of(cut)],
            send_sem=p_send.at[cut * half + k],
            recv_sem=p_recv.at[cut * half + k],
            device_id={"tile": partner},
            device_id_type=MESH,
        )

    def tile_copy(cut, k):
        return pltpu.make_async_remote_copy(
            src_ref=folded.at[k, rows_of(cut)],
            dst_ref=full.at[epoch * half + mine, rows_of(cut)],
            send_sem=t_send.at[cut * half + k],
            recv_sem=t_recv.at[cut * half + k],
            device_id={"tile": exclusive(mine, k, half) * 2 + side},
            device_id_type=MESH,
        )

    def epoch_copy(cut, k, j):
        origin = epoch * half + exclusive(mine, k, half)
        at = (cut * (epoch_count - 1) + j - 1) * half + k
        return pltpu.make_async_remote_copy(
            src_ref=full.at[origin, rows_of(cut)],
            dst_ref=full.at[origin, rows_of(cut)],
            send_sem=x_send.at[at],
            recv_sem=x_recv.at[at],
            device_id={"epoch": lax.rem(epoch + j, epoch_count)},
            device_id_type=MESH,
        )

    def transform(first, size):
        for h in range(chunks):
            values = []
            for a in range(tile_count):
                col = a * band + h * width
                lane, at = col % LANES, col // LANES
                value = [
                    acc_ref[p, at, pl.ds(SUB + first, size), lane : lane + width] for p in range(2)
                ]
                if col == 0:
                    for p in range(2):
                        value[p] += acc_ref[p, lane_blocks, pl.ds(SUB + first, size), :width]
                values.append(tuple(value))
            lanes = slice(h * width, (h + 1) * width)
            for m, (re, im) in enumerate(dft(values, tile_count)):
                c, s = cos_ref[m : m + 1, lanes], sin_ref[m : m + 1, lanes]
                pair = (re * c - im * s, re * s + im * c)
                for p in range(2):
                    start = p * band + h * width
                    turned[m, pl.ds(first, size), start : start + width] = pair[p].astype(
                        jnp.bfloat16
                    )

    edge_row = lax.broadcasted_iota(jnp.int32, (EDGE, width), 0)
    has_edge = jnp.where(epoch == epoch_count - 1, 1.0, 0.0)

    def sections(cut, tiles):
        rows = cut_rows + (EDGE if cut == cuts - 1 else 0)
        stack = [turned[tile, cut * cut_rows : cut * cut_rows + rows, :] for tile in tiles]
        moved = jnp.dot(
            jnp.concatenate(stack, 0), second_ref[...], preferred_element_type=jnp.float32
        )
        blocks = []
        for i in range(len(tiles)):
            pieces = [
                moved[i * rows : (i + 1) * rows, q * width : (q + 1) * width] for q in range(parts)
            ]
            block = [piece[:cut_rows] for piece in pieces]
            if cut == cuts - 1:
                edge = jnp.zeros((EDGE, width), jnp.float32)
                for q, piece in enumerate(pieces):
                    edge = jnp.where(edge_row == q, piece[cut_rows : cut_rows + 1] * has_edge, edge)
                block.append(edge)
            blocks.append(jnp.concatenate(block, 0))
        return blocks

    def forward(cut, k):
        tile_copy(cut, k).wait_recv()
        for j in range(1, epoch_count):
            epoch_copy(cut, k, j).start()

    order = [0] + [k for pair in zip(range(1, half), range(half // 2, half)) for k in pair]
    order = order[: 1 + 2 * (half // 2 - 1)] + [half - 1] if half > 1 else [0]
    pending = []
    for cut in range(cuts):

        def row_group(i, carry):
            transform(pl.multiple_of(i * group, group), group)
            return carry

        if not pending:
            steps = cut_rows // group
            lax.fori_loop(cut * steps, (cut + 1) * steps, row_group, 0)
        else:
            for i in range(cut_rows // group):
                transform(cut * cut_rows + i * group, group)
                if pending:
                    forward(*pending.pop(0))
        if cut == cuts - 1:
            transform(rows_here, EDGE)
        if cut == 0:
            pl.semaphore_wait(barrier, half + epoch_count - 1)
        for b in range(0, half, batch):
            ks = order[b : b + batch]
            tiles = [exclusive(mine, k, half) * 2 + 1 - side for k in ks]
            for k, block in zip(ks, sections(cut, tiles)):
                given[k, rows_of(cut), :] = block.astype(jnp.bfloat16)
                partner_copy(cut, k).start()
        for b in range(0, half, batch):
            ks = order[b : b + batch]
            tiles = [exclusive(mine, k, half) * 2 + side for k in ks]
            for k, block in zip(ks, sections(cut, tiles)):
                partner_copy(cut, k).wait_recv()
                both = (block + landed[k, rows_of(cut), :].astype(jnp.float32)).astype(jnp.bfloat16)
                if k == 0:
                    full[epoch * half + mine, rows_of(cut), :] = both
                    for j in range(1, epoch_count):
                        epoch_copy(cut, 0, j).start()
                else:
                    folded[k, rows_of(cut), :] = both
                    tile_copy(cut, k).start()
                if cut > 0 and pending:
                    forward(*pending.pop(0))
        pending += [(cut, k) for k in order[1:]]
    for cut, k in pending:
        forward(cut, k)

    def mix_rows(e, cut, first, edges=None):
        for h in range(chunks):
            values = []
            for j in range(half):
                value = tuple(
                    full[
                        e * half + j, pl.ds((cut * parts + h * 2 + p) * cut_rows + first, group), :
                    ].astype(jnp.float32)
                    for p in range(2)
                )
                values.append(epoch_turn(value, j, epoch, epoch_count))
            done = dft(values + [None] * half, kept)
            if edges is not None:
                top = lax.broadcasted_iota(jnp.int32, (group, width), 0) == 0
                done = [
                    tuple(a + jnp.where(top, b, 0.0) for a, b in zip(part, edge))
                    for part, edge in zip(done, edges[h])
                ]
            for c, part in enumerate(done):
                for p in range(2):
                    row = pl.multiple_of(
                        p * band + e * rows_here + cut * cut_rows + first, group
                    )
                    mixed_ref[c, pl.ds(row, group), h * width : (h + 1) * width] = part[p].astype(
                        jnp.bfloat16
                    )

    def mix(e, cut):
        def step(i, carry):
            mix_rows(e, cut, pl.multiple_of(i * group, group))
            return carry

        lax.fori_loop(0, cut_rows // group, step, 0)

    for cut in range(cuts):
        mix(epoch, cut)
    for cut in range(cuts):
        for j in range(1, epoch_count):

            def arrive(k, carry, cut=cut, j=j):
                epoch_copy(cut, k, j).wait_recv()
                return carry

            lax.fori_loop(0, half, arrive, 0)
            mix(lax.rem(epoch + epoch_count - j, epoch_count), cut)

    edges = []
    for h in range(chunks):
        values = [None]
        for j in range(half):
            block = full[(epoch_count - 1) * half + j, cuts * parts * cut_rows :, :]
            block = block.astype(jnp.float32)
            value = tuple(block[h * 2 + p : h * 2 + p + 1] for p in range(2))
            values.append(epoch_turn(value, j + 1, epoch, epoch_count))
        edges.append(dft(values + [None] * (tile_count - half - 1), kept))
    mix_rows(0, 0, 0, edges)
    table_copy.wait()

    for cut in range(cuts):

        def finish(k, carry, cut=cut):
            tile_copy(cut, k).wait_send()
            return carry

        lax.fori_loop(1, half, finish, 0)

        def settle(k, carry, cut=cut):
            partner_copy(cut, k).wait_send()
            for j in range(1, epoch_count):
                epoch_copy(cut, k, j).wait_send()
            return carry

        lax.fori_loop(0, half, settle, 0)


def image_kernel(image_scale, mixed_ref, last_ref, rows_ref, cols_ref, out_ref, held, sem):
    kept = held.shape[0]
    tall = jnp.transpose(rows_ref[...]) * image_scale
    copies = [pltpu.make_async_copy(held.at[c], out_ref.at[c], sem.at[c]) for c in range(kept)]
    for c in range(kept):
        pixels = jnp.dot(last_ref[c], mixed_ref[c], preferred_element_type=jnp.float32)
        held[c] = pixels * tall[:, c : c + 1] * cols_ref[...]
        copies[c].start()
    for c in range(kept):
        copies[c].wait()


def turns(product, modulus):
    angles = (product % modulus) * (2.0 * math.pi / modulus)
    return np.cos(angles), np.sin(angles)


def make_tables(tile_count, block_len):
    grid_size = tile_count * block_len
    long_idx = np.arange(block_len)
    tile_idx = np.arange(tile_count)
    turn_cos, turn_sin = turns(tile_idx[:, None] * long_idx[None, :], grid_size)
    c, s = turns(long_idx[:, None] * long_idx[None, :], block_len)
    second = np.stack([np.stack([c, s], 1), np.stack([-s, c], 1)], 0)
    width = min(LANES, block_len)
    second = second.reshape(2 * block_len, 2, block_len // width, width)
    second = second.transpose(0, 2, 1, 3).reshape(2 * block_len, 2 * block_len)
    pixel = long_idx[None, :] * tile_count + tile_idx[:, None]
    c, s = turns(pixel[:, :, None] * long_idx[None, None, :], grid_size)
    last = np.concatenate([c, -s], -1)
    return (
        turn_cos.astype(np.float32),
        turn_sin.astype(np.float32),
        second.astype(jnp.bfloat16),
        last.astype(jnp.bfloat16),
    )


def hbm(count):
    return [pl.BlockSpec(memory_space=pltpu.HBM)] * count


def vmem(count):
    return [pl.BlockSpec(memory_space=pltpu.VMEM)] * count


def body(tables, owners, row_offsets, col_offsets, samples, coords, taper_rows, taper_cols):
    tile_count = lax.axis_size("tile")
    epoch_count = lax.axis_size("epoch")
    n_slots = owners.shape[1]
    n_samples = samples.shape[3]
    capacity = max(2, n_slots * 5 // (4 * tile_count))
    capacity += capacity % 2
    lane_step = max(8, 1 << (capacity - 1).bit_length())
    band = taper_cols.shape[0]
    width = min(LANES, band)
    half, kept = tile_count // 2, tile_count // epoch_count
    rows_here = band // epoch_count
    parts = 2 * (band // width)
    sizes = (tile_count, epoch_count, capacity, lane_step, band)
    block_rows = capacity * SUB // 2 + EDGE
    spots = -(-tile_count // (LANES // lane_step)) * LANES

    tile_sems = pltpu.SemaphoreType.DMA((tile_count,))
    epoch_sems = pltpu.SemaphoreType.DMA(((epoch_count - 1) * tile_count,))
    pool, slot_list, weights = pl.pallas_call(
        functools.partial(grid_kernel, sizes),
        out_shape=[
            jax.ShapeDtypeStruct((epoch_count * tile_count, block_rows, LANES), jnp.bfloat16),
            jax.ShapeDtypeStruct((epoch_count, FIELDS, spots), jnp.int32),
            jax.ShapeDtypeStruct((epoch_count, FIELDS, LANES), jnp.float32),
        ],
        in_specs=hbm(5),
        out_specs=vmem(3),
        scratch_shapes=[
            *(
                pltpu.VMEM(array.shape, array.dtype)
                for array in (owners, row_offsets, col_offsets, coords, samples)
            ),
            pltpu.SemaphoreType.DMA((5,)),
            pltpu.VMEM((tile_count, block_rows, LANES), jnp.bfloat16),
            pltpu.VMEM((tile_count, 2 * lane_step, 2 * n_samples), jnp.float32),
            tile_sems,
            tile_sems,
            epoch_sems,
            epoch_sems,
        ],
        compiler_params=pltpu.CompilerParams(
            vmem_limit_bytes=VMEM_BYTES, collective_id=1, has_side_effects=True
        ),
        name="grid_slots",
    )(
        *(
            pltpu.with_memory_space_constraint(array, pltpu.HBM)
            for array in (owners, row_offsets, col_offsets, coords, samples)
        )
    )

    lane_blocks = tile_count * band // LANES
    acc = pl.pallas_call(
        functools.partial(place_kernel, tile_count),
        out_shape=jax.ShapeDtypeStruct(
            (2, lane_blocks + 1, rows_here + 2 * SUB, LANES), jnp.float32
        ),
        in_specs=[pl.BlockSpec(memory_space=pltpu.SMEM)] + vmem(2),
        out_specs=vmem(1)[0],
        compiler_params=pltpu.CompilerParams(vmem_limit_bytes=VMEM_BYTES),
        name="place_slots",
    )(slot_list, weights, pool)

    cuts = 2 if rows_here % 32 == 0 else 1
    block_shape = (parts * rows_here + EDGE, width)
    sems = [pltpu.SemaphoreType.DMA((cuts * half,))] * 4
    sems += [pltpu.SemaphoreType.DMA((cuts * (epoch_count - 1) * half,))] * 2
    mixed, last_here = pl.pallas_call(
        functools.partial(swap_kernel, (tile_count, epoch_count, band), cuts),
        out_shape=[
            jax.ShapeDtypeStruct((kept, 2 * band, band), jnp.bfloat16),
            jax.ShapeDtypeStruct((kept, band, 2 * band), jnp.bfloat16),
        ],
        in_specs=vmem(4) + hbm(1),
        out_specs=vmem(2),
        scratch_shapes=[
            pltpu.SemaphoreType.DMA((1,)),
            pltpu.VMEM((tile_count, rows_here + EDGE, 2 * band), jnp.bfloat16),
            pltpu.VMEM((half, *block_shape), jnp.bfloat16),
            pltpu.VMEM((half, *block_shape), jnp.bfloat16),
            pltpu.VMEM((half, *block_shape), jnp.bfloat16),
            pltpu.VMEM((epoch_count * half, *block_shape), jnp.bfloat16),
            *sems,
        ],
        compiler_params=pltpu.CompilerParams(
            vmem_limit_bytes=VMEM_BYTES, collective_id=0, has_side_effects=True
        ),
        name="swap_rows",
    )(acc, *(jnp.asarray(table) for table in tables))

    image_scale = math.sqrt(n_slots) / (64.0 * tile_count * math.sqrt(epoch_count))
    return pl.pallas_call(
        functools.partial(image_kernel, image_scale),
        out_shape=jax.ShapeDtypeStruct((kept, band, band), jnp.float32),
        in_specs=vmem(4),
        out_specs=hbm(1)[0],
        scratch_shapes=[
            pltpu.VMEM((kept, band, band), jnp.float32),
            pltpu.SemaphoreType.DMA((kept,)),
        ],
        compiler_params=pltpu.CompilerParams(vmem_limit_bytes=VMEM_BYTES),
        name="image_rows",
    )(mixed, last_here, taper_rows, taper_cols[None, :])


def solution(mesh):
    placed = (
        P("epoch", "tile"),
        P("epoch", "tile"),
        P("epoch", "tile"),
        P("epoch", "tile", None, None),
        P("epoch", "tile", None, None),
        P("epoch", None),
        P("tile"),
    )

    def whole(owners, row_offsets, col_offsets, samples, coords, taper_rows, taper_cols):
        tables = make_tables(mesh.shape["tile"], taper_cols.shape[0] // mesh.shape["tile"])
        return jax.shard_map(
            functools.partial(body, tables),
            mesh=mesh,
            in_specs=placed,
            out_specs=P("epoch", None, "tile"),
            check_vma=False,
        )(owners, row_offsets, col_offsets, samples, coords, taper_rows, taper_cols)

    return whole
```

```python
import functools
import math

import jax
import jax.numpy as jnp
import numpy as np
from jax import lax
from jax.experimental import pallas as pl
from jax.experimental.pallas import tpu as pltpu
from jax.sharding import PartitionSpec as P

SUB = 32
LANES = 128
EDGE = 16
FIELDS = 8
UNROLL = 8
BEHIND = 2
VMEM_BYTES = 24 * 1024 * 1024
MESH = pl.DeviceIdType.MESH


def dft(values, wanted, modulus=None):
    count = len(values)
    if all(v is None for v in values):
        return [None] * wanted
    if count == 1:
        return list(values)
    half = count // 2
    need = min(wanted, half)
    even, odd = dft(values[0::2], need), dft(values[1::2], need)
    low, high = [], []
    for k in range(need):
        e, o = even[k], odd[k]
        t = None if o is None else turn(o, k, count)
        low.append(plus(e, t))
        if half + k < wanted:
            high.append(minus(e, t))
    return low + high


def turn(value, k, count):
    re, im = value
    s = math.sqrt(0.5)
    k %= count
    if k == 0:
        return re, im
    if 2 * k == count:
        return -re, -im
    if 4 * k == count:
        return -im, re
    if 8 * k == count:
        return (re - im) * s, (re + im) * s
    if 8 * k == 3 * count:
        return (re + im) * -s, (re - im) * s
    c, s = math.cos(2 * math.pi * k / count), math.sin(2 * math.pi * k / count)
    return re * c - im * s, re * s + im * c


def plus(a, b):
    if a is None or b is None:
        return b if a is None else a
    return a[0] + b[0], a[1] + b[1]


def minus(a, b):
    if b is None:
        return a
    if a is None:
        return -b[0], -b[1]
    return a[0] - b[0], a[1] - b[1]


def epoch_turn(value, j, epoch, epoch_count):
    angles = [2 * math.pi * ((j * e) % epoch_count) / epoch_count for e in range(epoch_count)]

    def pick(numbers):
        chosen = jnp.float32(numbers[0])
        for e in range(1, epoch_count):
            chosen = jnp.where(epoch == e, jnp.float32(numbers[e]), chosen)
        return chosen

    cos, sin = [round(math.cos(a), 15) for a in angles], [round(math.sin(a), 15) for a in angles]
    re, im = value
    if not any(sin):
        if all(c == 1.0 for c in cos):
            return value
        c = pick(cos)
        return re * c, im * c
    c, s = pick(cos), pick(sin)
    return re * c - im * s, re * s + im * c


def exclusive(a, b, count):
    total = 0
    for bit in range(count.bit_length() - 1):
        x, y = lax.rem(a // (1 << bit), 2), lax.rem(b // (1 << bit), 2)
        total += (x + y - 2 * x * y) * (1 << bit)
    return total


def near_and_far(i, count):
    return jnp.where(
        i == count - 2,
        count - 1,
        jnp.where(lax.rem(i, 2) == 0, 1 + i // 2, count // 2 + i // 2),
    )


def grid_kernel(
    sizes,
    *refs,
):
    tile_count, epoch_count, capacity, band = sizes
    inputs, (pool_ref, list_ref, weight_ref), scratch = refs[:5], refs[5:8], refs[8:]
    owner_ref, row_ref, col_ref, coords_ref, samples_ref, in_sem = scratch[:6]
    packed, raw = scratch[6:8], scratch[8:10]
    t_send, t_recv, x_send, x_recv = scratch[10:]
    fetches = [
        pltpu.make_async_copy(given, held, in_sem.at[i])
        for i, (given, held) in enumerate(zip(inputs, scratch))
    ]
    for fetch in fetches:
        fetch.start()
    me, epoch = lax.axis_index("tile"), lax.axis_index("epoch")
    n_slots = owner_ref.shape[1]
    n_samples = coords_ref.shape[3]
    pieces = n_samples // LANES
    lane_step = max(FIELDS, 1 << (capacity - 1).bit_length())
    pad = -(-capacity // FIELDS) * FIELDS
    info = 2 * pieces * capacity
    info_rows = raw[1].shape[1] - info
    half = tile_count // 2
    per_meta = LANES // lane_step
    groups = -(-tile_count // per_meta)
    slot_rows = SUB // 2

    barrier = pltpu.get_barrier_semaphore()

    def greet(k, carry):
        peer = lax.rem(me + k, tile_count)
        pl.semaphore_signal(barrier, inc=1, device_id={"tile": peer}, device_id_type=MESH)
        return carry

    lax.fori_loop(1, tile_count, greet, 0)
    for k in range(1, epoch_count):
        peer = lax.rem(epoch + k, epoch_count)
        pl.semaphore_signal(barrier, inc=1, device_id={"epoch": peer}, device_id_type=MESH)

    for fetch in fetches:
        fetch.wait()
    owner = owner_ref[...]
    mirrored = owner >= half
    target = jnp.where(mirrored, 2 * (tile_count - 1 - owner) + 1, 2 * owner)
    row = jnp.where(mirrored, band - (SUB - 1) - row_ref[...], row_ref[...])
    col = jnp.where(mirrored, tile_count * band - (SUB - 1) - col_ref[...], col_ref[...])
    mine = lax.broadcasted_iota(jnp.int32, (tile_count, n_slots), 0) == target
    before = lax.broadcasted_iota(jnp.int32, (n_slots, n_slots), 0) < lax.broadcasted_iota(
        jnp.int32, (n_slots, n_slots), 1
    )
    rank = jnp.dot(
        jnp.where(mine, 1.0, 0.0).astype(jnp.bfloat16),
        jnp.where(before, 1.0, 0.0).astype(jnp.bfloat16),
        preferred_element_type=jnp.float32,
    ).astype(jnp.int32)
    key = jnp.where(mine, rank, -LANES)
    fields = [jnp.ones_like(row), row, col // LANES, col % LANES]
    fields = jnp.concatenate(fields + [jnp.zeros_like(row)] * (info_rows - len(fields)), 0)
    fields = fields.astype(jnp.float32).astype(jnp.bfloat16)
    lane = lax.broadcasted_iota(jnp.int32, (LANES, n_slots), 0) - lax.rem(me, per_meta) * lane_step
    first = lax.broadcasted_iota(jnp.int32, (pad, n_slots), 0)
    hits, notes = [], []
    for t in range(tile_count):
        hits.append(jnp.where(key[t : t + 1] == first, 1.0, 0.0))
        spot = jnp.where(key[t : t + 1] == lane, 1.0, 0.0).astype(jnp.bfloat16)
        notes.append(
            lax.dot_general(
                fields, spot, (((1,), (1,)), ((), ())), preferred_element_type=jnp.float32
            )
        )
    hits = jnp.concatenate(hits, 0)
    here = jnp.dot(
        hits,
        jnp.concatenate([coords_ref[0, :, p, :] for p in range(2)], 1) * 0.25,
        precision=lax.Precision.HIGHEST,
        preferred_element_type=jnp.float32,
    )
    samples = samples_ref[0].astype(jnp.float32)
    samples = jnp.concatenate([samples[:, p, :] for p in range(2)], 1).astype(jnp.bfloat16)
    values = jnp.dot(hits.astype(jnp.bfloat16), samples, preferred_element_type=jnp.float32)
    for t in range(tile_count):
        for part, block in enumerate((here, values)):
            rows = [
                block[t * pad : t * pad + capacity, q * LANES : (q + 1) * LANES]
                for q in range(2 * pieces)
            ]
            if part == 1:
                rows.append(notes[t])
            packed[part][t] = jnp.concatenate(rows, 0).astype(packed[part].dtype)
    pl.semaphore_wait(barrier, tile_count + epoch_count - 2)

    def tile_copies(k):
        peer = exclusive(me, k, tile_count)
        return [
            pltpu.make_async_remote_copy(
                src_ref=packed[part].at[peer],
                dst_ref=raw[part].at[me],
                send_sem=t_send.at[part, k],
                recv_sem=t_recv.at[part, k],
                device_id={"tile": peer},
                device_id_type=MESH,
            )
            for part in range(2)
        ]

    def epoch_copies(k, j):
        origin = exclusive(me, k, tile_count)
        return [
            pltpu.make_async_remote_copy(
                src_ref=raw[part].at[origin],
                dst_ref=raw[part].at[j * tile_count + origin],
                send_sem=x_send.at[part, (j - 1) * tile_count + k],
                recv_sem=x_recv.at[part, (j - 1) * tile_count + k],
                device_id={"epoch": lax.rem(epoch + j, epoch_count)},
                device_id_type=MESH,
            )
            for part in range(2)
        ]

    def send(i, carry):
        for copy in tile_copies(near_and_far(i, tile_count)):
            copy.start()
        return carry

    lax.fori_loop(0, tile_count - 1, send, 0)
    for part in range(2):
        raw[part][me] = packed[part][me]
    for j in range(1, epoch_count):
        for copy in epoch_copies(0, j):
            copy.start()

    flip = lax.rem(me, 2)
    cells = lax.broadcasted_iota(jnp.int32, (SUB, n_samples), 0)
    cells = jnp.where(flip == 1, SUB - 1 - cells, cells).astype(jnp.float32) * 0.25
    sign = (1 - 2 * flip).astype(jnp.float32)

    def weights(at):
        distance = cells - at
        return jnp.square(jnp.maximum(1.0 - distance * distance, 0.0))

    def make(at):
        points, values = raw[0][at], raw[1][at].astype(jnp.float32)

        def line(block, part, k):
            rows = [(part * pieces + q) * capacity + k for q in range(pieces)]
            return jnp.concatenate([block[row : row + 1] for row in rows], 1)

        for k in range(capacity):
            along_u = weights(line(points, 0, k)).astype(jnp.bfloat16)
            along_v = weights(line(points, 1, k))
            re = line(values, 0, k) * along_v
            im = (line(values, 1, k) * sign) * along_v
            subgrid = lax.dot_general(
                along_u,
                jnp.concatenate([re, im], 0).astype(jnp.bfloat16),
                (((1,), (1,)), ((), ())),
                preferred_element_type=jnp.float32,
            )
            pool_ref[at, k * slot_rows : (k + 1) * slot_rows, :] = jnp.concatenate(
                [subgrid[:slot_rows], subgrid[slot_rows:]], 1
            ).astype(jnp.bfloat16)

    make(me)

    def take(i):
        k = near_and_far(i, tile_count)
        for copy in tile_copies(k):
            copy.wait_recv()
        for j in range(1, epoch_count):
            for copy in epoch_copies(k, j):
                copy.start()
        make(exclusive(me, k, tile_count))

    def take_crossed(i):
        k = jnp.where(i == 0, 0, near_and_far(i - 1, tile_count))
        for j in range(1, epoch_count):
            for copy in epoch_copies(k, j):
                copy.wait_recv()
            make(j * tile_count + exclusive(me, k, tile_count))

    behind = min(BEHIND, tile_count - 1)

    def ahead(i, carry):
        take(i)
        return carry

    def both(i, carry):
        take(i)
        take_crossed(i - behind)
        return carry

    def crossed(i, carry):
        take_crossed(i)
        return carry

    lax.fori_loop(0, behind, ahead, 0)
    lax.fori_loop(behind, tile_count - 1, both, 0)

    rows_here = band // epoch_count
    first_row = (epoch * rows_here - SUB).astype(jnp.float32)
    spots = groups * LANES
    below = lax.broadcasted_iota(jnp.int32, (LANES, LANES), 0) < lax.broadcasted_iota(
        jnp.int32, (LANES, LANES), 1
    )
    below = jnp.where(below, 1.0, 0.0).astype(jnp.bfloat16)
    spot = lax.broadcasted_iota(jnp.int32, (spots, LANES), 0).astype(jnp.float32)
    lanes = lax.broadcasted_iota(jnp.int32, (1, LANES), 1)
    field = lax.broadcasted_iota(jnp.int32, (FIELDS, spots), 0)

    def list_slots(j):
        found, held = jnp.zeros((1, 1), jnp.float32), jnp.zeros((1, 1), jnp.float32)
        gathered = jnp.zeros((EDGE, spots), jnp.float32)
        for g in range(groups):
            total = jnp.zeros((info_rows, LANES), jnp.float32)
            for s in range(g * per_meta, min(tile_count, (g + 1) * per_meta)):
                total += raw[1][j * tile_count + s, info:, :].astype(jnp.float32)
            valid, row = total[0:1], total[1:2] - first_row
            inside = (valid > 0) & (row > 0) & (row < rows_here + SUB)
            mask = jnp.where(inside, 1.0, 0.0)
            order = jnp.dot(
                mask.astype(jnp.bfloat16), below, preferred_element_type=jnp.float32
            )
            chosen = spot == jnp.where(inside, order + found, -1.0)
            source = (g * per_meta + lanes // lane_step).astype(jnp.float32)
            place = (lanes % lane_step).astype(jnp.float32)
            rows = [source, row, total[2:3], total[3:4], place]
            rows = jnp.concatenate(rows + [jnp.zeros_like(row)] * (EDGE - len(rows)), 0)
            gathered += lax.dot_general(
                rows.astype(jnp.bfloat16),
                jnp.where(chosen, 1.0, 0.0).astype(jnp.bfloat16),
                (((1,), (1,)), ((), ())),
                preferred_element_type=jnp.float32,
            )
            found += jnp.sum(mask, 1, keepdims=True)
            held += jnp.sum(valid, 1, keepdims=True)
        listed = jnp.where(field == FIELDS - 1, found, gathered[:FIELDS])
        list_ref[j] = listed.astype(jnp.int32)
        weight_ref[j] = jnp.broadcast_to(1.0 / jnp.maximum(held, 1.0), (FIELDS, LANES))

    list_slots(0)
    lax.fori_loop(tile_count - 1 - behind, tile_count, crossed, 0)
    for j in range(1, epoch_count):
        list_slots(j)

    def finish(k, carry):
        for copy in tile_copies(k):
            copy.wait_send()
        return carry

    lax.fori_loop(1, tile_count, finish, 0)

    def settle(k, carry):
        for j in range(1, epoch_count):
            for copy in epoch_copies(k, j):
                copy.wait_send()
        return carry

    lax.fori_loop(0, tile_count, settle, 0)


def place_kernel(tile_count, list_ref, weight_ref, pool_ref, acc):
    acc_rows = acc.shape[2]
    slot_rows = SUB // 2

    def clear(i, carry):
        acc[0, i] = jnp.zeros((acc_rows, LANES), jnp.float32)
        acc[1, i] = jnp.zeros((acc_rows, LANES), jnp.float32)
        return carry

    lax.fori_loop(0, acc.shape[1], clear, 0)
    lanes = lax.broadcasted_iota(jnp.int32, (slot_rows, LANES), 1)

    for e in range(list_ref.shape[0]):
        weight = jnp.concatenate([weight_ref[e]] * (slot_rows // FIELDS), 0)

        def per_batch(b, carry, e=e, weight=weight):
            placed = []
            for k in range(UNROLL):
                at = b * UNROLL + k
                source, row, block, start, place = (list_ref[e, f, at] for f in range(5))
                first = pl.multiple_of(place * slot_rows, slot_rows)
                data = pool_ref[e * tile_count + source, pl.ds(first, slot_rows), :]
                data = data.astype(jnp.float32) * weight
                turned = [
                    pltpu.roll(data, lax.rem(start + (LANES - i * SUB), LANES), 1)
                    for i in range(4)
                ]
                near = (lanes >= start) & (lanes < start + SUB)
                far = lanes < start + SUB - LANES
                windows = [
                    jnp.concatenate([jnp.where(mask, turned[i], 0.0) for i in (p, 2 + p)], 0)
                    for p in range(2)
                    for mask in (near, far)
                ]
                placed.append((row, block, windows))
            for row, block, windows in placed:
                spots = [(p, block + h, pl.ds(row, SUB)) for p in range(2) for h in range(2)]
                sums = [acc[spot] + window for spot, window in zip(spots, windows)]
                for spot, total in zip(spots, sums):
                    acc[spot] = total
            return carry

        lax.fori_loop(0, (list_ref[e, FIELDS - 1, 0] + UNROLL - 1) // UNROLL, per_batch, 0)


def swap_kernel(
    sizes, cuts, acc_ref, cos_ref, sin_ref, second_ref, last_ref, mixed_ref, here_ref, *scratch
):
    tile_count, epoch_count, band = sizes
    table_sem, scratch = scratch[0], scratch[1:]
    turned, given, landed, folded, full = scratch[:5]
    p_send, p_recv, t_send, t_recv, x_send, x_recv = scratch[5:]
    me, epoch = lax.axis_index("tile"), lax.axis_index("epoch")
    half, kept = tile_count // 2, tile_count // epoch_count
    mine, side = me // 2, lax.rem(me, 2)
    partner = me + 1 - 2 * side
    table_copy = pltpu.make_async_copy(
        last_ref.at[pl.ds(epoch * kept, kept)], here_ref, table_sem.at[0]
    )
    table_copy.start()
    rows_here = band // epoch_count
    cut_rows = rows_here // cuts
    width = min(LANES, band)
    chunks = band // width
    parts = 2 * chunks
    lane_blocks = acc_ref.shape[1] - 1
    group = min(16, cut_rows)
    batch = min(4, half)

    barrier = pltpu.get_barrier_semaphore()

    def greet(k, carry):
        peer = exclusive(mine, k, half) * 2 + side
        pl.semaphore_signal(barrier, inc=1, device_id={"tile": peer}, device_id_type=MESH)
        return carry

    lax.fori_loop(1, half, greet, 0)
    pl.semaphore_signal(barrier, inc=1, device_id={"tile": partner}, device_id_type=MESH)
    for k in range(1, epoch_count):
        peer = lax.rem(epoch + k, epoch_count)
        pl.semaphore_signal(barrier, inc=1, device_id={"epoch": peer}, device_id_type=MESH)

    def rows_of(cut):
        edge = EDGE if cut == cuts - 1 else 0
        return pl.ds(cut * parts * cut_rows, parts * cut_rows + edge)

    def partner_copy(cut, k):
        return pltpu.make_async_remote_copy(
            src_ref=given.at[k, rows_of(cut)],
            dst_ref=landed.at[k, rows_of(cut)],
            send_sem=p_send.at[cut * half + k],
            recv_sem=p_recv.at[cut * half + k],
            device_id={"tile": partner},
            device_id_type=MESH,
        )

    def tile_copy(cut, k):
        return pltpu.make_async_remote_copy(
            src_ref=folded.at[k, rows_of(cut)],
            dst_ref=full.at[epoch * half + mine, rows_of(cut)],
            send_sem=t_send.at[cut * half + k],
            recv_sem=t_recv.at[cut * half + k],
            device_id={"tile": exclusive(mine, k, half) * 2 + side},
            device_id_type=MESH,
        )

    def epoch_copy(cut, k, j):
        origin = epoch * half + exclusive(mine, k, half)
        at = (cut * (epoch_count - 1) + j - 1) * half + k
        return pltpu.make_async_remote_copy(
            src_ref=full.at[origin, rows_of(cut)],
            dst_ref=full.at[origin, rows_of(cut)],
            send_sem=x_send.at[at],
            recv_sem=x_recv.at[at],
            device_id={"epoch": lax.rem(epoch + j, epoch_count)},
            device_id_type=MESH,
        )

    def transform(first, size):
        for h in range(chunks):
            values = []
            for a in range(tile_count):
                col = a * band + h * width
                lane, at = col % LANES, col // LANES
                value = [
                    acc_ref[p, at, pl.ds(SUB + first, size), lane : lane + width] for p in range(2)
                ]
                if col == 0:
                    for p in range(2):
                        value[p] += acc_ref[p, lane_blocks, pl.ds(SUB + first, size), :width]
                values.append(tuple(value))
            lanes = slice(h * width, (h + 1) * width)
            for m, (re, im) in enumerate(dft(values, tile_count)):
                c, s = cos_ref[m : m + 1, lanes], sin_ref[m : m + 1, lanes]
                pair = (re * c - im * s, re * s + im * c)
                for p in range(2):
                    start = p * band + h * width
                    turned[m, pl.ds(first, size), start : start + width] = pair[p].astype(
                        jnp.bfloat16
                    )

    edge_row = lax.broadcasted_iota(jnp.int32, (EDGE, width), 0)
    has_edge = jnp.where(epoch == epoch_count - 1, 1.0, 0.0)

    def sections(cut, tiles):
        rows = cut_rows + (EDGE if cut == cuts - 1 else 0)
        stack = [turned[tile, cut * cut_rows : cut * cut_rows + rows, :] for tile in tiles]
        moved = jnp.dot(
            jnp.concatenate(stack, 0), second_ref[...], preferred_element_type=jnp.float32
        )
        blocks = []
        for i in range(len(tiles)):
            pieces = [
                moved[i * rows : (i + 1) * rows, q * width : (q + 1) * width] for q in range(parts)
            ]
            block = [piece[:cut_rows] for piece in pieces]
            if cut == cuts - 1:
                edge = jnp.zeros((EDGE, width), jnp.float32)
                for q, piece in enumerate(pieces):
                    edge = jnp.where(edge_row == q, piece[cut_rows : cut_rows + 1] * has_edge, edge)
                block.append(edge)
            blocks.append(jnp.concatenate(block, 0))
        return blocks

    def forward(cut, k):
        tile_copy(cut, k).wait_recv()
        for j in range(1, epoch_count):
            epoch_copy(cut, k, j).start()

    order = [0] + [k for pair in zip(range(1, half), range(half // 2, half)) for k in pair]
    order = order[: 1 + 2 * (half // 2 - 1)] + [half - 1] if half > 1 else [0]
    pending = []
    for cut in range(cuts):

        def row_group(i, carry):
            transform(pl.multiple_of(i * group, group), group)
            return carry

        if not pending:
            steps = cut_rows // group
            lax.fori_loop(cut * steps, (cut + 1) * steps, row_group, 0)
        else:
            for i in range(cut_rows // group):
                transform(cut * cut_rows + i * group, group)
                if pending:
                    forward(*pending.pop(0))
        if cut == cuts - 1:
            transform(rows_here, EDGE)
        if cut == 0:
            pl.semaphore_wait(barrier, half + epoch_count - 1)
        for b in range(0, half, batch):
            ks = order[b : b + batch]
            tiles = [exclusive(mine, k, half) * 2 + 1 - side for k in ks]
            for k, block in zip(ks, sections(cut, tiles)):
                given[k, rows_of(cut), :] = block.astype(jnp.bfloat16)
                partner_copy(cut, k).start()
        for b in range(0, half, batch):
            ks = order[b : b + batch]
            tiles = [exclusive(mine, k, half) * 2 + side for k in ks]
            for k, block in zip(ks, sections(cut, tiles)):
                partner_copy(cut, k).wait_recv()
                both = (block + landed[k, rows_of(cut), :].astype(jnp.float32)).astype(jnp.bfloat16)
                if k == 0:
                    full[epoch * half + mine, rows_of(cut), :] = both
                    for j in range(1, epoch_count):
                        epoch_copy(cut, 0, j).start()
                else:
                    folded[k, rows_of(cut), :] = both
                    tile_copy(cut, k).start()
                if cut > 0 and pending:
                    forward(*pending.pop(0))
        pending += [(cut, k) for k in order[1:]]
    for cut, k in pending:
        forward(cut, k)

    def mix_rows(e, cut, first, edges=None):
        for h in range(chunks):
            values = []
            for j in range(half):
                value = tuple(
                    full[
                        e * half + j, pl.ds((cut * parts + h * 2 + p) * cut_rows + first, group), :
                    ].astype(jnp.float32)
                    for p in range(2)
                )
                values.append(epoch_turn(value, j, epoch, epoch_count))
            done = dft(values + [None] * half, kept)
            if edges is not None:
                top = lax.broadcasted_iota(jnp.int32, (group, width), 0) == 0
                done = [
                    tuple(a + jnp.where(top, b, 0.0) for a, b in zip(part, edge))
                    for part, edge in zip(done, edges[h])
                ]
            for c, part in enumerate(done):
                for p in range(2):
                    row = pl.multiple_of(
                        p * band + e * rows_here + cut * cut_rows + first, group
                    )
                    mixed_ref[c, pl.ds(row, group), h * width : (h + 1) * width] = part[p].astype(
                        jnp.bfloat16
                    )

    def mix(e, cut):
        def step(i, carry):
            mix_rows(e, cut, pl.multiple_of(i * group, group))
            return carry

        lax.fori_loop(0, cut_rows // group, step, 0)

    for cut in range(cuts):
        mix(epoch, cut)
    for cut in range(cuts):
        for j in range(1, epoch_count):

            def arrive(k, carry, cut=cut, j=j):
                epoch_copy(cut, k, j).wait_recv()
                return carry

            lax.fori_loop(0, half, arrive, 0)
            mix(lax.rem(epoch + epoch_count - j, epoch_count), cut)

    edges = []
    for h in range(chunks):
        values = [None]
        for j in range(half):
            block = full[(epoch_count - 1) * half + j, cuts * parts * cut_rows :, :]
            block = block.astype(jnp.float32)
            value = tuple(block[h * 2 + p : h * 2 + p + 1] for p in range(2))
            values.append(epoch_turn(value, j + 1, epoch, epoch_count))
        edges.append(dft(values + [None] * (tile_count - half - 1), kept))
    mix_rows(0, 0, 0, edges)
    table_copy.wait()

    for cut in range(cuts):

        def finish(k, carry, cut=cut):
            tile_copy(cut, k).wait_send()
            return carry

        lax.fori_loop(1, half, finish, 0)

        def settle(k, carry, cut=cut):
            partner_copy(cut, k).wait_send()
            for j in range(1, epoch_count):
                epoch_copy(cut, k, j).wait_send()
            return carry

        lax.fori_loop(0, half, settle, 0)


def image_kernel(image_scale, mixed_ref, last_ref, rows_ref, cols_ref, out_ref, held, sem):
    kept = held.shape[0]
    tall = jnp.transpose(rows_ref[...]) * image_scale
    copies = [pltpu.make_async_copy(held.at[c], out_ref.at[c], sem.at[c]) for c in range(kept)]
    for c in range(kept):
        pixels = jnp.dot(last_ref[c], mixed_ref[c], preferred_element_type=jnp.float32)
        held[c] = pixels * tall[:, c : c + 1] * cols_ref[...]
        copies[c].start()
    for c in range(kept):
        copies[c].wait()


def turns(product, modulus):
    angles = (product % modulus) * (2.0 * math.pi / modulus)
    return np.cos(angles), np.sin(angles)


def make_tables(tile_count, block_len):
    grid_size = tile_count * block_len
    long_idx = np.arange(block_len)
    tile_idx = np.arange(tile_count)
    turn_cos, turn_sin = turns(tile_idx[:, None] * long_idx[None, :], grid_size)
    c, s = turns(long_idx[:, None] * long_idx[None, :], block_len)
    second = np.stack([np.stack([c, s], 1), np.stack([-s, c], 1)], 0)
    width = min(LANES, block_len)
    second = second.reshape(2 * block_len, 2, block_len // width, width)
    second = second.transpose(0, 2, 1, 3).reshape(2 * block_len, 2 * block_len)
    pixel = long_idx[None, :] * tile_count + tile_idx[:, None]
    c, s = turns(pixel[:, :, None] * long_idx[None, None, :], grid_size)
    last = np.concatenate([c, -s], -1)
    return (
        turn_cos.astype(np.float32),
        turn_sin.astype(np.float32),
        second.astype(jnp.bfloat16),
        last.astype(jnp.bfloat16),
    )


def hbm(count):
    return [pl.BlockSpec(memory_space=pltpu.HBM)] * count


def vmem(count):
    return [pl.BlockSpec(memory_space=pltpu.VMEM)] * count


def body(tables, owners, row_offsets, col_offsets, samples, coords, taper_rows, taper_cols):
    tile_count = lax.axis_size("tile")
    epoch_count = lax.axis_size("epoch")
    n_slots = owners.shape[1]
    n_samples = samples.shape[3]
    capacity = max(2, n_slots * 5 // (4 * tile_count))
    capacity += capacity % 2
    lane_step = max(8, 1 << (capacity - 1).bit_length())
    band = taper_cols.shape[0]
    width = min(LANES, band)
    half, kept = tile_count // 2, tile_count // epoch_count
    rows_here = band // epoch_count
    parts = 2 * (band // width)
    sizes = (tile_count, epoch_count, capacity, band)
    raw_rows = 2 * n_samples // LANES * capacity
    raw_shapes = [
        ((raw_rows, LANES), jnp.float32),
        ((-(-(raw_rows + FIELDS) // EDGE) * EDGE, LANES), jnp.bfloat16),
    ]
    spots = -(-tile_count // (LANES // lane_step)) * LANES

    tile_sems = pltpu.SemaphoreType.DMA((2, tile_count))
    epoch_sems = pltpu.SemaphoreType.DMA((2, (epoch_count - 1) * tile_count))
    pool, slot_list, weights = pl.pallas_call(
        functools.partial(grid_kernel, sizes),
        out_shape=[
            jax.ShapeDtypeStruct(
                (epoch_count * tile_count, capacity * SUB // 2, LANES), jnp.bfloat16
            ),
            jax.ShapeDtypeStruct((epoch_count, FIELDS, spots), jnp.int32),
            jax.ShapeDtypeStruct((epoch_count, FIELDS, LANES), jnp.float32),
        ],
        in_specs=hbm(5),
        out_specs=vmem(3),
        scratch_shapes=[
            *(
                pltpu.VMEM(array.shape, array.dtype)
                for array in (owners, row_offsets, col_offsets, coords, samples)
            ),
            pltpu.SemaphoreType.DMA((5,)),
            *(
                pltpu.VMEM((count, *shape), dtype)
                for count in (tile_count, epoch_count * tile_count)
                for shape, dtype in raw_shapes
            ),
            tile_sems,
            tile_sems,
            epoch_sems,
            epoch_sems,
        ],
        compiler_params=pltpu.CompilerParams(
            vmem_limit_bytes=VMEM_BYTES, collective_id=1, has_side_effects=True
        ),
        name="grid_slots",
    )(
        *(
            pltpu.with_memory_space_constraint(array, pltpu.HBM)
            for array in (owners, row_offsets, col_offsets, coords, samples)
        )
    )

    lane_blocks = tile_count * band // LANES
    acc = pl.pallas_call(
        functools.partial(place_kernel, tile_count),
        out_shape=jax.ShapeDtypeStruct(
            (2, lane_blocks + 1, rows_here + 2 * SUB, LANES), jnp.float32
        ),
        in_specs=[pl.BlockSpec(memory_space=pltpu.SMEM)] + vmem(2),
        out_specs=vmem(1)[0],
        compiler_params=pltpu.CompilerParams(vmem_limit_bytes=VMEM_BYTES),
        name="place_slots",
    )(slot_list, weights, pool)

    cuts = 2 if rows_here % 32 == 0 else 1
    block_shape = (parts * rows_here + EDGE, width)
    sems = [pltpu.SemaphoreType.DMA((cuts * half,))] * 4
    sems += [pltpu.SemaphoreType.DMA((cuts * (epoch_count - 1) * half,))] * 2
    mixed, last_here = pl.pallas_call(
        functools.partial(swap_kernel, (tile_count, epoch_count, band), cuts),
        out_shape=[
            jax.ShapeDtypeStruct((kept, 2 * band, band), jnp.bfloat16),
            jax.ShapeDtypeStruct((kept, band, 2 * band), jnp.bfloat16),
        ],
        in_specs=vmem(4) + hbm(1),
        out_specs=vmem(2),
        scratch_shapes=[
            pltpu.SemaphoreType.DMA((1,)),
            pltpu.VMEM((tile_count, rows_here + EDGE, 2 * band), jnp.bfloat16),
            pltpu.VMEM((half, *block_shape), jnp.bfloat16),
            pltpu.VMEM((half, *block_shape), jnp.bfloat16),
            pltpu.VMEM((half, *block_shape), jnp.bfloat16),
            pltpu.VMEM((epoch_count * half, *block_shape), jnp.bfloat16),
            *sems,
        ],
        compiler_params=pltpu.CompilerParams(
            vmem_limit_bytes=VMEM_BYTES, collective_id=0, has_side_effects=True
        ),
        name="swap_rows",
    )(acc, *(jnp.asarray(table) for table in tables))

    image_scale = math.sqrt(n_slots) / (64.0 * tile_count * math.sqrt(epoch_count))
    return pl.pallas_call(
        functools.partial(image_kernel, image_scale),
        out_shape=jax.ShapeDtypeStruct((kept, band, band), jnp.float32),
        in_specs=vmem(4),
        out_specs=hbm(1)[0],
        scratch_shapes=[
            pltpu.VMEM((kept, band, band), jnp.float32),
            pltpu.SemaphoreType.DMA((kept,)),
        ],
        compiler_params=pltpu.CompilerParams(vmem_limit_bytes=VMEM_BYTES),
        name="image_rows",
    )(mixed, last_here, taper_rows, taper_cols[None, :])


def solution(mesh):
    placed = (
        P("epoch", "tile"),
        P("epoch", "tile"),
        P("epoch", "tile"),
        P("epoch", "tile", None, None),
        P("epoch", "tile", None, None),
        P("epoch", None),
        P("tile"),
    )

    def whole(owners, row_offsets, col_offsets, samples, coords, taper_rows, taper_cols):
        tables = make_tables(mesh.shape["tile"], taper_cols.shape[0] // mesh.shape["tile"])
        return jax.shard_map(
            functools.partial(body, tables),
            mesh=mesh,
            in_specs=placed,
            out_specs=P("epoch", None, "tile"),
            check_vma=False,
        )(owners, row_offsets, col_offsets, samples, coords, taper_rows, taper_cols)

    return whole
```

```python
import functools
import math

import jax
import jax.numpy as jnp
import numpy as np
from jax import lax
from jax.experimental import pallas as pl
from jax.experimental.pallas import tpu as pltpu
from jax.sharding import PartitionSpec as P

SUB = 32
LANES = 128
EDGE = 16
FIELDS = 8
UNROLL = 8
BEHIND = 3
CUTS = 4
VMEM_BYTES = 24 * 1024 * 1024
MESH = pl.DeviceIdType.MESH


def dft(values, wanted, modulus=None):
    count = len(values)
    if all(v is None for v in values):
        return [None] * wanted
    if count == 1:
        return list(values)
    half = count // 2
    need = min(wanted, half)
    even, odd = dft(values[0::2], need), dft(values[1::2], need)
    low, high = [], []
    for k in range(need):
        e, o = even[k], odd[k]
        t = None if o is None else turn(o, k, count)
        low.append(plus(e, t))
        if half + k < wanted:
            high.append(minus(e, t))
    return low + high


def turn(value, k, count):
    re, im = value
    s = math.sqrt(0.5)
    k %= count
    if k == 0:
        return re, im
    if 2 * k == count:
        return -re, -im
    if 4 * k == count:
        return -im, re
    if 8 * k == count:
        return (re - im) * s, (re + im) * s
    if 8 * k == 3 * count:
        return (re + im) * -s, (re - im) * s
    c, s = math.cos(2 * math.pi * k / count), math.sin(2 * math.pi * k / count)
    return re * c - im * s, re * s + im * c


def plus(a, b):
    if a is None or b is None:
        return b if a is None else a
    return a[0] + b[0], a[1] + b[1]


def minus(a, b):
    if b is None:
        return a
    if a is None:
        return -b[0], -b[1]
    return a[0] - b[0], a[1] - b[1]


def epoch_turn(value, j, epoch, epoch_count):
    angles = [2 * math.pi * ((j * e) % epoch_count) / epoch_count for e in range(epoch_count)]

    def pick(numbers):
        chosen = jnp.float32(numbers[0])
        for e in range(1, epoch_count):
            chosen = jnp.where(epoch == e, jnp.float32(numbers[e]), chosen)
        return chosen

    cos, sin = [round(math.cos(a), 15) for a in angles], [round(math.sin(a), 15) for a in angles]
    re, im = value
    if not any(sin):
        if all(c == 1.0 for c in cos):
            return value
        c = pick(cos)
        return re * c, im * c
    c, s = pick(cos), pick(sin)
    return re * c - im * s, re * s + im * c


def exclusive(a, b, count):
    total = 0
    for bit in range(count.bit_length() - 1):
        x, y = lax.rem(a // (1 << bit), 2), lax.rem(b // (1 << bit), 2)
        total += (x + y - 2 * x * y) * (1 << bit)
    return total


def near_and_far(i, count):
    return jnp.where(
        i == count - 2,
        count - 1,
        jnp.where(lax.rem(i, 2) == 0, 1 + i // 2, count // 2 + i // 2),
    )


def grid_kernel(
    sizes,
    *refs,
):
    tile_count, epoch_count, capacity, band = sizes
    inputs, (pool_ref, list_ref, weight_ref), scratch = refs[:5], refs[5:8], refs[8:]
    owner_ref, row_ref, col_ref, coords_ref, samples_ref, in_sem = scratch[:6]
    packed, raw = scratch[6:8], scratch[8:10]
    t_send, t_recv, x_send, x_recv = scratch[10:]
    fetches = [
        pltpu.make_async_copy(given, held, in_sem.at[i])
        for i, (given, held) in enumerate(zip(inputs, scratch))
    ]
    for fetch in fetches:
        fetch.start()
    me, epoch = lax.axis_index("tile"), lax.axis_index("epoch")
    n_slots = owner_ref.shape[1]
    n_samples = coords_ref.shape[3]
    pieces = n_samples // LANES
    lane_step = max(FIELDS, 1 << (capacity - 1).bit_length())
    pad = -(-capacity // FIELDS) * FIELDS
    info = 2 * pieces * capacity
    info_rows = raw[1].shape[1] - info
    half = tile_count // 2
    per_meta = LANES // lane_step
    groups = -(-tile_count // per_meta)
    slot_rows = SUB // 2

    barrier = pltpu.get_barrier_semaphore()

    def greet(k, carry):
        peer = lax.rem(me + k, tile_count)
        pl.semaphore_signal(barrier, inc=1, device_id={"tile": peer}, device_id_type=MESH)
        return carry

    lax.fori_loop(1, tile_count, greet, 0)
    for k in range(1, epoch_count):
        peer = lax.rem(epoch + k, epoch_count)
        pl.semaphore_signal(barrier, inc=1, device_id={"epoch": peer}, device_id_type=MESH)

    for fetch in fetches:
        fetch.wait()
    owner = owner_ref[...]
    mirrored = owner >= half
    target = jnp.where(mirrored, 2 * (tile_count - 1 - owner) + 1, 2 * owner)
    row = jnp.where(mirrored, band - (SUB - 1) - row_ref[...], row_ref[...])
    col = jnp.where(mirrored, tile_count * band - (SUB - 1) - col_ref[...], col_ref[...])
    mine = lax.broadcasted_iota(jnp.int32, (tile_count, n_slots), 0) == target
    before = lax.broadcasted_iota(jnp.int32, (n_slots, n_slots), 0) < lax.broadcasted_iota(
        jnp.int32, (n_slots, n_slots), 1
    )
    rank = jnp.dot(
        jnp.where(mine, 1.0, 0.0).astype(jnp.bfloat16),
        jnp.where(before, 1.0, 0.0).astype(jnp.bfloat16),
        preferred_element_type=jnp.float32,
    ).astype(jnp.int32)
    key = jnp.where(mine, rank, -LANES)
    fields = [jnp.ones_like(row), row, col // LANES, col % LANES]
    fields = jnp.concatenate(fields + [jnp.zeros_like(row)] * (info_rows - len(fields)), 0)
    fields = fields.astype(jnp.float32).astype(jnp.bfloat16)
    lane = lax.broadcasted_iota(jnp.int32, (LANES, n_slots), 0) - lax.rem(me, per_meta) * lane_step
    first = lax.broadcasted_iota(jnp.int32, (pad, n_slots), 0)
    hits, notes = [], []
    for t in range(tile_count):
        hits.append(jnp.where(key[t : t + 1] == first, 1.0, 0.0))
        spot = jnp.where(key[t : t + 1] == lane, 1.0, 0.0).astype(jnp.bfloat16)
        notes.append(
            lax.dot_general(
                fields, spot, (((1,), (1,)), ((), ())), preferred_element_type=jnp.float32
            )
        )
    hits = jnp.concatenate(hits, 0)
    here = jnp.dot(
        hits,
        jnp.concatenate([coords_ref[0, :, p, :] for p in range(2)], 1) * 0.25,
        precision=lax.Precision.HIGHEST,
        preferred_element_type=jnp.float32,
    )
    samples = samples_ref[0].astype(jnp.float32)
    samples = jnp.concatenate([samples[:, p, :] for p in range(2)], 1).astype(jnp.bfloat16)
    values = jnp.dot(hits.astype(jnp.bfloat16), samples, preferred_element_type=jnp.float32)
    for t in range(tile_count):
        for part, block in enumerate((here, values)):
            rows = [
                block[t * pad : t * pad + capacity, q * LANES : (q + 1) * LANES]
                for q in range(2 * pieces)
            ]
            if part == 1:
                rows.append(notes[t])
            packed[part][t] = jnp.concatenate(rows, 0).astype(packed[part].dtype)
    pl.semaphore_wait(barrier, tile_count + epoch_count - 2)

    def tile_copies(k):
        peer = exclusive(me, k, tile_count)
        return [
            pltpu.make_async_remote_copy(
                src_ref=packed[part].at[peer],
                dst_ref=raw[part].at[me],
                send_sem=t_send.at[part, k],
                recv_sem=t_recv.at[part, k],
                device_id={"tile": peer},
                device_id_type=MESH,
            )
            for part in range(2)
        ]

    def epoch_copies(k, j):
        origin = exclusive(me, k, tile_count)
        return [
            pltpu.make_async_remote_copy(
                src_ref=raw[part].at[origin],
                dst_ref=raw[part].at[j * tile_count + origin],
                send_sem=x_send.at[part, (j - 1) * tile_count + k],
                recv_sem=x_recv.at[part, (j - 1) * tile_count + k],
                device_id={"epoch": lax.rem(epoch + j, epoch_count)},
                device_id_type=MESH,
            )
            for part in range(2)
        ]

    def send(i, carry):
        for copy in tile_copies(near_and_far(i, tile_count)):
            copy.start()
        return carry

    lax.fori_loop(0, tile_count - 1, send, 0)
    for part in range(2):
        raw[part][me] = packed[part][me]
    for j in range(1, epoch_count):
        for copy in epoch_copies(0, j):
            copy.start()

    flip = lax.rem(me, 2)
    cells = lax.broadcasted_iota(jnp.int32, (SUB, n_samples), 0)
    cells = jnp.where(flip == 1, SUB - 1 - cells, cells).astype(jnp.float32) * 0.25
    sign = (1 - 2 * flip).astype(jnp.float32)

    def weights(at):
        distance = cells - at
        return jnp.square(jnp.maximum(1.0 - distance * distance, 0.0))

    def make(at):
        points, values = raw[0][at], raw[1][at].astype(jnp.float32)

        def line(block, part, k):
            rows = [(part * pieces + q) * capacity + k for q in range(pieces)]
            return jnp.concatenate([block[row : row + 1] for row in rows], 1)

        for k in range(capacity):
            along_u = weights(line(points, 0, k)).astype(jnp.bfloat16)
            along_v = weights(line(points, 1, k))
            re = line(values, 0, k) * along_v
            im = (line(values, 1, k) * sign) * along_v
            subgrid = lax.dot_general(
                along_u,
                jnp.concatenate([re, im], 0).astype(jnp.bfloat16),
                (((1,), (1,)), ((), ())),
                preferred_element_type=jnp.float32,
            )
            pool_ref[at, k * slot_rows : (k + 1) * slot_rows, :] = jnp.concatenate(
                [subgrid[:slot_rows], subgrid[slot_rows:]], 1
            ).astype(jnp.bfloat16)

    make(me)

    def take(i):
        k = near_and_far(i, tile_count)
        for copy in tile_copies(k):
            copy.wait_recv()
        for j in range(1, epoch_count):
            for copy in epoch_copies(k, j):
                copy.start()
        make(exclusive(me, k, tile_count))

    def take_crossed(i):
        k = jnp.where(i == 0, 0, near_and_far(i - 1, tile_count))
        for j in range(1, epoch_count):
            for copy in epoch_copies(k, j):
                copy.wait_recv()
            make(j * tile_count + exclusive(me, k, tile_count))

    behind = min(BEHIND, tile_count - 1)

    def ahead(i, carry):
        take(i)
        return carry

    def both(i, carry):
        take(i)
        take_crossed(i - behind)
        return carry

    def crossed(i, carry):
        take_crossed(i)
        return carry

    lax.fori_loop(0, behind, ahead, 0)
    lax.fori_loop(behind, tile_count - 1, both, 0)

    rows_here = band // epoch_count
    first_row = (epoch * rows_here - SUB).astype(jnp.float32)
    spots = groups * LANES
    below = lax.broadcasted_iota(jnp.int32, (LANES, LANES), 0) < lax.broadcasted_iota(
        jnp.int32, (LANES, LANES), 1
    )
    below = jnp.where(below, 1.0, 0.0).astype(jnp.bfloat16)
    spot = lax.broadcasted_iota(jnp.int32, (spots, LANES), 0).astype(jnp.float32)
    lanes = lax.broadcasted_iota(jnp.int32, (1, LANES), 1)
    field = lax.broadcasted_iota(jnp.int32, (FIELDS, spots), 0)

    def list_slots(j):
        found, held = jnp.zeros((1, 1), jnp.float32), jnp.zeros((1, 1), jnp.float32)
        gathered = jnp.zeros((EDGE, spots), jnp.float32)
        for g in range(groups):
            total = jnp.zeros((info_rows, LANES), jnp.float32)
            for s in range(g * per_meta, min(tile_count, (g + 1) * per_meta)):
                total += raw[1][j * tile_count + s, info:, :].astype(jnp.float32)
            valid, row = total[0:1], total[1:2] - first_row
            inside = (valid > 0) & (row > 0) & (row < rows_here + SUB)
            mask = jnp.where(inside, 1.0, 0.0)
            order = jnp.dot(
                mask.astype(jnp.bfloat16), below, preferred_element_type=jnp.float32
            )
            chosen = spot == jnp.where(inside, order + found, -1.0)
            source = (g * per_meta + lanes // lane_step).astype(jnp.float32)
            place = (lanes % lane_step).astype(jnp.float32)
            rows = [source, row, total[2:3], total[3:4], place]
            rows = jnp.concatenate(rows + [jnp.zeros_like(row)] * (EDGE - len(rows)), 0)
            gathered += lax.dot_general(
                rows.astype(jnp.bfloat16),
                jnp.where(chosen, 1.0, 0.0).astype(jnp.bfloat16),
                (((1,), (1,)), ((), ())),
                preferred_element_type=jnp.float32,
            )
            found += jnp.sum(mask, 1, keepdims=True)
            held += jnp.sum(valid, 1, keepdims=True)
        listed = jnp.where(field == FIELDS - 1, found, gathered[:FIELDS])
        list_ref[j] = listed.astype(jnp.int32)
        weight_ref[j] = jnp.broadcast_to(1.0 / jnp.maximum(held, 1.0), (FIELDS, LANES))

    list_slots(0)
    lax.fori_loop(tile_count - 1 - behind, tile_count, crossed, 0)
    for j in range(1, epoch_count):
        list_slots(j)

    def finish(k, carry):
        for copy in tile_copies(k):
            copy.wait_send()
        return carry

    lax.fori_loop(1, tile_count, finish, 0)

    def settle(k, carry):
        for j in range(1, epoch_count):
            for copy in epoch_copies(k, j):
                copy.wait_send()
        return carry

    lax.fori_loop(0, tile_count, settle, 0)


def place_kernel(tile_count, list_ref, weight_ref, pool_ref, acc):
    acc_rows = acc.shape[2]
    slot_rows = SUB // 2

    def clear(i, carry):
        acc[0, i] = jnp.zeros((acc_rows, LANES), jnp.float32)
        acc[1, i] = jnp.zeros((acc_rows, LANES), jnp.float32)
        return carry

    lax.fori_loop(0, acc.shape[1], clear, 0)
    lanes = lax.broadcasted_iota(jnp.int32, (slot_rows, LANES), 1)

    for e in range(list_ref.shape[0]):
        weight = jnp.concatenate([weight_ref[e]] * (slot_rows // FIELDS), 0)

        def per_batch(b, carry, e=e, weight=weight):
            placed = []
            for k in range(UNROLL):
                at = b * UNROLL + k
                source, row, block, start, place = (list_ref[e, f, at] for f in range(5))
                first = pl.multiple_of(place * slot_rows, slot_rows)
                data = pool_ref[e * tile_count + source, pl.ds(first, slot_rows), :]
                data = data.astype(jnp.float32) * weight
                turned = [
                    pltpu.roll(data, lax.rem(start + (LANES - i * SUB), LANES), 1)
                    for i in range(4)
                ]
                near = (lanes >= start) & (lanes < start + SUB)
                far = lanes < start + SUB - LANES
                windows = [
                    jnp.concatenate([jnp.where(mask, turned[i], 0.0) for i in (p, 2 + p)], 0)
                    for p in range(2)
                    for mask in (near, far)
                ]
                placed.append((row, block, windows))
            for row, block, windows in placed:
                spots = [(p, block + h, pl.ds(row, SUB)) for p in range(2) for h in range(2)]
                sums = [acc[spot] + window for spot, window in zip(spots, windows)]
                for spot, total in zip(spots, sums):
                    acc[spot] = total
            return carry

        lax.fori_loop(0, (list_ref[e, FIELDS - 1, 0] + UNROLL - 1) // UNROLL, per_batch, 0)


def swap_kernel(
    sizes, cuts, acc_ref, cos_ref, sin_ref, second_ref, last_ref, mixed_ref, here_ref, *scratch
):
    tile_count, epoch_count, band = sizes
    table_sem, scratch = scratch[0], scratch[1:]
    turned, given, landed, folded, full = scratch[:5]
    p_send, p_recv, t_send, t_recv, x_send, x_recv = scratch[5:]
    me, epoch = lax.axis_index("tile"), lax.axis_index("epoch")
    half, kept = tile_count // 2, tile_count // epoch_count
    mine, side = me // 2, lax.rem(me, 2)
    partner = me + 1 - 2 * side
    table_copy = pltpu.make_async_copy(
        last_ref.at[pl.ds(epoch * kept, kept)], here_ref, table_sem.at[0]
    )
    table_copy.start()
    rows_here = band // epoch_count
    cut_rows = rows_here // cuts
    width = min(LANES, band)
    chunks = band // width
    parts = 2 * chunks
    lane_blocks = acc_ref.shape[1] - 1
    group = min(16, cut_rows)
    batch = min(8, half)

    barrier = pltpu.get_barrier_semaphore()

    def greet(k, carry):
        peer = exclusive(mine, k, half) * 2 + side
        pl.semaphore_signal(barrier, inc=1, device_id={"tile": peer}, device_id_type=MESH)
        return carry

    lax.fori_loop(1, half, greet, 0)
    pl.semaphore_signal(barrier, inc=1, device_id={"tile": partner}, device_id_type=MESH)
    for k in range(1, epoch_count):
        peer = lax.rem(epoch + k, epoch_count)
        pl.semaphore_signal(barrier, inc=1, device_id={"epoch": peer}, device_id_type=MESH)

    def rows_of(cut):
        edge = EDGE if cut == cuts - 1 else 0
        return pl.ds(cut * parts * cut_rows, parts * cut_rows + edge)

    def partner_copy(cut, k):
        return pltpu.make_async_remote_copy(
            src_ref=given.at[k, rows_of(cut)],
            dst_ref=landed.at[k, rows_of(cut)],
            send_sem=p_send.at[cut * half + k],
            recv_sem=p_recv.at[cut * half + k],
            device_id={"tile": partner},
            device_id_type=MESH,
        )

    def tile_copy(cut, k):
        return pltpu.make_async_remote_copy(
            src_ref=folded.at[k, rows_of(cut)],
            dst_ref=full.at[epoch * half + mine, rows_of(cut)],
            send_sem=t_send.at[cut * half + k],
            recv_sem=t_recv.at[cut * half + k],
            device_id={"tile": exclusive(mine, k, half) * 2 + side},
            device_id_type=MESH,
        )

    def epoch_copy(cut, k, j):
        origin = epoch * half + exclusive(mine, k, half)
        at = (cut * (epoch_count - 1) + j - 1) * half + k
        return pltpu.make_async_remote_copy(
            src_ref=full.at[origin, rows_of(cut)],
            dst_ref=full.at[origin, rows_of(cut)],
            send_sem=x_send.at[at],
            recv_sem=x_recv.at[at],
            device_id={"epoch": lax.rem(epoch + j, epoch_count)},
            device_id_type=MESH,
        )

    def transform(first, size):
        for h in range(chunks):
            values = []
            for a in range(tile_count):
                col = a * band + h * width
                lane, at = col % LANES, col // LANES
                value = [
                    acc_ref[p, at, pl.ds(SUB + first, size), lane : lane + width] for p in range(2)
                ]
                if col == 0:
                    for p in range(2):
                        value[p] += acc_ref[p, lane_blocks, pl.ds(SUB + first, size), :width]
                values.append(tuple(value))
            lanes = slice(h * width, (h + 1) * width)
            for m, (re, im) in enumerate(dft(values, tile_count)):
                c, s = cos_ref[m : m + 1, lanes], sin_ref[m : m + 1, lanes]
                pair = (re * c - im * s, re * s + im * c)
                for p in range(2):
                    start = p * band + h * width
                    turned[m, pl.ds(first, size), start : start + width] = pair[p].astype(
                        jnp.bfloat16
                    )

    edge_row = lax.broadcasted_iota(jnp.int32, (EDGE, width), 0)
    has_edge = jnp.where(epoch == epoch_count - 1, 1.0, 0.0)

    def sections(cut, tiles):
        rows = cut_rows + (EDGE if cut == cuts - 1 else 0)
        stack = [turned[tile, cut * cut_rows : cut * cut_rows + rows, :] for tile in tiles]
        moved = jnp.dot(
            jnp.concatenate(stack, 0), second_ref[...], preferred_element_type=jnp.float32
        )
        blocks = []
        for i in range(len(tiles)):
            pieces = [
                moved[i * rows : (i + 1) * rows, q * width : (q + 1) * width] for q in range(parts)
            ]
            block = [piece[:cut_rows] for piece in pieces]
            if cut == cuts - 1:
                edge = jnp.zeros((EDGE, width), jnp.float32)
                for q, piece in enumerate(pieces):
                    edge = jnp.where(edge_row == q, piece[cut_rows : cut_rows + 1] * has_edge, edge)
                block.append(edge)
            blocks.append(jnp.concatenate(block, 0))
        return blocks

    def forward(cut, k):
        tile_copy(cut, k).wait_recv()
        for j in range(1, epoch_count):
            epoch_copy(cut, k, j).start()

    order = [0] + [k for pair in zip(range(1, half), range(half // 2, half)) for k in pair]
    order = order[: 1 + 2 * (half // 2 - 1)] + [half - 1] if half > 1 else [0]
    pending = []
    for cut in range(cuts):

        def row_group(i, carry):
            transform(pl.multiple_of(i * group, group), group)
            return carry

        if not pending:
            steps = cut_rows // group
            lax.fori_loop(cut * steps, (cut + 1) * steps, row_group, 0)
        else:
            for i in range(cut_rows // group):
                transform(cut * cut_rows + i * group, group)
                if pending:
                    forward(*pending.pop(0))
        if cut == cuts - 1:
            transform(rows_here, EDGE)
        if cut == 0:
            pl.semaphore_wait(barrier, half + epoch_count - 1)
        for b in range(0, half, batch):
            ks = order[b : b + batch]
            tiles = [exclusive(mine, k, half) * 2 + 1 - side for k in ks]
            for k, block in zip(ks, sections(cut, tiles)):
                given[k, rows_of(cut), :] = block.astype(jnp.bfloat16)
                partner_copy(cut, k).start()
        for b in range(0, half, batch):
            ks = order[b : b + batch]
            tiles = [exclusive(mine, k, half) * 2 + side for k in ks]
            for k, block in zip(ks, sections(cut, tiles)):
                partner_copy(cut, k).wait_recv()
                both = (block + landed[k, rows_of(cut), :].astype(jnp.float32)).astype(jnp.bfloat16)
                if k == 0:
                    full[epoch * half + mine, rows_of(cut), :] = both
                    for j in range(1, epoch_count):
                        epoch_copy(cut, 0, j).start()
                else:
                    folded[k, rows_of(cut), :] = both
                    tile_copy(cut, k).start()
                if cut > 0 and pending:
                    forward(*pending.pop(0))
        pending += [(cut, k) for k in order[1:]]
    def mix_rows(e, cut, first, edges=None):
        for h in range(chunks):
            values = []
            for j in range(half):
                value = tuple(
                    full[
                        e * half + j, pl.ds((cut * parts + h * 2 + p) * cut_rows + first, group), :
                    ].astype(jnp.float32)
                    for p in range(2)
                )
                values.append(epoch_turn(value, j, epoch, epoch_count))
            done = dft(values + [None] * half, kept)
            if edges is not None:
                top = lax.broadcasted_iota(jnp.int32, (group, width), 0) == 0
                done = [
                    tuple(a + jnp.where(top, b, 0.0) for a, b in zip(part, edge))
                    for part, edge in zip(done, edges[h])
                ]
            for c, part in enumerate(done):
                for p in range(2):
                    row = pl.multiple_of(
                        p * band + e * rows_here + cut * cut_rows + first, group
                    )
                    mixed_ref[c, pl.ds(row, group), h * width : (h + 1) * width] = part[p].astype(
                        jnp.bfloat16
                    )

    def mix(e, cut):
        def step(i, carry):
            mix_rows(e, cut, pl.multiple_of(i * group, group))
            return carry

        lax.fori_loop(0, cut_rows // group, step, 0)

    def mix_crossed(cut):
        for j in range(1, epoch_count):

            def arrive(k, carry, j=j):
                epoch_copy(cut, k, j).wait_recv()
                return carry

            lax.fori_loop(0, half, arrive, 0)
            mix(lax.rem(epoch + epoch_count - j, epoch_count), cut)

    for cut in range(cuts):
        for item in pending:
            if item[0] == cut:
                forward(*item)
        mix(epoch, cut)
        if cut > 0:
            mix_crossed(cut - 1)
    mix_crossed(cuts - 1)

    edges = []
    for h in range(chunks):
        values = [None]
        for j in range(half):
            block = full[(epoch_count - 1) * half + j, cuts * parts * cut_rows :, :]
            block = block.astype(jnp.float32)
            value = tuple(block[h * 2 + p : h * 2 + p + 1] for p in range(2))
            values.append(epoch_turn(value, j + 1, epoch, epoch_count))
        edges.append(dft(values + [None] * (tile_count - half - 1), kept))
    mix_rows(0, 0, 0, edges)
    table_copy.wait()

    for cut in range(cuts):

        def finish(k, carry, cut=cut):
            tile_copy(cut, k).wait_send()
            return carry

        lax.fori_loop(1, half, finish, 0)

        def settle(k, carry, cut=cut):
            partner_copy(cut, k).wait_send()
            for j in range(1, epoch_count):
                epoch_copy(cut, k, j).wait_send()
            return carry

        lax.fori_loop(0, half, settle, 0)


def image_kernel(image_scale, mixed_ref, last_ref, rows_ref, cols_ref, out_ref, held, sem):
    kept = held.shape[0]
    tall = jnp.transpose(rows_ref[...]) * image_scale
    copies = [pltpu.make_async_copy(held.at[c], out_ref.at[c], sem.at[c]) for c in range(kept)]
    for c in range(kept):
        pixels = jnp.dot(last_ref[c], mixed_ref[c], preferred_element_type=jnp.float32)
        held[c] = pixels * tall[:, c : c + 1] * cols_ref[...]
        copies[c].start()
    for c in range(kept):
        copies[c].wait()


def turns(product, modulus):
    angles = (product % modulus) * (2.0 * math.pi / modulus)
    return np.cos(angles), np.sin(angles)


def make_tables(tile_count, block_len):
    grid_size = tile_count * block_len
    long_idx = np.arange(block_len)
    tile_idx = np.arange(tile_count)
    turn_cos, turn_sin = turns(tile_idx[:, None] * long_idx[None, :], grid_size)
    c, s = turns(long_idx[:, None] * long_idx[None, :], block_len)
    second = np.stack([np.stack([c, s], 1), np.stack([-s, c], 1)], 0)
    width = min(LANES, block_len)
    second = second.reshape(2 * block_len, 2, block_len // width, width)
    second = second.transpose(0, 2, 1, 3).reshape(2 * block_len, 2 * block_len)
    pixel = long_idx[None, :] * tile_count + tile_idx[:, None]
    c, s = turns(pixel[:, :, None] * long_idx[None, None, :], grid_size)
    last = np.concatenate([c, -s], -1)
    return (
        turn_cos.astype(np.float32),
        turn_sin.astype(np.float32),
        second.astype(jnp.bfloat16),
        last.astype(jnp.bfloat16),
    )


def hbm(count):
    return [pl.BlockSpec(memory_space=pltpu.HBM)] * count


def vmem(count):
    return [pl.BlockSpec(memory_space=pltpu.VMEM)] * count


def body(tables, owners, row_offsets, col_offsets, samples, coords, taper_rows, taper_cols):
    tile_count = lax.axis_size("tile")
    epoch_count = lax.axis_size("epoch")
    n_slots = owners.shape[1]
    n_samples = samples.shape[3]
    capacity = max(2, n_slots * 5 // (4 * tile_count))
    capacity += capacity % 2
    lane_step = max(8, 1 << (capacity - 1).bit_length())
    band = taper_cols.shape[0]
    width = min(LANES, band)
    half, kept = tile_count // 2, tile_count // epoch_count
    rows_here = band // epoch_count
    parts = 2 * (band // width)
    sizes = (tile_count, epoch_count, capacity, band)
    raw_rows = 2 * n_samples // LANES * capacity
    raw_shapes = [
        ((raw_rows, LANES), jnp.float32),
        ((-(-(raw_rows + FIELDS) // EDGE) * EDGE, LANES), jnp.bfloat16),
    ]
    spots = -(-tile_count // (LANES // lane_step)) * LANES

    tile_sems = pltpu.SemaphoreType.DMA((2, tile_count))
    epoch_sems = pltpu.SemaphoreType.DMA((2, (epoch_count - 1) * tile_count))
    pool, slot_list, weights = pl.pallas_call(
        functools.partial(grid_kernel, sizes),
        out_shape=[
            jax.ShapeDtypeStruct(
                (epoch_count * tile_count, capacity * SUB // 2, LANES), jnp.bfloat16
            ),
            jax.ShapeDtypeStruct((epoch_count, FIELDS, spots), jnp.int32),
            jax.ShapeDtypeStruct((epoch_count, FIELDS, LANES), jnp.float32),
        ],
        in_specs=hbm(5),
        out_specs=vmem(3),
        scratch_shapes=[
            *(
                pltpu.VMEM(array.shape, array.dtype)
                for array in (owners, row_offsets, col_offsets, coords, samples)
            ),
            pltpu.SemaphoreType.DMA((5,)),
            *(
                pltpu.VMEM((count, *shape), dtype)
                for count in (tile_count, epoch_count * tile_count)
                for shape, dtype in raw_shapes
            ),
            tile_sems,
            tile_sems,
            epoch_sems,
            epoch_sems,
        ],
        compiler_params=pltpu.CompilerParams(
            vmem_limit_bytes=VMEM_BYTES, collective_id=1, has_side_effects=True
        ),
        name="grid_slots",
    )(
        *(
            pltpu.with_memory_space_constraint(array, pltpu.HBM)
            for array in (owners, row_offsets, col_offsets, coords, samples)
        )
    )

    lane_blocks = tile_count * band // LANES
    acc = pl.pallas_call(
        functools.partial(place_kernel, tile_count),
        out_shape=jax.ShapeDtypeStruct(
            (2, lane_blocks + 1, rows_here + 2 * SUB, LANES), jnp.float32
        ),
        in_specs=[pl.BlockSpec(memory_space=pltpu.SMEM)] + vmem(2),
        out_specs=vmem(1)[0],
        compiler_params=pltpu.CompilerParams(vmem_limit_bytes=VMEM_BYTES),
        name="place_slots",
    )(slot_list, weights, pool)

    cuts = max(1, min(CUTS, rows_here // 16))
    block_shape = (parts * rows_here + EDGE, width)
    sems = [pltpu.SemaphoreType.DMA((cuts * half,))] * 4
    sems += [pltpu.SemaphoreType.DMA((cuts * (epoch_count - 1) * half,))] * 2
    mixed, last_here = pl.pallas_call(
        functools.partial(swap_kernel, (tile_count, epoch_count, band), cuts),
        out_shape=[
            jax.ShapeDtypeStruct((kept, 2 * band, band), jnp.bfloat16),
            jax.ShapeDtypeStruct((kept, band, 2 * band), jnp.bfloat16),
        ],
        in_specs=vmem(4) + hbm(1),
        out_specs=vmem(2),
        scratch_shapes=[
            pltpu.SemaphoreType.DMA((1,)),
            pltpu.VMEM((tile_count, rows_here + EDGE, 2 * band), jnp.bfloat16),
            pltpu.VMEM((half, *block_shape), jnp.bfloat16),
            pltpu.VMEM((half, *block_shape), jnp.bfloat16),
            pltpu.VMEM((half, *block_shape), jnp.bfloat16),
            pltpu.VMEM((epoch_count * half, *block_shape), jnp.bfloat16),
            *sems,
        ],
        compiler_params=pltpu.CompilerParams(
            vmem_limit_bytes=VMEM_BYTES, collective_id=0, has_side_effects=True
        ),
        name="swap_rows",
    )(acc, *(jnp.asarray(table) for table in tables))

    image_scale = math.sqrt(n_slots) / (64.0 * tile_count * math.sqrt(epoch_count))
    return pl.pallas_call(
        functools.partial(image_kernel, image_scale),
        out_shape=jax.ShapeDtypeStruct((kept, band, band), jnp.float32),
        in_specs=vmem(4),
        out_specs=hbm(1)[0],
        scratch_shapes=[
            pltpu.VMEM((kept, band, band), jnp.float32),
            pltpu.SemaphoreType.DMA((kept,)),
        ],
        compiler_params=pltpu.CompilerParams(vmem_limit_bytes=VMEM_BYTES),
        name="image_rows",
    )(mixed, last_here, taper_rows, taper_cols[None, :])


def solution(mesh):
    placed = (
        P("epoch", "tile"),
        P("epoch", "tile"),
        P("epoch", "tile"),
        P("epoch", "tile", None, None),
        P("epoch", "tile", None, None),
        P("epoch", None),
        P("tile"),
    )

    def whole(owners, row_offsets, col_offsets, samples, coords, taper_rows, taper_cols):
        tables = make_tables(mesh.shape["tile"], taper_cols.shape[0] // mesh.shape["tile"])
        return jax.shard_map(
            functools.partial(body, tables),
            mesh=mesh,
            in_specs=placed,
            out_specs=P("epoch", None, "tile"),
            check_vma=False,
        )(owners, row_offsets, col_offsets, samples, coords, taper_rows, taper_cols)

    return whole
```

```python
import functools
import math

import jax
import jax.numpy as jnp
import numpy as np
from jax import lax
from jax.experimental import pallas as pl
from jax.experimental.pallas import tpu as pltpu
from jax.sharding import PartitionSpec as P

SUB = 32
LANES = 128
EDGE = 16
FIELDS = 8
UNROLL = 32
BEHIND = 4
CUTS = (32, 64, 32)
VMEM_BYTES = 24 * 1024 * 1024
MESH = pl.DeviceIdType.MESH


def dft(values, wanted, modulus=None):
    count = len(values)
    if all(v is None for v in values):
        return [None] * wanted
    if count == 1:
        return list(values)
    half = count // 2
    need = min(wanted, half)
    even, odd = dft(values[0::2], need), dft(values[1::2], need)
    low, high = [], []
    for k in range(need):
        e, o = even[k], odd[k]
        t = None if o is None else turn(o, k, count)
        low.append(plus(e, t))
        if half + k < wanted:
            high.append(minus(e, t))
    return low + high


def turn(value, k, count):
    re, im = value
    s = math.sqrt(0.5)
    k %= count
    if k == 0:
        return re, im
    if 2 * k == count:
        return -re, -im
    if 4 * k == count:
        return -im, re
    if 8 * k == count:
        return (re - im) * s, (re + im) * s
    if 8 * k == 3 * count:
        return (re + im) * -s, (re - im) * s
    c, s = math.cos(2 * math.pi * k / count), math.sin(2 * math.pi * k / count)
    return re * c - im * s, re * s + im * c


def plus(a, b):
    if a is None or b is None:
        return b if a is None else a
    return a[0] + b[0], a[1] + b[1]


def minus(a, b):
    if b is None:
        return a
    if a is None:
        return -b[0], -b[1]
    return a[0] - b[0], a[1] - b[1]


def epoch_turn(value, j, epoch, epoch_count):
    angles = [2 * math.pi * ((j * e) % epoch_count) / epoch_count for e in range(epoch_count)]

    def pick(numbers):
        chosen = jnp.float32(numbers[0])
        for e in range(1, epoch_count):
            chosen = jnp.where(epoch == e, jnp.float32(numbers[e]), chosen)
        return chosen

    cos, sin = [round(math.cos(a), 15) for a in angles], [round(math.sin(a), 15) for a in angles]
    re, im = value
    if not any(sin):
        if all(c == 1.0 for c in cos):
            return value
        c = pick(cos)
        return re * c, im * c
    c, s = pick(cos), pick(sin)
    return re * c - im * s, re * s + im * c


def exclusive(a, b, count):
    total = 0
    for bit in range(count.bit_length() - 1):
        x, y = lax.rem(a // (1 << bit), 2), lax.rem(b // (1 << bit), 2)
        total += (x + y - 2 * x * y) * (1 << bit)
    return total


def near_and_far(i, count):
    return jnp.where(
        i == count - 2,
        count - 1,
        jnp.where(lax.rem(i, 2) == 0, 1 + i // 2, count // 2 + i // 2),
    )


def grid_kernel(
    sizes,
    *refs,
):
    tile_count, epoch_count, capacity, band = sizes
    inputs, (pool_ref, list_ref, weight_ref), scratch = refs[:5], refs[5:8], refs[8:]
    owner_ref, row_ref, col_ref, coords_ref, samples_ref, in_sem = scratch[:6]
    packed, raw = scratch[6:8], scratch[8:10]
    t_send, t_recv, x_send, x_recv = scratch[10:]
    fetches = [
        pltpu.make_async_copy(given, held, in_sem.at[i])
        for i, (given, held) in enumerate(zip(inputs, scratch))
    ]
    for fetch in fetches:
        fetch.start()
    me, epoch = lax.axis_index("tile"), lax.axis_index("epoch")
    n_slots = owner_ref.shape[1]
    n_samples = coords_ref.shape[3]
    pieces = n_samples // LANES
    lane_step = max(FIELDS, 1 << (capacity - 1).bit_length())
    pad = -(-capacity // FIELDS) * FIELDS
    info = 2 * pieces * capacity
    info_rows = raw[1].shape[1] - info
    half = tile_count // 2
    per_meta = LANES // lane_step
    groups = -(-tile_count // per_meta)
    slot_rows = SUB // 2

    barrier = pltpu.get_barrier_semaphore()

    def greet(k, carry):
        peer = lax.rem(me + k, tile_count)
        pl.semaphore_signal(barrier, inc=1, device_id={"tile": peer}, device_id_type=MESH)
        return carry

    lax.fori_loop(1, tile_count, greet, 0)
    for k in range(1, epoch_count):
        peer = lax.rem(epoch + k, epoch_count)
        pl.semaphore_signal(barrier, inc=1, device_id={"epoch": peer}, device_id_type=MESH)

    for fetch in fetches:
        fetch.wait()
    owner = owner_ref[...]
    mirrored = owner >= half
    target = jnp.where(mirrored, 2 * (tile_count - 1 - owner) + 1, 2 * owner)
    row = jnp.where(mirrored, band - (SUB - 1) - row_ref[...], row_ref[...])
    col = jnp.where(mirrored, tile_count * band - (SUB - 1) - col_ref[...], col_ref[...])
    mine = lax.broadcasted_iota(jnp.int32, (tile_count, n_slots), 0) == target
    before = lax.broadcasted_iota(jnp.int32, (n_slots, n_slots), 0) < lax.broadcasted_iota(
        jnp.int32, (n_slots, n_slots), 1
    )
    rank = jnp.dot(
        jnp.where(mine, 1.0, 0.0).astype(jnp.bfloat16),
        jnp.where(before, 1.0, 0.0).astype(jnp.bfloat16),
        preferred_element_type=jnp.float32,
    ).astype(jnp.int32)
    key = jnp.where(mine, rank, -LANES)
    fields = [jnp.ones_like(row), row, col // LANES, col % LANES]
    fields = jnp.concatenate(fields + [jnp.zeros_like(row)] * (info_rows - len(fields)), 0)
    fields = fields.astype(jnp.float32).astype(jnp.bfloat16)
    lane = lax.broadcasted_iota(jnp.int32, (LANES, n_slots), 0) - lax.rem(me, per_meta) * lane_step
    first = lax.broadcasted_iota(jnp.int32, (pad, n_slots), 0)
    hits, notes = [], []
    for t in range(tile_count):
        hits.append(jnp.where(key[t : t + 1] == first, 1.0, 0.0))
        spot = jnp.where(key[t : t + 1] == lane, 1.0, 0.0).astype(jnp.bfloat16)
        notes.append(
            lax.dot_general(
                fields, spot, (((1,), (1,)), ((), ())), preferred_element_type=jnp.float32
            )
        )
    hits = jnp.concatenate(hits, 0)
    here = jnp.dot(
        hits,
        jnp.concatenate([coords_ref[0, :, p, :] for p in range(2)], 1) * 0.25,
        precision=lax.Precision.HIGHEST,
        preferred_element_type=jnp.float32,
    )
    samples = samples_ref[0].astype(jnp.float32)
    samples = jnp.concatenate([samples[:, p, :] for p in range(2)], 1).astype(jnp.bfloat16)
    values = jnp.dot(hits.astype(jnp.bfloat16), samples, preferred_element_type=jnp.float32)
    for t in range(tile_count):
        for part, block in enumerate((here, values)):
            rows = [
                block[t * pad : t * pad + capacity, q * LANES : (q + 1) * LANES]
                for q in range(2 * pieces)
            ]
            if part == 1:
                rows.append(notes[t])
            packed[part][t] = jnp.concatenate(rows, 0).astype(packed[part].dtype)
    pl.semaphore_wait(barrier, tile_count + epoch_count - 2)

    def tile_copies(k):
        peer = exclusive(me, k, tile_count)
        return [
            pltpu.make_async_remote_copy(
                src_ref=packed[part].at[peer],
                dst_ref=raw[part].at[me],
                send_sem=t_send.at[part, k],
                recv_sem=t_recv.at[part, k],
                device_id={"tile": peer},
                device_id_type=MESH,
            )
            for part in range(2)
        ]

    def epoch_copies(k, j):
        origin = exclusive(me, k, tile_count)
        return [
            pltpu.make_async_remote_copy(
                src_ref=raw[part].at[origin],
                dst_ref=raw[part].at[j * tile_count + origin],
                send_sem=x_send.at[part, (j - 1) * tile_count + k],
                recv_sem=x_recv.at[part, (j - 1) * tile_count + k],
                device_id={"epoch": lax.rem(epoch + j, epoch_count)},
                device_id_type=MESH,
            )
            for part in range(2)
        ]

    def send(i, carry):
        for copy in tile_copies(near_and_far(i, tile_count)):
            copy.start()
        return carry

    lax.fori_loop(0, tile_count - 1, send, 0)
    for part in range(2):
        raw[part][me] = packed[part][me]
    for j in range(1, epoch_count):
        for copy in epoch_copies(0, j):
            copy.start()

    flip = lax.rem(me, 2)
    cells = lax.broadcasted_iota(jnp.int32, (SUB, n_samples), 0)
    cells = jnp.where(flip == 1, SUB - 1 - cells, cells).astype(jnp.float32) * 0.25
    sign = (1 - 2 * flip).astype(jnp.float32)

    def weights(at):
        distance = cells - at
        return jnp.square(jnp.maximum(1.0 - distance * distance, 0.0))

    def make(at):
        points, values = raw[0][at], raw[1][at].astype(jnp.float32)

        def line(block, part, k):
            rows = [(part * pieces + q) * capacity + k for q in range(pieces)]
            return jnp.concatenate([block[row : row + 1] for row in rows], 1)

        for k in range(capacity):
            along_u = weights(line(points, 0, k)).astype(jnp.bfloat16)
            along_v = weights(line(points, 1, k))
            re = line(values, 0, k) * along_v
            im = (line(values, 1, k) * sign) * along_v
            subgrid = lax.dot_general(
                along_u,
                jnp.concatenate([re, im], 0).astype(jnp.bfloat16),
                (((1,), (1,)), ((), ())),
                preferred_element_type=jnp.float32,
            )
            pool_ref[at, k * slot_rows : (k + 1) * slot_rows, :] = jnp.concatenate(
                [subgrid[:slot_rows], subgrid[slot_rows:]], 1
            ).astype(jnp.bfloat16)

    make(me)

    def take(i):
        k = near_and_far(i, tile_count)
        for copy in tile_copies(k):
            copy.wait_recv()
        for j in range(1, epoch_count):
            for copy in epoch_copies(k, j):
                copy.start()
        make(exclusive(me, k, tile_count))

    def take_crossed(i):
        k = jnp.where(i == 0, 0, near_and_far(i - 1, tile_count))
        for j in range(1, epoch_count):
            for copy in epoch_copies(k, j):
                copy.wait_recv()
            make(j * tile_count + exclusive(me, k, tile_count))

    behind = min(BEHIND, tile_count - 1)

    def ahead(i, carry):
        take(i)
        return carry

    def both(i, carry):
        take(i)
        take_crossed(i - behind)
        return carry

    def crossed(i, carry):
        take_crossed(i)
        return carry

    lax.fori_loop(0, behind, ahead, 0)
    lax.fori_loop(behind, tile_count - 1, both, 0)

    rows_here = band // epoch_count
    first_row = (epoch * rows_here - SUB).astype(jnp.float32)
    spots = groups * LANES
    below = lax.broadcasted_iota(jnp.int32, (LANES, LANES), 0) < lax.broadcasted_iota(
        jnp.int32, (LANES, LANES), 1
    )
    below = jnp.where(below, 1.0, 0.0).astype(jnp.bfloat16)
    spot = lax.broadcasted_iota(jnp.int32, (spots, LANES), 0).astype(jnp.float32)
    lanes = lax.broadcasted_iota(jnp.int32, (1, LANES), 1)
    field = lax.broadcasted_iota(jnp.int32, (FIELDS, spots), 0)

    def list_slots(j):
        held, wide, narrow = (jnp.zeros((1, 1), jnp.float32) for _ in range(3))
        kinds = []
        for g in range(groups):
            total = jnp.zeros((info_rows, LANES), jnp.float32)
            for s in range(g * per_meta, min(tile_count, (g + 1) * per_meta)):
                total += raw[1][j * tile_count + s, info:, :].astype(jnp.float32)
            valid, row, start = total[0:1], total[1:2] - first_row, total[3:4]
            inside = (valid > 0) & (row > 0) & (row < rows_here + SUB)
            masks = [inside & (start > LANES - SUB), inside & (start <= LANES - SUB)]
            flags = jnp.concatenate([jnp.where(mask, 1.0, 0.0) for mask in masks], 0)
            order = jnp.dot(
                flags.astype(jnp.bfloat16), below, preferred_element_type=jnp.float32
            )
            kinds.append((total, row, masks, order, wide, narrow))
            sums = jnp.sum(flags, 1, keepdims=True)
            wide, narrow = wide + sums[0:1], narrow + sums[1:2]
            held += jnp.sum(valid, 1, keepdims=True)
        gathered = jnp.zeros((EDGE, spots), jnp.float32)
        for g, (total, row, masks, order, wide_before, narrow_before) in enumerate(kinds):
            chosen = spot == jnp.where(
                masks[0],
                order[0:1] + wide_before,
                jnp.where(masks[1], order[1:2] + wide + narrow_before, -1.0),
            )
            source = (g * per_meta + lanes // lane_step).astype(jnp.float32)
            place = (lanes % lane_step).astype(jnp.float32)
            rows = [source, row, total[2:3], total[3:4], place]
            rows = jnp.concatenate(rows + [jnp.zeros_like(row)] * (EDGE - len(rows)), 0)
            gathered += lax.dot_general(
                rows.astype(jnp.bfloat16),
                jnp.where(chosen, 1.0, 0.0).astype(jnp.bfloat16),
                (((1,), (1,)), ((), ())),
                preferred_element_type=jnp.float32,
            )
        listed = jnp.where(field == FIELDS - 2, wide, gathered[:FIELDS])
        listed = jnp.where(field == FIELDS - 1, wide + narrow, listed)
        list_ref[j] = listed.astype(jnp.int32)
        weight_ref[j] = jnp.broadcast_to(1.0 / jnp.maximum(held, 1.0), (FIELDS, LANES))

    list_slots(0)
    lax.fori_loop(tile_count - 1 - behind, tile_count, crossed, 0)
    for j in range(1, epoch_count):
        list_slots(j)

    def finish(k, carry):
        for copy in tile_copies(k):
            copy.wait_send()
        return carry

    lax.fori_loop(1, tile_count, finish, 0)

    def settle(k, carry):
        for j in range(1, epoch_count):
            for copy in epoch_copies(k, j):
                copy.wait_send()
        return carry

    lax.fori_loop(0, tile_count, settle, 0)


def place_kernel(tile_count, list_ref, weight_ref, pool_ref, acc):
    acc_rows = acc.shape[2]
    slot_rows = SUB // 2

    def clear(i, carry):
        acc[0, i] = jnp.zeros((acc_rows, LANES), jnp.float32)
        acc[1, i] = jnp.zeros((acc_rows, LANES), jnp.float32)
        return carry

    lax.fori_loop(0, acc.shape[1], clear, 0)
    lanes = lax.broadcasted_iota(jnp.int32, (slot_rows, LANES), 1)

    for e in range(list_ref.shape[0]):
        weight = jnp.concatenate([weight_ref[e]] * (slot_rows // FIELDS), 0)

        def per_batch(b, carry, e=e, weight=weight, blocks=2):
            placed = []
            for k in range(UNROLL):
                at = b * UNROLL + k
                source, row, block, start, place = (list_ref[e, f, at] for f in range(5))
                first = pl.multiple_of(place * slot_rows, slot_rows)
                data = pool_ref[e * tile_count + source, pl.ds(first, slot_rows), :]
                data = data.astype(jnp.float32) * weight
                turned = [
                    pltpu.roll(data, lax.rem(start + (LANES - i * SUB), LANES), 1)
                    for i in range(4)
                ]
                near = (lanes >= start) & (lanes < start + SUB)
                far = lanes < start + SUB - LANES
                windows = [
                    jnp.concatenate([jnp.where(mask, turned[i], 0.0) for i in (p, 2 + p)], 0)
                    for p in range(2)
                    for mask in (near, far)[:blocks]
                ]
                placed.append((row, block, windows))
            for row, block, windows in placed:
                spots = [(p, block + h, pl.ds(row, SUB)) for p in range(2) for h in range(blocks)]
                sums = [acc[spot] + window for spot, window in zip(spots, windows)]
                for spot, total in zip(spots, sums):
                    acc[spot] = total
            return carry

        both = (list_ref[e, FIELDS - 2, 0] + UNROLL - 1) // UNROLL
        last = (list_ref[e, FIELDS - 1, 0] + UNROLL - 1) // UNROLL
        lax.fori_loop(0, both, per_batch, 0)
        lax.fori_loop(both, last, functools.partial(per_batch, blocks=1), 0)


def swap_kernel(
    sizes, spans, acc_ref, cos_ref, sin_ref, second_ref, last_ref, mixed_ref, here_ref, *scratch
):
    tile_count, epoch_count, band = sizes
    table_sem, scratch = scratch[0], scratch[1:]
    turned, given, landed, folded, full = scratch[:5]
    p_send, p_recv, t_send, t_recv, x_send, x_recv = scratch[5:]
    me, epoch = lax.axis_index("tile"), lax.axis_index("epoch")
    half, kept = tile_count // 2, tile_count // epoch_count
    mine, side = me // 2, lax.rem(me, 2)
    partner = me + 1 - 2 * side
    table_copy = pltpu.make_async_copy(
        last_ref.at[pl.ds(epoch * kept, kept)], here_ref, table_sem.at[0]
    )
    table_copy.start()
    rows_here = band // epoch_count
    cuts = len(spans)
    starts = [sum(spans[:cut]) for cut in range(cuts)]
    width = min(LANES, band)
    chunks = band // width
    parts = 2 * chunks
    lane_blocks = acc_ref.shape[1] - 1
    group = min(16, rows_here)
    batch = min(8, half)

    barrier = pltpu.get_barrier_semaphore()

    def greet(k, carry):
        peer = exclusive(mine, k, half) * 2 + side
        pl.semaphore_signal(barrier, inc=1, device_id={"tile": peer}, device_id_type=MESH)
        return carry

    lax.fori_loop(1, half, greet, 0)
    pl.semaphore_signal(barrier, inc=1, device_id={"tile": partner}, device_id_type=MESH)
    for k in range(1, epoch_count):
        peer = lax.rem(epoch + k, epoch_count)
        pl.semaphore_signal(barrier, inc=1, device_id={"epoch": peer}, device_id_type=MESH)

    def rows_of(cut):
        edge = EDGE if cut == cuts - 1 else 0
        return pl.ds(parts * starts[cut], parts * spans[cut] + edge)

    def partner_copy(cut, k):
        return pltpu.make_async_remote_copy(
            src_ref=given.at[k, rows_of(cut)],
            dst_ref=landed.at[k, rows_of(cut)],
            send_sem=p_send.at[cut * half + k],
            recv_sem=p_recv.at[cut * half + k],
            device_id={"tile": partner},
            device_id_type=MESH,
        )

    def tile_copy(cut, k):
        return pltpu.make_async_remote_copy(
            src_ref=folded.at[k, rows_of(cut)],
            dst_ref=full.at[epoch * half + mine, rows_of(cut)],
            send_sem=t_send.at[cut * half + k],
            recv_sem=t_recv.at[cut * half + k],
            device_id={"tile": exclusive(mine, k, half) * 2 + side},
            device_id_type=MESH,
        )

    def epoch_copy(cut, k, j):
        origin = epoch * half + exclusive(mine, k, half)
        at = (cut * (epoch_count - 1) + j - 1) * half + k
        return pltpu.make_async_remote_copy(
            src_ref=full.at[origin, rows_of(cut)],
            dst_ref=full.at[origin, rows_of(cut)],
            send_sem=x_send.at[at],
            recv_sem=x_recv.at[at],
            device_id={"epoch": lax.rem(epoch + j, epoch_count)},
            device_id_type=MESH,
        )

    def transform(first, size):
        for h in range(chunks):
            values = []
            for a in range(tile_count):
                col = a * band + h * width
                lane, at = col % LANES, col // LANES
                value = [
                    acc_ref[p, at, pl.ds(SUB + first, size), lane : lane + width] for p in range(2)
                ]
                if col == 0:
                    for p in range(2):
                        value[p] += acc_ref[p, lane_blocks, pl.ds(SUB + first, size), :width]
                values.append(tuple(value))
            lanes = slice(h * width, (h + 1) * width)
            for m, (re, im) in enumerate(dft(values, tile_count)):
                c, s = cos_ref[m : m + 1, lanes], sin_ref[m : m + 1, lanes]
                pair = (re * c - im * s, re * s + im * c)
                for p in range(2):
                    start = p * band + h * width
                    turned[m, pl.ds(first, size), start : start + width] = pair[p].astype(
                        jnp.bfloat16
                    )

    edge_row = lax.broadcasted_iota(jnp.int32, (EDGE, width), 0)
    has_edge = jnp.where(epoch == epoch_count - 1, 1.0, 0.0)

    def sections(cut, tiles):
        cut_rows = spans[cut]
        rows = cut_rows + (EDGE if cut == cuts - 1 else 0)
        stack = [turned[tile, starts[cut] : starts[cut] + rows, :] for tile in tiles]
        moved = jnp.dot(
            jnp.concatenate(stack, 0), second_ref[...], preferred_element_type=jnp.float32
        )
        blocks = []
        for i in range(len(tiles)):
            pieces = [
                moved[i * rows : (i + 1) * rows, q * width : (q + 1) * width] for q in range(parts)
            ]
            block = [piece[:cut_rows] for piece in pieces]
            if cut == cuts - 1:
                edge = jnp.zeros((EDGE, width), jnp.float32)
                for q, piece in enumerate(pieces):
                    edge = jnp.where(edge_row == q, piece[cut_rows : cut_rows + 1] * has_edge, edge)
                block.append(edge)
            blocks.append(jnp.concatenate(block, 0))
        return blocks

    def forward(cut, k):
        tile_copy(cut, k).wait_recv()
        for j in range(1, epoch_count):
            epoch_copy(cut, k, j).start()

    order = [0] + [k for pair in zip(range(1, half), range(half // 2, half)) for k in pair]
    order = order[: 1 + 2 * (half // 2 - 1)] + [half - 1] if half > 1 else [0]
    nearby = [k for k in order[1:] if 2 * k < half]
    distant = [k for k in order[1:] if 2 * k >= half]
    for cut in range(cuts):

        def row_group(i, carry):
            transform(pl.multiple_of(i * group, group), group)
            return carry

        first = starts[cut] // group
        lax.fori_loop(first, first + spans[cut] // group, row_group, 0)
        if cut == cuts - 1:
            transform(rows_here, EDGE)
        if cut == 0:
            pl.semaphore_wait(barrier, half + epoch_count - 1)
        for b in range(0, half, batch):
            ks = order[b : b + batch]
            tiles = [exclusive(mine, k, half) * 2 + 1 - side for k in ks]
            for k, block in zip(ks, sections(cut, tiles)):
                given[k, rows_of(cut), :] = block.astype(jnp.bfloat16)
                partner_copy(cut, k).start()
        for b in range(0, half, batch):
            ks = order[b : b + batch]
            tiles = [exclusive(mine, k, half) * 2 + side for k in ks]
            for k, block in zip(ks, sections(cut, tiles)):
                partner_copy(cut, k).wait_recv()
                both = (block + landed[k, rows_of(cut), :].astype(jnp.float32)).astype(jnp.bfloat16)
                if k == 0:
                    full[epoch * half + mine, rows_of(cut), :] = both
                    for j in range(1, epoch_count):
                        epoch_copy(cut, 0, j).start()
                else:
                    folded[k, rows_of(cut), :] = both
                    tile_copy(cut, k).start()
        if cut > 0:
            for k in nearby:
                forward(cut - 1, k)
    def mix_rows(e, cut, first, edges=None):
        for h in range(chunks):
            values = []
            for j in range(half):
                value = tuple(
                    full[
                        e * half + j,
                        pl.ds(parts * starts[cut] + (h * 2 + p) * spans[cut] + first, group),
                        :,
                    ].astype(jnp.float32)
                    for p in range(2)
                )
                values.append(epoch_turn(value, j, epoch, epoch_count))
            done = dft(values + [None] * half, kept)
            if edges is not None:
                top = lax.broadcasted_iota(jnp.int32, (group, width), 0) == 0
                done = [
                    tuple(a + jnp.where(top, b, 0.0) for a, b in zip(part, edge))
                    for part, edge in zip(done, edges[h])
                ]
            for c, part in enumerate(done):
                for p in range(2):
                    row = pl.multiple_of(
                        p * band + e * rows_here + starts[cut] + first, group
                    )
                    mixed_ref[c, pl.ds(row, group), h * width : (h + 1) * width] = part[p].astype(
                        jnp.bfloat16
                    )

    def mix(e, cut):
        def step(i, carry):
            mix_rows(e, cut, pl.multiple_of(i * group, group))
            return carry

        lax.fori_loop(0, spans[cut] // group, step, 0)

    def mix_crossed(cut):
        for j in range(1, epoch_count):

            def arrive(k, carry, j=j):
                epoch_copy(cut, k, j).wait_recv()
                return carry

            lax.fori_loop(0, half, arrive, 0)
            mix(lax.rem(epoch + epoch_count - j, epoch_count), cut)

    for cut in range(cuts):
        for k in distant:
            forward(cut, k)
        if cut == 0:
            for k in nearby:
                forward(cuts - 1, k)
        mix(epoch, cut)
        if cut > 0:
            mix_crossed(cut - 1)
    mix_crossed(cuts - 1)

    edges = []
    for h in range(chunks):
        values = [None]
        for j in range(half):
            block = full[(epoch_count - 1) * half + j, parts * rows_here :, :]
            block = block.astype(jnp.float32)
            value = tuple(block[h * 2 + p : h * 2 + p + 1] for p in range(2))
            values.append(epoch_turn(value, j + 1, epoch, epoch_count))
        edges.append(dft(values + [None] * (tile_count - half - 1), kept))
    mix_rows(0, 0, 0, edges)
    table_copy.wait()

    for cut in range(cuts):

        def finish(k, carry, cut=cut):
            tile_copy(cut, k).wait_send()
            return carry

        lax.fori_loop(1, half, finish, 0)

        def settle(k, carry, cut=cut):
            partner_copy(cut, k).wait_send()
            for j in range(1, epoch_count):
                epoch_copy(cut, k, j).wait_send()
            return carry

        lax.fori_loop(0, half, settle, 0)


def image_kernel(image_scale, mixed_ref, last_ref, rows_ref, cols_ref, out_ref, held, sem):
    kept = held.shape[0]
    tall = jnp.transpose(rows_ref[...]) * image_scale
    copies = [pltpu.make_async_copy(held.at[c], out_ref.at[c], sem.at[c]) for c in range(kept)]
    for c in range(kept):
        pixels = jnp.dot(last_ref[c], mixed_ref[c], preferred_element_type=jnp.float32)
        held[c] = pixels * tall[:, c : c + 1] * cols_ref[...]
        copies[c].start()
    for c in range(kept):
        copies[c].wait()


def turns(product, modulus):
    angles = (product % modulus) * (2.0 * math.pi / modulus)
    return np.cos(angles), np.sin(angles)


def make_tables(tile_count, block_len):
    grid_size = tile_count * block_len
    long_idx = np.arange(block_len)
    tile_idx = np.arange(tile_count)
    turn_cos, turn_sin = turns(tile_idx[:, None] * long_idx[None, :], grid_size)
    c, s = turns(long_idx[:, None] * long_idx[None, :], block_len)
    second = np.stack([np.stack([c, s], 1), np.stack([-s, c], 1)], 0)
    width = min(LANES, block_len)
    second = second.reshape(2 * block_len, 2, block_len // width, width)
    second = second.transpose(0, 2, 1, 3).reshape(2 * block_len, 2 * block_len)
    pixel = long_idx[None, :] * tile_count + tile_idx[:, None]
    c, s = turns(pixel[:, :, None] * long_idx[None, None, :], grid_size)
    last = np.concatenate([c, -s], -1)
    return (
        turn_cos.astype(np.float32),
        turn_sin.astype(np.float32),
        second.astype(jnp.bfloat16),
        last.astype(jnp.bfloat16),
    )


def hbm(count):
    return [pl.BlockSpec(memory_space=pltpu.HBM)] * count


def vmem(count):
    return [pl.BlockSpec(memory_space=pltpu.VMEM)] * count


def body(tables, owners, row_offsets, col_offsets, samples, coords, taper_rows, taper_cols):
    tile_count = lax.axis_size("tile")
    epoch_count = lax.axis_size("epoch")
    n_slots = owners.shape[1]
    n_samples = samples.shape[3]
    capacity = max(2, n_slots * 5 // (4 * tile_count))
    capacity += capacity % 2
    lane_step = max(8, 1 << (capacity - 1).bit_length())
    band = taper_cols.shape[0]
    width = min(LANES, band)
    half, kept = tile_count // 2, tile_count // epoch_count
    rows_here = band // epoch_count
    parts = 2 * (band // width)
    sizes = (tile_count, epoch_count, capacity, band)
    raw_rows = 2 * n_samples // LANES * capacity
    raw_shapes = [
        ((raw_rows, LANES), jnp.float32),
        ((-(-(raw_rows + FIELDS) // EDGE) * EDGE, LANES), jnp.bfloat16),
    ]
    spots = -(-tile_count // (LANES // lane_step)) * LANES

    tile_sems = pltpu.SemaphoreType.DMA((2, tile_count))
    epoch_sems = pltpu.SemaphoreType.DMA((2, (epoch_count - 1) * tile_count))
    pool, slot_list, weights = pl.pallas_call(
        functools.partial(grid_kernel, sizes),
        out_shape=[
            jax.ShapeDtypeStruct(
                (epoch_count * tile_count, capacity * SUB // 2, LANES), jnp.bfloat16
            ),
            jax.ShapeDtypeStruct((epoch_count, FIELDS, spots), jnp.int32),
            jax.ShapeDtypeStruct((epoch_count, FIELDS, LANES), jnp.float32),
        ],
        in_specs=hbm(5),
        out_specs=vmem(3),
        scratch_shapes=[
            *(
                pltpu.VMEM(array.shape, array.dtype)
                for array in (owners, row_offsets, col_offsets, coords, samples)
            ),
            pltpu.SemaphoreType.DMA((5,)),
            *(
                pltpu.VMEM((count, *shape), dtype)
                for count in (tile_count, epoch_count * tile_count)
                for shape, dtype in raw_shapes
            ),
            tile_sems,
            tile_sems,
            epoch_sems,
            epoch_sems,
        ],
        compiler_params=pltpu.CompilerParams(
            vmem_limit_bytes=VMEM_BYTES, collective_id=1, has_side_effects=True
        ),
        name="grid_slots",
    )(
        *(
            pltpu.with_memory_space_constraint(array, pltpu.HBM)
            for array in (owners, row_offsets, col_offsets, coords, samples)
        )
    )

    lane_blocks = tile_count * band // LANES
    acc = pl.pallas_call(
        functools.partial(place_kernel, tile_count),
        out_shape=jax.ShapeDtypeStruct(
            (2, lane_blocks + 1, rows_here + 2 * SUB, LANES), jnp.float32
        ),
        in_specs=[pl.BlockSpec(memory_space=pltpu.SMEM)] + vmem(2),
        out_specs=vmem(1)[0],
        compiler_params=pltpu.CompilerParams(vmem_limit_bytes=VMEM_BYTES),
        name="place_slots",
    )(slot_list, weights, pool)

    groups = [rows_here * share // 128 for share in CUTS]
    spans = groups if all(span % 16 == 0 for span in groups) else [rows_here]
    cuts = len(spans)
    block_shape = (parts * rows_here + EDGE, width)
    sems = [pltpu.SemaphoreType.DMA((cuts * half,))] * 4
    sems += [pltpu.SemaphoreType.DMA((cuts * (epoch_count - 1) * half,))] * 2
    mixed, last_here = pl.pallas_call(
        functools.partial(swap_kernel, (tile_count, epoch_count, band), spans),
        out_shape=[
            jax.ShapeDtypeStruct((kept, 2 * band, band), jnp.bfloat16),
            jax.ShapeDtypeStruct((kept, band, 2 * band), jnp.bfloat16),
        ],
        in_specs=vmem(4) + hbm(1),
        out_specs=vmem(2),
        scratch_shapes=[
            pltpu.SemaphoreType.DMA((1,)),
            pltpu.VMEM((tile_count, rows_here + EDGE, 2 * band), jnp.bfloat16),
            pltpu.VMEM((half, *block_shape), jnp.bfloat16),
            pltpu.VMEM((half, *block_shape), jnp.bfloat16),
            pltpu.VMEM((half, *block_shape), jnp.bfloat16),
            pltpu.VMEM((epoch_count * half, *block_shape), jnp.bfloat16),
            *sems,
        ],
        compiler_params=pltpu.CompilerParams(
            vmem_limit_bytes=VMEM_BYTES, collective_id=0, has_side_effects=True
        ),
        name="swap_rows",
    )(acc, *(jnp.asarray(table) for table in tables))

    image_scale = math.sqrt(n_slots) / (64.0 * tile_count * math.sqrt(epoch_count))
    return pl.pallas_call(
        functools.partial(image_kernel, image_scale),
        out_shape=jax.ShapeDtypeStruct((kept, band, band), jnp.float32),
        in_specs=vmem(4),
        out_specs=hbm(1)[0],
        scratch_shapes=[
            pltpu.VMEM((kept, band, band), jnp.float32),
            pltpu.SemaphoreType.DMA((kept,)),
        ],
        compiler_params=pltpu.CompilerParams(vmem_limit_bytes=VMEM_BYTES),
        name="image_rows",
    )(mixed, last_here, taper_rows, taper_cols[None, :])


def solution(mesh):
    placed = (
        P("epoch", "tile"),
        P("epoch", "tile"),
        P("epoch", "tile"),
        P("epoch", "tile", None, None),
        P("epoch", "tile", None, None),
        P("epoch", None),
        P("tile"),
    )

    def whole(owners, row_offsets, col_offsets, samples, coords, taper_rows, taper_cols):
        tables = make_tables(mesh.shape["tile"], taper_cols.shape[0] // mesh.shape["tile"])
        return jax.shard_map(
            functools.partial(body, tables),
            mesh=mesh,
            in_specs=placed,
            out_specs=P("epoch", None, "tile"),
            check_vma=False,
        )(owners, row_offsets, col_offsets, samples, coords, taper_rows, taper_cols)

    return whole
```

```python
import functools
import math

import jax
import jax.numpy as jnp
import numpy as np
from jax import lax
from jax.experimental import pallas as pl
from jax.experimental.pallas import tpu as pltpu
from jax.sharding import PartitionSpec as P

SUB = 32
LANES = 128
EDGE = 16
FIELDS = 8
UNROLL = 32
BEHIND = 4
CUTS = (32, 64, 32)
VMEM_BYTES = 24 * 1024 * 1024
MESH = pl.DeviceIdType.MESH


def dft(values, wanted, modulus=None):
    count = len(values)
    if all(v is None for v in values):
        return [None] * wanted
    if count == 1:
        return list(values)
    half = count // 2
    need = min(wanted, half)
    even, odd = dft(values[0::2], need), dft(values[1::2], need)
    low, high = [], []
    for k in range(need):
        e, o = even[k], odd[k]
        t = None if o is None else turn(o, k, count)
        low.append(plus(e, t))
        if half + k < wanted:
            high.append(minus(e, t))
    return low + high


def turn(value, k, count):
    re, im = value
    s = math.sqrt(0.5)
    k %= count
    if k == 0:
        return re, im
    if 2 * k == count:
        return -re, -im
    if 4 * k == count:
        return -im, re
    if 8 * k == count:
        return (re - im) * s, (re + im) * s
    if 8 * k == 3 * count:
        return (re + im) * -s, (re - im) * s
    c, s = math.cos(2 * math.pi * k / count), math.sin(2 * math.pi * k / count)
    return re * c - im * s, re * s + im * c


def plus(a, b):
    if a is None or b is None:
        return b if a is None else a
    return a[0] + b[0], a[1] + b[1]


def minus(a, b):
    if b is None:
        return a
    if a is None:
        return -b[0], -b[1]
    return a[0] - b[0], a[1] - b[1]


def epoch_turn(value, j, epoch, epoch_count):
    angles = [2 * math.pi * ((j * e) % epoch_count) / epoch_count for e in range(epoch_count)]

    def pick(numbers):
        chosen = jnp.float32(numbers[0])
        for e in range(1, epoch_count):
            chosen = jnp.where(epoch == e, jnp.float32(numbers[e]), chosen)
        return chosen

    cos, sin = [round(math.cos(a), 15) for a in angles], [round(math.sin(a), 15) for a in angles]
    re, im = value
    if not any(sin):
        if all(c == 1.0 for c in cos):
            return value
        c = pick(cos)
        return re * c, im * c
    c, s = pick(cos), pick(sin)
    return re * c - im * s, re * s + im * c


def exclusive(a, b, count):
    total = 0
    for bit in range(count.bit_length() - 1):
        x, y = lax.rem(a // (1 << bit), 2), lax.rem(b // (1 << bit), 2)
        total += (x + y - 2 * x * y) * (1 << bit)
    return total


def grid_kernel(
    sizes,
    *refs,
):
    tile_count, epoch_count, capacity, band = sizes
    inputs, (pool_ref, list_ref, weight_ref), scratch = refs[:5], refs[5:8], refs[8:]
    owner_ref, row_ref, col_ref, coords_ref, samples_ref, in_sem = scratch[:6]
    packed, raw = scratch[6:8], scratch[8:10]
    t_send, t_recv, x_send, x_recv = scratch[10:]
    fetches = [
        pltpu.make_async_copy(given, held, in_sem.at[i])
        for i, (given, held) in enumerate(zip(inputs, scratch))
    ]
    for fetch in fetches:
        fetch.start()
    me, epoch = lax.axis_index("tile"), lax.axis_index("epoch")
    n_slots = owner_ref.shape[1]
    n_samples = coords_ref.shape[3]
    pieces = n_samples // LANES
    lane_step = max(FIELDS, 1 << (capacity - 1).bit_length())
    pad = -(-capacity // FIELDS) * FIELDS
    info = 2 * pieces * capacity
    info_rows = raw[1].shape[1] - info
    half = tile_count // 2
    per_meta = LANES // lane_step
    groups = -(-tile_count // per_meta)
    slot_rows = SUB // 2

    barrier = pltpu.get_barrier_semaphore()

    def greet(k, carry):
        peer = lax.rem(me + k, tile_count)
        pl.semaphore_signal(barrier, inc=1, device_id={"tile": peer}, device_id_type=MESH)
        return carry

    lax.fori_loop(1, tile_count, greet, 0)
    for k in range(1, epoch_count):
        peer = lax.rem(epoch + k, epoch_count)
        pl.semaphore_signal(barrier, inc=1, device_id={"epoch": peer}, device_id_type=MESH)

    for fetch in fetches:
        fetch.wait()
    owner = owner_ref[...]
    mirrored = owner >= half
    target = jnp.where(mirrored, 2 * (tile_count - 1 - owner) + 1, 2 * owner)
    row = jnp.where(mirrored, band - (SUB - 1) - row_ref[...], row_ref[...])
    col = jnp.where(mirrored, tile_count * band - (SUB - 1) - col_ref[...], col_ref[...])
    mine = lax.broadcasted_iota(jnp.int32, (tile_count, n_slots), 0) == target
    before = lax.broadcasted_iota(jnp.int32, (n_slots, n_slots), 0) < lax.broadcasted_iota(
        jnp.int32, (n_slots, n_slots), 1
    )
    rank = jnp.dot(
        jnp.where(mine, 1.0, 0.0).astype(jnp.bfloat16),
        jnp.where(before, 1.0, 0.0).astype(jnp.bfloat16),
        preferred_element_type=jnp.float32,
    ).astype(jnp.int32)
    key = jnp.where(mine, rank, -LANES)
    fields = [jnp.ones_like(row), row, col // LANES, col % LANES]
    fields = jnp.concatenate(fields + [jnp.zeros_like(row)] * (info_rows - len(fields)), 0)
    fields = fields.astype(jnp.float32).astype(jnp.bfloat16)
    lane = lax.broadcasted_iota(jnp.int32, (LANES, n_slots), 0) - lax.rem(me, per_meta) * lane_step
    first = lax.broadcasted_iota(jnp.int32, (pad, n_slots), 0)
    hits, notes = [], []
    for t in range(tile_count):
        hits.append(jnp.where(key[t : t + 1] == first, 1.0, 0.0))
        spot = jnp.where(key[t : t + 1] == lane, 1.0, 0.0).astype(jnp.bfloat16)
        notes.append(
            lax.dot_general(
                fields, spot, (((1,), (1,)), ((), ())), preferred_element_type=jnp.float32
            )
        )
    hits = jnp.concatenate(hits, 0)
    here = jnp.dot(
        hits,
        jnp.concatenate([coords_ref[0, :, p, :] for p in range(2)], 1) * 0.25,
        precision=lax.Precision.HIGHEST,
        preferred_element_type=jnp.float32,
    )
    samples = samples_ref[0].astype(jnp.float32)
    samples = jnp.concatenate([samples[:, p, :] for p in range(2)], 1).astype(jnp.bfloat16)
    values = jnp.dot(hits.astype(jnp.bfloat16), samples, preferred_element_type=jnp.float32)
    for t in range(tile_count):
        for part, block in enumerate((here, values)):
            rows = [
                block[t * pad : t * pad + capacity, q * LANES : (q + 1) * LANES]
                for q in range(2 * pieces)
            ]
            if part == 1:
                rows.append(notes[t])
            packed[part][t] = jnp.concatenate(rows, 0).astype(packed[part].dtype)
    pl.semaphore_wait(barrier, tile_count + epoch_count - 2)

    def tile_copies(k):
        peer = exclusive(me, k, tile_count)
        return [
            pltpu.make_async_remote_copy(
                src_ref=packed[part].at[peer],
                dst_ref=raw[part].at[me],
                send_sem=t_send.at[part, k],
                recv_sem=t_recv.at[part, k],
                device_id={"tile": peer},
                device_id_type=MESH,
            )
            for part in range(2)
        ]

    def epoch_copies(k, j):
        origin = exclusive(me, k, tile_count)
        return [
            pltpu.make_async_remote_copy(
                src_ref=raw[part].at[origin],
                dst_ref=raw[part].at[j * tile_count + origin],
                send_sem=x_send.at[part, (j - 1) * tile_count + k],
                recv_sem=x_recv.at[part, (j - 1) * tile_count + k],
                device_id={"epoch": lax.rem(epoch + j, epoch_count)},
                device_id_type=MESH,
            )
            for part in range(2)
        ]

    def send(k, carry):
        for copy in tile_copies(k):
            copy.start()
        return carry

    lax.fori_loop(1, tile_count, send, 0)
    for part in range(2):
        raw[part][me] = packed[part][me]
    for j in range(1, epoch_count):
        for copy in epoch_copies(0, j):
            copy.start()

    flip = lax.rem(me, 2)
    cells = lax.broadcasted_iota(jnp.int32, (SUB, n_samples), 0)
    cells = jnp.where(flip == 1, SUB - 1 - cells, cells).astype(jnp.float32) * 0.25
    sign = (1 - 2 * flip).astype(jnp.float32)

    def weights(at):
        distance = cells - at
        return jnp.square(jnp.maximum(1.0 - distance * distance, 0.0))

    def make(at):
        points, values = raw[0][at], raw[1][at].astype(jnp.float32)

        def line(block, part, k):
            rows = [(part * pieces + q) * capacity + k for q in range(pieces)]
            return jnp.concatenate([block[row : row + 1] for row in rows], 1)

        for k in range(capacity):
            along_u = weights(line(points, 0, k)).astype(jnp.bfloat16)
            along_v = weights(line(points, 1, k))
            re = line(values, 0, k) * along_v
            im = (line(values, 1, k) * sign) * along_v
            subgrid = lax.dot_general(
                along_u,
                jnp.concatenate([re, im], 0).astype(jnp.bfloat16),
                (((1,), (1,)), ((), ())),
                preferred_element_type=jnp.float32,
            )
            pool_ref[at, k * slot_rows : (k + 1) * slot_rows, :] = jnp.concatenate(
                [subgrid[:slot_rows], subgrid[slot_rows:]], 1
            ).astype(jnp.bfloat16)

    make(me)

    def take(k):
        for copy in tile_copies(k):
            copy.wait_recv()
        for j in range(1, epoch_count):
            for copy in epoch_copies(k, j):
                copy.start()
        make(exclusive(me, k, tile_count))

    def take_crossed(k):
        for j in range(1, epoch_count):
            for copy in epoch_copies(k, j):
                copy.wait_recv()
            make(j * tile_count + exclusive(me, k, tile_count))

    behind = min(BEHIND, tile_count - 1)

    def ahead(k, carry):
        take(k)
        return carry

    def both(k, carry):
        take(k)
        take_crossed(k - 1 - behind)
        return carry

    def crossed(k, carry):
        take_crossed(k)
        return carry

    lax.fori_loop(1, 1 + behind, ahead, 0)
    lax.fori_loop(1 + behind, tile_count, both, 0)

    rows_here = band // epoch_count
    first_row = (epoch * rows_here - SUB).astype(jnp.float32)
    spots = groups * LANES
    below = lax.broadcasted_iota(jnp.int32, (LANES, LANES), 0) < lax.broadcasted_iota(
        jnp.int32, (LANES, LANES), 1
    )
    below = jnp.where(below, 1.0, 0.0).astype(jnp.bfloat16)
    spot = lax.broadcasted_iota(jnp.int32, (spots, LANES), 0).astype(jnp.float32)
    lanes = lax.broadcasted_iota(jnp.int32, (1, LANES), 1)
    field = lax.broadcasted_iota(jnp.int32, (FIELDS, spots), 0)

    def list_slots(j):
        held, wide, narrow = (jnp.zeros((1, 1), jnp.float32) for _ in range(3))
        kinds = []
        for g in range(groups):
            total = jnp.zeros((info_rows, LANES), jnp.float32)
            for s in range(g * per_meta, min(tile_count, (g + 1) * per_meta)):
                total += raw[1][j * tile_count + s, info:, :].astype(jnp.float32)
            valid, row, start = total[0:1], total[1:2] - first_row, total[3:4]
            inside = (valid > 0) & (row > 0) & (row < rows_here + SUB)
            masks = [inside & (start > LANES - SUB), inside & (start <= LANES - SUB)]
            flags = jnp.concatenate([jnp.where(mask, 1.0, 0.0) for mask in masks], 0)
            order = jnp.dot(
                flags.astype(jnp.bfloat16), below, preferred_element_type=jnp.float32
            )
            kinds.append((total, row, masks, order, wide, narrow))
            sums = jnp.sum(flags, 1, keepdims=True)
            wide, narrow = wide + sums[0:1], narrow + sums[1:2]
            held += jnp.sum(valid, 1, keepdims=True)
        gathered = jnp.zeros((EDGE, spots), jnp.float32)
        for g, (total, row, masks, order, wide_before, narrow_before) in enumerate(kinds):
            chosen = spot == jnp.where(
                masks[0],
                order[0:1] + wide_before,
                jnp.where(masks[1], order[1:2] + wide + narrow_before, -1.0),
            )
            source = (g * per_meta + lanes // lane_step).astype(jnp.float32)
            place = (lanes % lane_step).astype(jnp.float32)
            rows = [source, row, total[2:3], total[3:4], place]
            rows = jnp.concatenate(rows + [jnp.zeros_like(row)] * (EDGE - len(rows)), 0)
            gathered += lax.dot_general(
                rows.astype(jnp.bfloat16),
                jnp.where(chosen, 1.0, 0.0).astype(jnp.bfloat16),
                (((1,), (1,)), ((), ())),
                preferred_element_type=jnp.float32,
            )
        listed = jnp.where(field == FIELDS - 2, wide, gathered[:FIELDS])
        listed = jnp.where(field == FIELDS - 1, wide + narrow, listed)
        list_ref[j] = listed.astype(jnp.int32)
        weight_ref[j] = jnp.broadcast_to(1.0 / jnp.maximum(held, 1.0), (FIELDS, LANES))

    list_slots(0)
    lax.fori_loop(tile_count - 1 - behind, tile_count, crossed, 0)
    for j in range(1, epoch_count):
        list_slots(j)

    def finish(k, carry):
        for copy in tile_copies(k):
            copy.wait_send()
        return carry

    lax.fori_loop(1, tile_count, finish, 0)

    def settle(k, carry):
        for j in range(1, epoch_count):
            for copy in epoch_copies(k, j):
                copy.wait_send()
        return carry

    lax.fori_loop(0, tile_count, settle, 0)


def place_kernel(tile_count, list_ref, weight_ref, pool_ref, acc):
    acc_rows = acc.shape[2]
    slot_rows = SUB // 2

    def clear(i, carry):
        acc[0, i] = jnp.zeros((acc_rows, LANES), jnp.float32)
        acc[1, i] = jnp.zeros((acc_rows, LANES), jnp.float32)
        return carry

    lax.fori_loop(0, acc.shape[1], clear, 0)
    lanes = lax.broadcasted_iota(jnp.int32, (slot_rows, LANES), 1)

    for e in range(list_ref.shape[0]):
        weight = jnp.concatenate([weight_ref[e]] * (slot_rows // FIELDS), 0)

        def per_batch(b, carry, e=e, weight=weight, blocks=2):
            placed = []
            for k in range(UNROLL):
                at = b * UNROLL + k
                source, row, block, start, place = (list_ref[e, f, at] for f in range(5))
                first = pl.multiple_of(place * slot_rows, slot_rows)
                data = pool_ref[e * tile_count + source, pl.ds(first, slot_rows), :]
                data = data.astype(jnp.float32) * weight
                turned = [
                    pltpu.roll(data, lax.rem(start + (LANES - i * SUB), LANES), 1)
                    for i in range(4)
                ]
                near = (lanes >= start) & (lanes < start + SUB)
                far = lanes < start + SUB - LANES
                windows = [
                    jnp.concatenate([jnp.where(mask, turned[i], 0.0) for i in (p, 2 + p)], 0)
                    for p in range(2)
                    for mask in (near, far)[:blocks]
                ]
                placed.append((row, block, windows))
            for row, block, windows in placed:
                spots = [(p, block + h, pl.ds(row, SUB)) for p in range(2) for h in range(blocks)]
                sums = [acc[spot] + window for spot, window in zip(spots, windows)]
                for spot, total in zip(spots, sums):
                    acc[spot] = total
            return carry

        both = (list_ref[e, FIELDS - 2, 0] + UNROLL - 1) // UNROLL
        last = (list_ref[e, FIELDS - 1, 0] + UNROLL - 1) // UNROLL
        lax.fori_loop(0, both, per_batch, 0)
        lax.fori_loop(both, last, functools.partial(per_batch, blocks=1), 0)


def swap_kernel(
    sizes, spans, acc_ref, cos_ref, sin_ref, second_ref, last_ref, mixed_ref, here_ref, *scratch
):
    tile_count, epoch_count, band = sizes
    table_sem, scratch = scratch[0], scratch[1:]
    turned, given, landed, folded, full = scratch[:5]
    p_send, p_recv, t_send, t_recv, x_send, x_recv = scratch[5:]
    me, epoch = lax.axis_index("tile"), lax.axis_index("epoch")
    half, kept = tile_count // 2, tile_count // epoch_count
    mine, side = me // 2, lax.rem(me, 2)
    partner = me + 1 - 2 * side
    table_copy = pltpu.make_async_copy(
        last_ref.at[pl.ds(epoch * kept, kept)], here_ref, table_sem.at[0]
    )
    table_copy.start()
    rows_here = band // epoch_count
    cuts = len(spans)
    starts = [sum(spans[:cut]) for cut in range(cuts)]
    width = min(LANES, band)
    chunks = band // width
    parts = 2 * chunks
    lane_blocks = acc_ref.shape[1] - 1
    group = min(16, rows_here)
    batch = min(8, half)

    barrier = pltpu.get_barrier_semaphore()

    def greet(k, carry):
        peer = exclusive(mine, k, half) * 2 + side
        pl.semaphore_signal(barrier, inc=1, device_id={"tile": peer}, device_id_type=MESH)
        return carry

    lax.fori_loop(1, half, greet, 0)
    pl.semaphore_signal(barrier, inc=1, device_id={"tile": partner}, device_id_type=MESH)
    for k in range(1, epoch_count):
        peer = lax.rem(epoch + k, epoch_count)
        pl.semaphore_signal(barrier, inc=1, device_id={"epoch": peer}, device_id_type=MESH)

    def rows_of(cut):
        edge = EDGE if cut == cuts - 1 else 0
        return pl.ds(parts * starts[cut], parts * spans[cut] + edge)

    def partner_copy(cut, k):
        return pltpu.make_async_remote_copy(
            src_ref=given.at[k, rows_of(cut)],
            dst_ref=landed.at[k, rows_of(cut)],
            send_sem=p_send.at[cut * half + k],
            recv_sem=p_recv.at[cut * half + k],
            device_id={"tile": partner},
            device_id_type=MESH,
        )

    def tile_copy(cut, k):
        return pltpu.make_async_remote_copy(
            src_ref=folded.at[k, rows_of(cut)],
            dst_ref=full.at[epoch * half + mine, rows_of(cut)],
            send_sem=t_send.at[cut * half + k],
            recv_sem=t_recv.at[cut * half + k],
            device_id={"tile": exclusive(mine, k, half) * 2 + side},
            device_id_type=MESH,
        )

    def epoch_copy(cut, k, j):
        origin = epoch * half + exclusive(mine, k, half)
        at = (cut * (epoch_count - 1) + j - 1) * half + k
        return pltpu.make_async_remote_copy(
            src_ref=full.at[origin, rows_of(cut)],
            dst_ref=full.at[origin, rows_of(cut)],
            send_sem=x_send.at[at],
            recv_sem=x_recv.at[at],
            device_id={"epoch": lax.rem(epoch + j, epoch_count)},
            device_id_type=MESH,
        )

    def transform(first, size):
        for h in range(chunks):
            values = []
            for a in range(tile_count):
                col = a * band + h * width
                lane, at = col % LANES, col // LANES
                value = [
                    acc_ref[p, at, pl.ds(SUB + first, size), lane : lane + width] for p in range(2)
                ]
                if col == 0:
                    for p in range(2):
                        value[p] += acc_ref[p, lane_blocks, pl.ds(SUB + first, size), :width]
                values.append(tuple(value))
            lanes = slice(h * width, (h + 1) * width)
            for m, (re, im) in enumerate(dft(values, tile_count)):
                c, s = cos_ref[m : m + 1, lanes], sin_ref[m : m + 1, lanes]
                pair = (re * c - im * s, re * s + im * c)
                for p in range(2):
                    start = p * band + h * width
                    turned[m, pl.ds(first, size), start : start + width] = pair[p].astype(
                        jnp.bfloat16
                    )

    edge_row = lax.broadcasted_iota(jnp.int32, (EDGE, width), 0)
    has_edge = jnp.where(epoch == epoch_count - 1, 1.0, 0.0)

    def sections(cut, tiles):
        cut_rows = spans[cut]
        rows = cut_rows + (EDGE if cut == cuts - 1 else 0)
        stack = [turned[tile, starts[cut] : starts[cut] + rows, :] for tile in tiles]
        moved = jnp.dot(
            jnp.concatenate(stack, 0), second_ref[...], preferred_element_type=jnp.float32
        )
        blocks = []
        for i in range(len(tiles)):
            pieces = [
                moved[i * rows : (i + 1) * rows, q * width : (q + 1) * width] for q in range(parts)
            ]
            block = [piece[:cut_rows] for piece in pieces]
            if cut == cuts - 1:
                edge = jnp.zeros((EDGE, width), jnp.float32)
                for q, piece in enumerate(pieces):
                    edge = jnp.where(edge_row == q, piece[cut_rows : cut_rows + 1] * has_edge, edge)
                block.append(edge)
            blocks.append(jnp.concatenate(block, 0))
        return blocks

    def forward(cut, k):
        tile_copy(cut, k).wait_recv()
        for j in range(1, epoch_count):
            epoch_copy(cut, k, j).start()

    order = list(range(half))
    nearby = [k for k in order[1:] if 2 * k < half]
    distant = [k for k in order[1:] if 2 * k >= half]
    for cut in range(cuts):

        def row_group(i, carry):
            transform(pl.multiple_of(i * group, group), group)
            return carry

        first = starts[cut] // group
        lax.fori_loop(first, first + spans[cut] // group, row_group, 0)
        if cut == cuts - 1:
            transform(rows_here, EDGE)
        if cut == 0:
            pl.semaphore_wait(barrier, half + epoch_count - 1)
        for b in range(0, half, batch):
            ks = order[b : b + batch]
            tiles = [exclusive(mine, k, half) * 2 + 1 - side for k in ks]
            for k, block in zip(ks, sections(cut, tiles)):
                given[k, rows_of(cut), :] = block.astype(jnp.bfloat16)
                partner_copy(cut, k).start()
        for b in range(0, half, batch):
            ks = order[b : b + batch]
            tiles = [exclusive(mine, k, half) * 2 + side for k in ks]
            for k, block in zip(ks, sections(cut, tiles)):
                partner_copy(cut, k).wait_recv()
                both = (block + landed[k, rows_of(cut), :].astype(jnp.float32)).astype(jnp.bfloat16)
                if k == 0:
                    full[epoch * half + mine, rows_of(cut), :] = both
                    for j in range(1, epoch_count):
                        epoch_copy(cut, 0, j).start()
                else:
                    folded[k, rows_of(cut), :] = both
                    tile_copy(cut, k).start()
        if cut > 0:
            for k in nearby:
                forward(cut - 1, k)
    def mix_rows(e, cut, first, edges=None):
        for h in range(chunks):
            values = []
            for j in range(half):
                value = tuple(
                    full[
                        e * half + j,
                        pl.ds(parts * starts[cut] + (h * 2 + p) * spans[cut] + first, group),
                        :,
                    ].astype(jnp.float32)
                    for p in range(2)
                )
                values.append(epoch_turn(value, j, epoch, epoch_count))
            done = dft(values + [None] * half, kept)
            if edges is not None:
                top = lax.broadcasted_iota(jnp.int32, (group, width), 0) == 0
                done = [
                    tuple(a + jnp.where(top, b, 0.0) for a, b in zip(part, edge))
                    for part, edge in zip(done, edges[h])
                ]
            for c, part in enumerate(done):
                for p in range(2):
                    row = pl.multiple_of(
                        p * band + e * rows_here + starts[cut] + first, group
                    )
                    mixed_ref[c, pl.ds(row, group), h * width : (h + 1) * width] = part[p].astype(
                        jnp.bfloat16
                    )

    def mix(e, cut):
        def step(i, carry):
            mix_rows(e, cut, pl.multiple_of(i * group, group))
            return carry

        lax.fori_loop(0, spans[cut] // group, step, 0)

    def mix_crossed(cut):
        for j in range(1, epoch_count):

            def arrive(k, carry, j=j):
                epoch_copy(cut, k, j).wait_recv()
                return carry

            lax.fori_loop(0, half, arrive, 0)
            mix(lax.rem(epoch + epoch_count - j, epoch_count), cut)

    for cut in range(cuts):
        for k in distant:
            forward(cut, k)
        if cut == 0:
            for k in nearby:
                forward(cuts - 1, k)
        mix(epoch, cut)
        if cut > 0:
            mix_crossed(cut - 1)
    mix_crossed(cuts - 1)

    edges = []
    for h in range(chunks):
        values = [None]
        for j in range(half):
            block = full[(epoch_count - 1) * half + j, parts * rows_here :, :]
            block = block.astype(jnp.float32)
            value = tuple(block[h * 2 + p : h * 2 + p + 1] for p in range(2))
            values.append(epoch_turn(value, j + 1, epoch, epoch_count))
        edges.append(dft(values + [None] * (tile_count - half - 1), kept))
    mix_rows(0, 0, 0, edges)
    table_copy.wait()

    for cut in range(cuts):

        def finish(k, carry, cut=cut):
            tile_copy(cut, k).wait_send()
            return carry

        lax.fori_loop(1, half, finish, 0)

        def settle(k, carry, cut=cut):
            partner_copy(cut, k).wait_send()
            for j in range(1, epoch_count):
                epoch_copy(cut, k, j).wait_send()
            return carry

        lax.fori_loop(0, half, settle, 0)


def image_kernel(image_scale, mixed_ref, last_ref, rows_ref, cols_ref, out_ref, held, sem):
    kept = held.shape[0]
    tall = jnp.transpose(rows_ref[...]) * image_scale
    copies = [pltpu.make_async_copy(held.at[c], out_ref.at[c], sem.at[c]) for c in range(kept)]
    for c in range(kept):
        pixels = jnp.dot(last_ref[c], mixed_ref[c], preferred_element_type=jnp.float32)
        held[c] = pixels * tall[:, c : c + 1] * cols_ref[...]
        copies[c].start()
    for c in range(kept):
        copies[c].wait()


def turns(product, modulus):
    angles = (product % modulus) * (2.0 * math.pi / modulus)
    return np.cos(angles), np.sin(angles)


def make_tables(tile_count, block_len):
    grid_size = tile_count * block_len
    long_idx = np.arange(block_len)
    tile_idx = np.arange(tile_count)
    turn_cos, turn_sin = turns(tile_idx[:, None] * long_idx[None, :], grid_size)
    c, s = turns(long_idx[:, None] * long_idx[None, :], block_len)
    second = np.stack([np.stack([c, s], 1), np.stack([-s, c], 1)], 0)
    width = min(LANES, block_len)
    second = second.reshape(2 * block_len, 2, block_len // width, width)
    second = second.transpose(0, 2, 1, 3).reshape(2 * block_len, 2 * block_len)
    pixel = long_idx[None, :] * tile_count + tile_idx[:, None]
    c, s = turns(pixel[:, :, None] * long_idx[None, None, :], grid_size)
    last = np.concatenate([c, -s], -1)
    return (
        turn_cos.astype(np.float32),
        turn_sin.astype(np.float32),
        second.astype(jnp.bfloat16),
        last.astype(jnp.bfloat16),
    )


def hbm(count):
    return [pl.BlockSpec(memory_space=pltpu.HBM)] * count


def vmem(count):
    return [pl.BlockSpec(memory_space=pltpu.VMEM)] * count


def body(tables, owners, row_offsets, col_offsets, samples, coords, taper_rows, taper_cols):
    tile_count = lax.axis_size("tile")
    epoch_count = lax.axis_size("epoch")
    n_slots = owners.shape[1]
    n_samples = samples.shape[3]
    capacity = max(2, n_slots * 5 // (4 * tile_count))
    capacity += capacity % 2
    lane_step = max(8, 1 << (capacity - 1).bit_length())
    band = taper_cols.shape[0]
    width = min(LANES, band)
    half, kept = tile_count // 2, tile_count // epoch_count
    rows_here = band // epoch_count
    parts = 2 * (band // width)
    sizes = (tile_count, epoch_count, capacity, band)
    raw_rows = 2 * n_samples // LANES * capacity
    raw_shapes = [
        ((raw_rows, LANES), jnp.float32),
        ((-(-(raw_rows + FIELDS) // EDGE) * EDGE, LANES), jnp.bfloat16),
    ]
    spots = -(-tile_count // (LANES // lane_step)) * LANES

    tile_sems = pltpu.SemaphoreType.DMA((2, tile_count))
    epoch_sems = pltpu.SemaphoreType.DMA((2, (epoch_count - 1) * tile_count))
    pool, slot_list, weights = pl.pallas_call(
        functools.partial(grid_kernel, sizes),
        out_shape=[
            jax.ShapeDtypeStruct(
                (epoch_count * tile_count, capacity * SUB // 2, LANES), jnp.bfloat16
            ),
            jax.ShapeDtypeStruct((epoch_count, FIELDS, spots), jnp.int32),
            jax.ShapeDtypeStruct((epoch_count, FIELDS, LANES), jnp.float32),
        ],
        in_specs=hbm(5),
        out_specs=vmem(3),
        scratch_shapes=[
            *(
                pltpu.VMEM(array.shape, array.dtype)
                for array in (owners, row_offsets, col_offsets, coords, samples)
            ),
            pltpu.SemaphoreType.DMA((5,)),
            *(
                pltpu.VMEM((count, *shape), dtype)
                for count in (tile_count, epoch_count * tile_count)
                for shape, dtype in raw_shapes
            ),
            tile_sems,
            tile_sems,
            epoch_sems,
            epoch_sems,
        ],
        compiler_params=pltpu.CompilerParams(
            vmem_limit_bytes=VMEM_BYTES, collective_id=1, has_side_effects=True
        ),
        name="grid_slots",
    )(
        *(
            pltpu.with_memory_space_constraint(array, pltpu.HBM)
            for array in (owners, row_offsets, col_offsets, coords, samples)
        )
    )

    lane_blocks = tile_count * band // LANES
    acc = pl.pallas_call(
        functools.partial(place_kernel, tile_count),
        out_shape=jax.ShapeDtypeStruct(
            (2, lane_blocks + 1, rows_here + 2 * SUB, LANES), jnp.float32
        ),
        in_specs=[pl.BlockSpec(memory_space=pltpu.SMEM)] + vmem(2),
        out_specs=vmem(1)[0],
        compiler_params=pltpu.CompilerParams(vmem_limit_bytes=VMEM_BYTES),
        name="place_slots",
    )(slot_list, weights, pool)

    groups = [rows_here * share // 128 for share in CUTS]
    spans = groups if all(span % 16 == 0 for span in groups) else [rows_here]
    cuts = len(spans)
    block_shape = (parts * rows_here + EDGE, width)
    sems = [pltpu.SemaphoreType.DMA((cuts * half,))] * 4
    sems += [pltpu.SemaphoreType.DMA((cuts * (epoch_count - 1) * half,))] * 2
    mixed, last_here = pl.pallas_call(
        functools.partial(swap_kernel, (tile_count, epoch_count, band), spans),
        out_shape=[
            jax.ShapeDtypeStruct((kept, 2 * band, band), jnp.bfloat16),
            jax.ShapeDtypeStruct((kept, band, 2 * band), jnp.bfloat16),
        ],
        in_specs=vmem(4) + hbm(1),
        out_specs=vmem(2),
        scratch_shapes=[
            pltpu.SemaphoreType.DMA((1,)),
            pltpu.VMEM((tile_count, rows_here + EDGE, 2 * band), jnp.bfloat16),
            pltpu.VMEM((half, *block_shape), jnp.bfloat16),
            pltpu.VMEM((half, *block_shape), jnp.bfloat16),
            pltpu.VMEM((half, *block_shape), jnp.bfloat16),
            pltpu.VMEM((epoch_count * half, *block_shape), jnp.bfloat16),
            *sems,
        ],
        compiler_params=pltpu.CompilerParams(
            vmem_limit_bytes=VMEM_BYTES, collective_id=0, has_side_effects=True
        ),
        name="swap_rows",
    )(acc, *(jnp.asarray(table) for table in tables))

    image_scale = math.sqrt(n_slots) / (64.0 * tile_count * math.sqrt(epoch_count))
    return pl.pallas_call(
        functools.partial(image_kernel, image_scale),
        out_shape=jax.ShapeDtypeStruct((kept, band, band), jnp.float32),
        in_specs=vmem(4),
        out_specs=hbm(1)[0],
        scratch_shapes=[
            pltpu.VMEM((kept, band, band), jnp.float32),
            pltpu.SemaphoreType.DMA((kept,)),
        ],
        compiler_params=pltpu.CompilerParams(vmem_limit_bytes=VMEM_BYTES),
        name="image_rows",
    )(mixed, last_here, taper_rows, taper_cols[None, :])


def solution(mesh):
    placed = (
        P("epoch", "tile"),
        P("epoch", "tile"),
        P("epoch", "tile"),
        P("epoch", "tile", None, None),
        P("epoch", "tile", None, None),
        P("epoch", None),
        P("tile"),
    )

    def whole(owners, row_offsets, col_offsets, samples, coords, taper_rows, taper_cols):
        tables = make_tables(mesh.shape["tile"], taper_cols.shape[0] // mesh.shape["tile"])
        return jax.shard_map(
            functools.partial(body, tables),
            mesh=mesh,
            in_specs=placed,
            out_specs=P("epoch", None, "tile"),
            check_vma=False,
        )(owners, row_offsets, col_offsets, samples, coords, taper_rows, taper_cols)

    return whole
```
